32 devices in a mesh: groups: 2 (over y), frag: 4 (over z), grid: 2 (over x), sub: 2 (over core).
Axes of the slice: x: 2, y: 2, z: 4, core: 2. Of those that a mesh axis runs over, the one named last changes fastest.
Arguments:
- density: bfloat16 [16, 384, 384], P(('groups', 'frag')), parts along dimension 0, may hold values from -6 to 6
- basis_size: int32 [8], replicated, may hold values from 192 to 384
- coupling: bfloat16 [256, 384, 384], P(('groups', 'frag', 'grid', 'sub')), parts along dimension 0, may hold values from -0.3125 to 0.3125
- pair_first: int32 [128], P(('frag', 'grid', 'sub')), may hold values from 0 to 7, as said below
- pair_second: int32 [128], P(('frag', 'grid', 'sub')), may hold values from 0 to 7, as said below
- dimer_count: int32 [16], P(('frag', 'grid', 'sub')), may hold values from 4 to 8, as said below
- source_coords: float32 [16, 3, 384], P(('groups', 'frag')), parts along dimension 0, may hold values from 0 to 16
- grid_region: int32 [8, 512], P(('grid', 'sub')), may hold values from 0 to 7
Outputs:
- new_density: bfloat16 [16, 384, 384], P(('groups', 'frag'), ('grid', 'sub')), parts along dimension 0
- potential: float32 [16, 512], P(('groups', 'grid', 'sub'), 'frag'), parts along dimension 0
The draws below stay inside these ranges and needn't reach their ends.
There are 2 independent parts, one for each index of `groups`. The reference program is written for one: setup_inputs(seed, part) draws one part's arguments, and reference() takes and returns one part's arrays. A program takes and returns all parts, laid end to end along the dimension named above; an argument that names none is the same for every part. Nothing has to cross between parts.
Inputs may be any that keep to these rules, and one draw needn't show every extreme that they name: `pair_first`: slot s belongs to owner s // 8; its first fragment is one of the 2 fragments t * 2 to t * 2 + 1 with t = (s // 8) // 4. `pair_second`: differs from the slot's first fragment and is one of the fragments of team t or team t + 1, t as for pair_first. Only the first dimer_count[d] slots of owner d are dimers; some owner has 8.
All inputs are finite; a program needn't handle non-finite values.
Results may differ from the reference program's by a relative error of at most 0.0051.
Values may be sent and summed in bfloat16 or wider, within the bound.
No kernel may reach another device: no remote copies, remote signals or barrier semaphores. Data moves between devices by JAX's collectives and lax.ppermute only.
A program may use at most 192 MiB of HBM per device.

```python
import jax
import jax.numpy as jnp
from jax import lax

NB = 384
FRAG_DEV = 2
CAP = 8
GRID_DEV = 128
NFRAG = 8
TEAM = 4
OWNERS = 16
SLOTS = 128
ROWS = 8
COLS = 512
N_FRAG = 4


def dimer_pairs(key):
    key_local, key_step, key_last = jax.random.split(key, 3)
    slot_ids = jnp.arange(SLOTS, dtype=jnp.int32)
    team_id = slot_ids // CAP // TEAM
    local_first = jax.random.randint(key_local, (SLOTS,), 0, FRAG_DEV, dtype=jnp.int32)
    first_id = team_id * FRAG_DEV + local_first
    step_up = jax.random.randint(key_step, (SLOTS,), 1, FRAG_DEV + 1, dtype=jnp.int32)
    step_last = jax.random.randint(key_last, (SLOTS,), 1, FRAG_DEV, dtype=jnp.int32)
    at_end = team_id == N_FRAG - 1
    second_id = jnp.where(at_end, team_id * FRAG_DEV + (local_first + step_last) % FRAG_DEV, first_id + step_up)
    return (first_id, second_id)


def draw_pair_first(key, part):
    first_id, second_id = dimer_pairs(key)
    return first_id


def draw_pair_second(key, part):
    first_id, second_id = dimer_pairs(key)
    return second_id


def draw_dimer_count(key, part):
    key = jax.random.fold_in(key, 7)
    key_count, key_top = jax.random.split(key)
    counts = jax.random.randint(key_count, (OWNERS,), CAP // 2, CAP + 1, dtype=jnp.int32)
    busiest = jax.random.randint(key_top, (), 0, OWNERS, dtype=jnp.int32)
    return counts.at[busiest].set(CAP)


def touch_ends(values, key, low, top_value):
    dims = values.shape
    index_at = [jax.random.randint(jax.random.fold_in(key, axis), (), 0, dims[axis]) for axis in range(len(dims))]
    values = values.at[tuple(index_at)].set(low)
    longest = dims.index(max(dims))
    index_at[longest] = (index_at[longest] + 1) % dims[longest]
    return values.at[tuple(index_at)].set(top_value)


def levels(rng, dims, shards, smallest, top_value):
    loudness = 1.0
    for dim, shards_of in shards:
        draws = jax.random.uniform(jax.random.fold_in(jax.random.fold_in(rng, 6), dim), (shards_of,), jnp.float32, smallest / len(shards), top_value / len(shards))
        loudness = loudness * jnp.repeat(jnp.exp(draws), dims[dim] // shards_of).reshape((-1,) + (1,) * (len(dims) - 1 - dim))
    return loudness


def bell_draw(key, dims, spread, most, pieces=(), kind=jnp.bfloat16):
    array = jax.random.normal(key, dims, jnp.float32) * spread
    if len(pieces) > 0:
        array = levels(key, dims, pieces, -0.22, 0.18) * array
    return jnp.clip(array, min=-most, max=most).astype(kind)


def setup_inputs(seed: int = 0, part: int = 0) -> dict:
    streams_of = jax.random.split(jax.random.key(seed), 9)
    part_splits = jax.random.split(jax.random.fold_in(streams_of[8], part), 9)
    return {
        "density": bell_draw(part_splits[0], (NFRAG, NB, NB), 1.0, 6.0, ((0, 4),)),
        "basis_size": touch_ends(jax.random.randint(streams_of[1], (NFRAG,), NB // 2, NB + 1), jax.random.fold_in(streams_of[1], 1), NB // 2, NB).astype(jnp.int32),
        "coupling": bell_draw(part_splits[2], (SLOTS, NB, NB), NB ** -0.5, 0.3125, ((0, 16),)),
        "pair_first": draw_pair_first(jax.random.fold_in(streams_of[8], 71), part),
        "pair_second": draw_pair_second(jax.random.fold_in(streams_of[8], 71), part),
        "dimer_count": draw_dimer_count(jax.random.fold_in(streams_of[8], 71), part),
        "source_coords": jnp.clip(16.0 * jax.random.uniform(part_splits[6], (NFRAG, 3, NB), jnp.float32) ** levels(part_splits[6], (NFRAG, 3, NB), ((0, 4),), -0.2, 0.2), 0.0, 16.0),
        "grid_region": touch_ends(jax.random.randint(streams_of[7], (ROWS, COLS), 0, NFRAG), jax.random.fold_in(streams_of[7], 1), 0, NFRAG - 1).astype(jnp.int32),
    }


def reference(density, basis_size, coupling, pair_first, pair_second, dimer_count, source_coords, grid_region):
    index_nb = jnp.arange(NB, dtype=jnp.int32)
    live_rows = (index_nb[None, :] < basis_size[:, None]).astype(jnp.float32)
    mask = live_rows[:, :, None] * live_rows[:, None, :]
    masked = (density.astype(jnp.float32) * mask).astype(jnp.bfloat16)
    slot_ids = jnp.arange(SLOTS, dtype=jnp.int32)
    live = slot_ids % CAP < dimer_count[slot_ids // CAP]

    def one_slot(totals, item):
        factor, first_id, second_id, active = item

        def work(totals):
            left_part = jnp.dot(factor, masked[second_id], preferred_element_type=jnp.float32).astype(jnp.bfloat16)
            corr_first = jnp.dot(left_part, factor.T, preferred_element_type=jnp.float32)
            right_part = lax.dot_general(factor, masked[first_id], (((0,), (0,)), ((), ())), preferred_element_type=jnp.float32).astype(jnp.bfloat16)
            corr_second = jnp.dot(right_part, factor, preferred_element_type=jnp.float32)
            return totals.at[first_id].add(corr_first).at[second_id].add(corr_second)
        return (lax.cond(active, work, lambda kept: kept, totals), None)
    zeros = jnp.zeros((NFRAG, NB, NB), jnp.float32)
    correction, _ = lax.scan(one_slot, zeros, (coupling, pair_first, pair_second, live))
    new_density = (masked.astype(jnp.float32) + correction * mask).astype(jnp.bfloat16)
    charge = jnp.diagonal(masked.astype(jnp.float32), axis1=1, axis2=2)
    row_ids = jnp.arange(ROWS, dtype=jnp.int32)

    def column_block(block_id):
        cols = block_id * GRID_DEV + jnp.arange(GRID_DEV, dtype=jnp.int32)
        point_x = 0.25 * jnp.broadcast_to(row_ids[:, None], (ROWS, GRID_DEV)).astype(jnp.float32)
        point_y = 0.25 * jnp.broadcast_to((cols // 64)[None, :], (ROWS, GRID_DEV)).astype(jnp.float32)
        point_z = 0.25 * jnp.broadcast_to((cols % 64)[None, :], (ROWS, GRID_DEV)).astype(jnp.float32)
        region = lax.dynamic_slice_in_dim(grid_region, (block_id * GRID_DEV).astype(jnp.int32), GRID_DEV, 1)

        def frag_step(total, member):
            where_src = source_coords[member]
            dist_sq = (point_x[..., None] - where_src[0]) ** 2 + (point_y[..., None] - where_src[1]) ** 2 + (point_z[..., None] - where_src[2]) ** 2
            contrib = lax.optimization_barrier(jnp.sum(charge[member] / jnp.sqrt(dist_sq + 1.0), axis=-1))
            return (total + jnp.where(region != member, contrib, 0.0), None)
        total, _ = lax.scan(frag_step, jnp.zeros((ROWS, GRID_DEV), jnp.float32), jnp.arange(NFRAG, dtype=jnp.int32))
        return total
    blocks = lax.map(column_block, jnp.arange(N_FRAG, dtype=jnp.int32))
    potential = jnp.transpose(blocks, (1, 0, 2)).reshape(ROWS, COLS)
    potential = potential * (8.0 / jnp.sqrt(jnp.float32(NFRAG * NB)))
    return (new_density, potential)
```

```python
import functools

import jax
import jax.numpy as jnp
from jax import lax
from jax.experimental import pallas as pl
from jax.experimental.pallas import tpu as pltpu
from jax.sharding import PartitionSpec as P

VMEM_LIMIT = 24 * 1024 * 1024


def live_square(values, size):
    rows = lax.broadcasted_iota(jnp.int32, values.shape, 0)
    cols = lax.broadcasted_iota(jnp.int32, values.shape, 1)
    return jnp.where((rows < size) & (cols < size), values, jnp.zeros_like(values))


def slot_ids(first_ref, second_ref, count_ref, slot, base, frag_dev):
    first = jnp.clip(first_ref[slot] - base, 0, frag_dev - 1)
    second = jnp.clip(second_ref[slot] - base, 0, 2 * frag_dev - 1)
    return first, second, slot < count_ref[0]


def right_kernel(
    size_ref, first_ref, second_ref, count_ref, density_ref, coupling_ref, coords_ref, region_ref,
    keep_ref, send_ref, own_ref, pot_ref,
    factor_ref, masked_ref, total_ref, sems,
):
    frag_dev, nbasis = density_ref.shape[0], density_ref.shape[1]
    slots = coupling_ref.shape[0]
    copies = [
        pltpu.make_async_copy(coupling_ref.at[s], factor_ref.at[s], sems.at[s]) for s in range(slots)
    ]
    for copy in copies:
        copy.start()
    team = lax.axis_index("frag")
    base = team * frag_dev
    for f in range(frag_dev):
        masked_ref[f] = live_square(density_ref[f].astype(jnp.float32), size_ref[base + f]).astype(
            jnp.bfloat16
        )
    total_ref[...] = jnp.zeros_like(total_ref)

    pts_rows = region_ref.shape[0]
    blocks, block_cols = pot_ref.shape[0], pot_ref.shape[2]
    member = lax.axis_index("grid") * lax.axis_size("sub") + lax.axis_index("sub")
    columns = []
    for f in range(frag_dev):
        diag = live_square(density_ref[f].astype(jnp.float32), size_ref[base + f])
        rows = lax.broadcasted_iota(jnp.int32, diag.shape, 0)
        cols = lax.broadcasted_iota(jnp.int32, diag.shape, 1)
        charge = jnp.sum(jnp.where(rows == cols, diag, 0.0), axis=1, keepdims=True)
        place = jnp.transpose(jnp.concatenate([coords_ref[f], jnp.zeros((5, nbasis), jnp.float32)]))
        columns.append((charge, place[:, 0:1], place[:, 1:2], place[:, 2:3]))
    lane = lax.broadcasted_iota(jnp.int32, (1, block_cols), 1)

    def one_block(step, carry):
        block = lax.rem(team + step, blocks)
        col = block * block_cols + lane
        point_y = 0.25 * (col // 64).astype(jnp.float32)
        point_z = 0.25 * (col % 64).astype(jnp.float32)
        start = pl.multiple_of(block * block_cols, block_cols)
        for r in range(pts_rows):
            point_x = 0.25 * (member * pts_rows + r).astype(jnp.float32)
            region = region_ref[r : r + 1, pl.ds(start, block_cols)]
            total = jnp.zeros((1, block_cols), jnp.float32)
            for f in range(frag_dev):
                charge, src_x, src_y, src_z = columns[f]
                dist_sq = (
                    (point_x - src_x) ** 2 + (point_y - src_y) ** 2 + (point_z - src_z) ** 2
                )
                value = jnp.sum(charge * lax.rsqrt(dist_sq + 1.0), axis=0, keepdims=True)
                total = total + jnp.where(region != base + f, value, 0.0)
            pot_ref[step, r : r + 1, :] = total
        return carry

    lax.fori_loop(0, blocks, one_block, 0)

    for s in range(slots):
        copies[s].wait()
        first, second, live = slot_ids(first_ref, second_ref, count_ref, s, base, frag_dev)
        factor = factor_ref[s]
        right = jnp.dot(factor.T, masked_ref[first], preferred_element_type=jnp.float32)
        corr = jnp.dot(right.astype(jnp.bfloat16), factor, preferred_element_type=jnp.float32)
        target = jnp.where(live, second, 2 * frag_dev)
        total_ref[target] = total_ref[target] + corr

    own_ref[...] = total_ref[:frag_dev]
    split_rows(total_ref, frag_dev, keep_ref, send_ref)


def split_rows(total_ref, start, keep_ref, send_ref):
    frag_dev, grid_size, share, _ = keep_ref.shape
    sub_size = lax.axis_size("sub")
    me = lax.axis_index("sub")
    for f in range(frag_dev):
        for g in range(grid_size):
            mine = pl.multiple_of((g * sub_size + me) * share, share)
            other = pl.multiple_of((g * sub_size + 1 - me) * share, share)
            keep_ref[f, g] = total_ref[start + f, pl.ds(mine, share), :].astype(keep_ref.dtype)
            send_ref[f, g] = total_ref[start + f, pl.ds(other, share), :].astype(send_ref.dtype)


def left_kernel(
    size_ref, first_ref, second_ref, count_ref, density_ref, mine_ref, other_ref, own_ref, coupling_ref,
    keep_ref, send_ref,
    factor_ref, masked_ref, total_ref, sems,
):
    frag_dev = density_ref.shape[0]
    slots = coupling_ref.shape[0]
    half = mine_ref.shape[0]
    copies = [
        pltpu.make_async_copy(coupling_ref.at[s], factor_ref.at[s], sems.at[s]) for s in range(slots)
    ]
    for copy in copies:
        copy.start()
    base = lax.axis_index("frag") * frag_dev
    me = lax.axis_index("sub")
    last = size_ref.shape[0] - 1

    def put(place, values):
        size = size_ref[jnp.minimum(base + place, last)]
        masked_ref[place] = live_square(values.astype(jnp.float32), size).astype(jnp.bfloat16)

    for f in range(frag_dev):
        put(f, density_ref[f])
    for f in range(half):
        put(frag_dev + me * half + f, mine_ref[f])
        put(frag_dev + (1 - me) * half + f, other_ref[f])
    total_ref[:frag_dev] = own_ref[...]
    total_ref[frag_dev] = jnp.zeros_like(total_ref[frag_dev])
    for s in range(slots):
        copies[s].wait()
        first, second, live = slot_ids(first_ref, second_ref, count_ref, s, base, frag_dev)
        factor = factor_ref[s]
        left = jnp.dot(factor, masked_ref[second], preferred_element_type=jnp.float32)
        corr = lax.dot_general(
            left.astype(jnp.bfloat16), factor, (((1,), (1,)), ((), ())), preferred_element_type=jnp.float32
        )
        target = jnp.where(live, first, frag_dev)
        total_ref[target] = total_ref[target] + corr
    split_rows(total_ref, 0, keep_ref, send_ref)


def shifted(value, axis, steps):
    count = lax.axis_size(axis)
    pairs = [(s, s + steps) for s in range(count) if 0 <= s + steps < count]
    return lax.ppermute(value, axis, pairs)


def turned(value, axis, steps):
    count = lax.axis_size(axis)
    return lax.ppermute(value, axis, [(s, (s + steps) % count) for s in range(count)])


def per_device(
    density, basis_size, coupling, pair_first, pair_second, dimer_count, source_coords, grid_region
):
    frag_dev, nbasis, _ = density.shape
    slots = coupling.shape[0]
    teams, grid_size, sub_size = (lax.axis_size(a) for a in ("frag", "grid", "sub"))
    assert sub_size == 2 and frag_dev % sub_size == 0 and teams & (teams - 1) == 0
    share = nbasis // (grid_size * sub_size)
    half = frag_dev // sub_size
    pts_rows, total_cols = grid_region.shape
    team, grid_at, sub_at = (lax.axis_index(a) for a in ("frag", "grid", "sub"))

    smem = pl.BlockSpec(memory_space=pltpu.SMEM)
    vmem = pl.BlockSpec(memory_space=pltpu.VMEM)
    anywhere = pl.BlockSpec(memory_space=pl.ANY)
    params = pltpu.CompilerParams(vmem_limit_bytes=VMEM_LIMIT)
    cost = pl.CostEstimate(
        flops=4 * slots * nbasis**3, bytes_accessed=2 * slots * nbasis * nbasis, transcendentals=0
    )

    def scratch(masks, totals):
        return [
            pltpu.VMEM((slots, nbasis, nbasis), jnp.bfloat16),
            pltpu.VMEM((masks, nbasis, nbasis), jnp.bfloat16),
            pltpu.VMEM((totals, nbasis, nbasis), jnp.float32),
            pltpu.SemaphoreType.DMA((slots,)),
        ]

    halves = (frag_dev, grid_size, share, nbasis)
    mine = shifted(lax.dynamic_slice_in_dim(density, sub_at * half, half), "frag", -1)
    next_keep, next_send, own_part, pot = pl.pallas_call(
        right_kernel,
        out_shape=(
            jax.ShapeDtypeStruct(halves, jnp.bfloat16),
            jax.ShapeDtypeStruct(halves, jnp.bfloat16),
            jax.ShapeDtypeStruct((frag_dev, nbasis, nbasis), jnp.float32),
            jax.ShapeDtypeStruct((teams, pts_rows, total_cols // teams), jnp.float32),
        ),
        in_specs=[smem] * 4 + [vmem, anywhere, vmem, vmem],
        out_specs=(vmem,) * 4,
        scratch_shapes=scratch(frag_dev, 2 * frag_dev + 1),
        compiler_params=params,
        cost_estimate=cost,
        name="right",
    )(basis_size, pair_first, pair_second, dimer_count, density, coupling, source_coords, grid_region)

    next_sum = (
        next_keep.astype(jnp.float32) + turned(next_send, "sub", 1).astype(jnp.float32)
    ).astype(jnp.bfloat16)
    from_before = shifted(next_sum, "frag", 1)

    other = turned(mine, "sub", 1)
    own_keep, own_send = pl.pallas_call(
        left_kernel,
        out_shape=(
            jax.ShapeDtypeStruct(halves, jnp.float32),
            jax.ShapeDtypeStruct(halves, jnp.bfloat16),
        ),
        in_specs=[smem] * 4 + [vmem] * 4 + [anywhere],
        out_specs=(vmem,) * 2,
        scratch_shapes=scratch(2 * frag_dev, frag_dev + 1),
        compiler_params=params,
        cost_estimate=cost,
        name="left",
    )(basis_size, pair_first, pair_second, dimer_count, density, mine, other, own_part, coupling)
    own_sum = own_keep + turned(own_send, "sub", 1).astype(jnp.float32) + from_before.astype(jnp.float32)

    correction = lax.dynamic_index_in_dim(own_sum, grid_at, 1, keepdims=False)
    for step in range(1, grid_size):
        part = lax.dynamic_index_in_dim(own_sum, (grid_at + step) % grid_size, 1, keepdims=False)
        correction = correction + turned(part.astype(jnp.bfloat16), "grid", step).astype(jnp.float32)

    row_start = (grid_at * sub_size + sub_at) * share
    sizes = lax.dynamic_slice_in_dim(basis_size, team * frag_dev, frag_dev)[:, None, None]
    own_rows = lax.dynamic_slice_in_dim(density, row_start, share, 1).astype(jnp.float32)
    live = (row_start + jnp.arange(share, dtype=jnp.int32)[None, :, None] < sizes) & (
        jnp.arange(nbasis, dtype=jnp.int32)[None, None, :] < sizes
    )
    new_density = jnp.where(live, own_rows + correction, 0.0).astype(jnp.bfloat16)

    while pot.shape[0] > 1:
        rest = pot.shape[0] // 2
        pot = pot[:rest] + turned(pot[rest:], "frag", rest)
    scale = 8.0 / jnp.sqrt(jnp.float32(frag_dev * teams * nbasis))
    return (new_density, pot[0] * scale)


def solution(mesh):
    placed = (
        P(("groups", "frag"), None, None),
        P(),
        P(("groups", "frag", "grid", "sub"), None, None),
        P(("frag", "grid", "sub")),
        P(("frag", "grid", "sub")),
        P(("frag", "grid", "sub")),
        P(("groups", "frag"), None, None),
        P(("grid", "sub"), None),
    )
    return jax.shard_map(
        per_device,
        mesh=mesh,
        in_specs=placed,
        out_specs=(
            P(("groups", "frag"), ("grid", "sub"), None),
            P(("groups", "grid", "sub"), "frag"),
        ),
        check_vma=False,
    )
```

```python
import functools
import math

import jax
import jax.numpy as jnp
from jax import lax
from jax.experimental import pallas as pl
from jax.experimental.pallas import tpu as pltpu
from jax.sharding import PartitionSpec as P

VMEM_LIMIT = 24 * 1024 * 1024
BF16, F32, I32 = jnp.bfloat16, jnp.float32, jnp.int32


def live_square(values, size):
    rows = lax.broadcasted_iota(I32, values.shape, 0)
    cols = lax.broadcasted_iota(I32, values.shape, 1)
    return jnp.where((rows < size) & (cols < size), values.astype(F32), 0.0).astype(BF16)


def charges(masked_ref, f):
    nbasis, tile = masked_ref.shape[1], 128
    parts = []
    for at in range(0, nbasis, tile):
        block = masked_ref[f, at : at + tile, at : at + tile].astype(F32)
        rows = lax.broadcasted_iota(I32, block.shape, 0)
        cols = lax.broadcasted_iota(I32, block.shape, 1)
        parts.append(jnp.sum(jnp.where(rows == cols, block, 0.0), axis=1, keepdims=True))
    return jnp.concatenate(parts, axis=0)


def split_rows(read, keep_ref, send_ref):
    frag_dev, grid_size, share, _ = keep_ref.shape
    sub_size, me = lax.axis_size("sub"), lax.axis_index("sub")
    for f in range(frag_dev):
        for g in range(grid_size):
            mine = pl.multiple_of((g * sub_size + me) * share, share)
            other = pl.multiple_of((g * sub_size + 1 - me) * share, share)
            keep_ref[f, g] = read(f, pl.ds(mine, share)).astype(keep_ref.dtype)
            send_ref[f, g] = read(f, pl.ds(other, share)).astype(send_ref.dtype)


def pipelined(slots, first_dot, second_dot, add):
    held = None
    for slot in range(slots + 1):
        now = first_dot(slot).astype(BF16) if slot < slots else None
        if held is not None:
            add(slot - 1, second_dot(slot - 1, held))
        held = now


def dot(a, b):
    return jnp.dot(a, b, preferred_element_type=F32)


def dot_t(a, b):
    return lax.dot_general(a, b, (((1,), (1,)), ((), ())), preferred_element_type=F32)


def right_kernel(
    size_hbm, first_hbm, second_hbm, count_hbm, density_ref, coupling_hbm, coords_hbm, region_hbm,
    keep_ref, send_ref, own_ref, factor_ref, masked_ref, far_ref, near_ref, ids_ref,
    size_ref, first_ref, second_ref, count_ref, coords_ref, region_ref, total_ref, sems,
):
    frag_dev, nbasis = density_ref.shape[0], density_ref.shape[1]
    slots = factor_ref.shape[0]
    copies = [
        pltpu.make_async_copy(source, target, sems.at[i])
        for i, (source, target) in enumerate(
            [
                (size_hbm, size_ref), (first_hbm, first_ref), (second_hbm, second_ref),
                (count_hbm, count_ref), (coords_hbm, coords_ref), (region_hbm, region_ref),
            ]
            + [(coupling_hbm.at[s], factor_ref.at[s]) for s in range(slots)]
        )
    ]
    for copy in copies:
        copy.start()
    total_ref[...] = jnp.zeros_like(total_ref)
    for copy in copies[:6]:
        copy.wait()
    team = lax.axis_index("frag")
    base = team * frag_dev
    trash = 2 * frag_dev
    for s in range(slots):
        live = s < count_ref[0]
        first = jnp.clip(first_ref[s] - base, 0, frag_dev - 1)
        second = jnp.clip(second_ref[s] - base, 0, trash - 1)
        ids_ref[s] = first
        ids_ref[slots + s] = second
        ids_ref[2 * slots + s] = jnp.where(live, first, frag_dev)
        ids_ref[3 * slots + s] = jnp.where(live, second, trash)
    for f in range(2 * frag_dev):
        ids_ref[4 * slots + f] = size_ref[jnp.minimum(base + f, size_ref.shape[0] - 1)]
    for f in range(frag_dev):
        masked_ref[f] = live_square(density_ref[f], size_ref[base + f])

    pts_rows = region_ref.shape[0]
    near, block_cols = near_ref.shape[0], near_ref.shape[2]
    teams = near + far_ref.shape[0]
    member = lax.axis_index("grid") * lax.axis_size("sub") + lax.axis_index("sub")
    columns = []
    for f in range(frag_dev):
        place = [coords_ref[d, f : f + 1, :] for d in range(3)]
        place = jnp.transpose(jnp.concatenate(place + [jnp.zeros((5, nbasis), F32)]))
        columns.append((charges(masked_ref, f), place[:, 0:1], place[:, 1:2], place[:, 2:3]))
    lane = lax.broadcasted_iota(I32, (1, block_cols), 1)

    def one_block(step, slab_ref, at):
        block = lax.rem(team + step, teams)
        col = block * block_cols + lane
        point_y = 0.25 * (col // 64).astype(F32)
        point_z = 0.25 * (col % 64).astype(F32)
        start = pl.multiple_of(block * block_cols, block_cols)
        totals = [jnp.zeros((1, block_cols), F32) for _ in range(pts_rows)]
        for f in range(frag_dev):
            charge, src_x, src_y, src_z = columns[f]
            in_plane = (point_y - src_y) ** 2 + (point_z - src_z) ** 2 + 1.0
            for r in range(pts_rows):
                point_x = 0.25 * (member * pts_rows + r).astype(F32)
                value = charge * lax.rsqrt((point_x - src_x) ** 2 + in_plane)
                value = jnp.sum(value, axis=0, keepdims=True)
                region = region_ref[r : r + 1, pl.ds(start, block_cols)]
                totals[r] = totals[r] + jnp.where(region != base + f, value, 0.0)
        for r in range(pts_rows):
            slab_ref[at, r : r + 1, :] = totals[r]

    @pl.loop(0, near)
    def _(step):
        one_block(step, near_ref, step)
        one_block(near + step, far_ref, step)

    for copy in copies[6:]:
        copy.wait()

    def add(s, corr):
        target = ids_ref[3 * slots + s]
        total_ref[target] = total_ref[target] + corr

    pipelined(
        slots,
        lambda s: dot(factor_ref[s].T, masked_ref[ids_ref[s]]),
        lambda s, right: dot(right, factor_ref[s]),
        add,
    )
    own_ref[...] = total_ref[:frag_dev]
    split_rows(lambda f, rows: total_ref[frag_dev + f, rows, :], keep_ref, send_ref)


def left_kernel(
    ids_ref, masked_ref, mine_ref, other_ref, own_ref, factor_ref,
    keep_ref, send_ref,
    all_ref, total_ref,
):
    frag_dev, slots, half = masked_ref.shape[0], factor_ref.shape[0], mine_ref.shape[0]
    me = lax.axis_index("sub")
    for f in range(frag_dev):
        all_ref[f] = masked_ref[f]
        total_ref[f] = own_ref[f]
    total_ref[frag_dev] = jnp.zeros_like(total_ref[frag_dev])
    for f in range(half):
        at = frag_dev + me * half + f
        all_ref[at] = live_square(mine_ref[f], ids_ref[4 * slots + at])
        at = frag_dev + (1 - me) * half + f
        all_ref[at] = live_square(other_ref[f], ids_ref[4 * slots + at])

    def add(s, corr):
        target = ids_ref[2 * slots + s]
        total_ref[target] = total_ref[target] + corr

    pipelined(
        slots,
        lambda s: dot(factor_ref[s], all_ref[ids_ref[slots + s]]),
        lambda s, left: dot_t(left, factor_ref[s]),
        add,
    )
    split_rows(lambda f, rows: total_ref[f, rows, :], keep_ref, send_ref)


def next_kernel(keep_ref, recv_ref, out_ref):
    out_ref[...] = (keep_ref[...].astype(F32) + recv_ref[...].astype(F32)).astype(BF16)


def sum_kernel(keep_ref, recv_ref, before_ref, near_ref, far_ref, own_ref, pot_ref, pass_ref, *part_refs):
    grid_size = keep_ref.shape[1]
    me = lax.axis_index("grid")

    def total(g):
        return keep_ref[:, g] + recv_ref[:, g].astype(F32) + before_ref[:, g].astype(F32)

    own_ref[...] = total(me)
    for step, part_ref in enumerate(part_refs, 1):
        part_ref[...] = total(lax.rem(me + step, grid_size)).astype(BF16)
    pot_ref[...] = near_ref[0:1] + far_ref[0:1]
    pass_ref[...] = near_ref[1:2] + far_ref[1:2]


def last_kernel(scale, slots, ids_ref, masked_ref, own_ref, pot_ref, passed_ref, *rest):
    part_refs, (out_ref, potential_ref) = rest[:-2], rest[-2:]
    frag_dev, share, nbasis = out_ref.shape
    member = lax.axis_index("grid") * lax.axis_size("sub") + lax.axis_index("sub")
    row_start = pl.multiple_of(member * share, share)
    rows = row_start + lax.broadcasted_iota(I32, (share, nbasis), 0)
    cols = lax.broadcasted_iota(I32, (share, nbasis), 1)
    for f in range(frag_dev):
        size = ids_ref[4 * slots + f]
        correction = own_ref[f]
        for part_ref in part_refs:
            correction = correction + part_ref[f].astype(F32)
        correction = jnp.where((rows < size) & (cols < size), correction, 0.0)
        out_ref[f] = (masked_ref[f, pl.ds(row_start, share), :].astype(F32) + correction).astype(BF16)
    potential_ref[...] = (pot_ref[0] + passed_ref[0]) * scale


def shifted(value, axis, steps):
    count = lax.axis_size(axis)
    return lax.ppermute(value, axis, [(s, s + steps) for s in range(count) if 0 <= s + steps < count])


def turned(value, axis, steps):
    count = lax.axis_size(axis)
    return lax.ppermute(value, axis, [(s, (s + steps) % count) for s in range(count)])


def in_hbm(value):
    return pltpu.with_memory_space_constraint(value, pltpu.HBM)


def shape(dims, dtype):
    return jax.ShapeDtypeStruct(dims, dtype)


def per_device(
    density, basis_size, coupling, pair_first, pair_second, dimer_count, source_coords, grid_region
):
    frag_dev, nbasis, _ = density.shape
    slots = coupling.shape[0]
    teams, grid_size, sub_size = (lax.axis_size(a) for a in ("frag", "grid", "sub"))
    assert sub_size == 2 and frag_dev % sub_size == 0
    assert teams >= 4 and teams & (teams - 1) == 0
    share = nbasis // (grid_size * sub_size)
    half = frag_dev // sub_size
    pts_rows, total_cols = grid_region.shape
    block_cols = total_cols // teams

    smem = pl.BlockSpec(memory_space=pltpu.SMEM)
    vmem = pl.BlockSpec(memory_space=pltpu.VMEM)
    hbm = pl.BlockSpec(memory_space=pltpu.HBM)
    halves = (frag_dev, grid_size, share, nbasis)
    square = (nbasis, nbasis)

    def call(kernel, name, ins, outs, out_specs, scratch=(), flops=0):
        return pl.pallas_call(
            kernel,
            out_shape=outs,
            in_specs=ins,
            out_specs=out_specs,
            scratch_shapes=scratch,
            compiler_params=pltpu.CompilerParams(vmem_limit_bytes=VMEM_LIMIT),
            cost_estimate=pl.CostEstimate(flops=flops, bytes_accessed=1 << 20, transcendentals=0),
            name=name,
        )

    work = 4 * slots * nbasis**3
    mine = shifted(lax.dynamic_slice_in_dim(density, lax.axis_index("sub") * half, half), "frag", -1)
    slabs = shape((teams // 2, pts_rows, block_cols), F32)
    next_keep, next_send, own_part, factors, masked, far, near, ids = call(
        right_kernel,
        "right",
        [hbm] * 4 + [vmem] + [hbm] * 3,
        (
            shape(halves, BF16), shape(halves, BF16), shape((frag_dev,) + square, F32),
            shape((slots,) + square, BF16), shape((frag_dev,) + square, BF16), slabs, slabs,
            shape((4 * slots + 2 * frag_dev,), I32),
        ),
        (vmem,) * 7 + (smem,),
        [
            pltpu.SMEM(basis_size.shape, I32), pltpu.SMEM((slots,), I32), pltpu.SMEM((slots,), I32),
            pltpu.SMEM((1,), I32), pltpu.VMEM((3, frag_dev, nbasis), F32), pltpu.VMEM(grid_region.shape, I32),
            pltpu.VMEM((2 * frag_dev + 1,) + square, F32), pltpu.SemaphoreType.DMA((6 + slots,)),
        ],
        work,
    )(
        in_hbm(basis_size), in_hbm(pair_first), in_hbm(pair_second), dimer_count, density, in_hbm(coupling),
        in_hbm(jnp.transpose(source_coords, (1, 0, 2))), in_hbm(grid_region),
    )

    next_sum = call(next_kernel, "next_sum", [vmem] * 2, shape(halves, BF16), vmem)(
        next_keep, turned(next_send, "sub", 1)
    )
    before = shifted(next_sum, "frag", 1)

    far = turned(far, "frag", teams // 2)
    while near.shape[0] > 2:
        near, rest = near + far, near.shape[0] // 2
        near, far = near[:rest], turned(near[rest:], "frag", rest)

    other = turned(mine, "sub", 1)
    own_keep, own_send = call(
        left_kernel,
        "left",
        [smem] + [vmem] * 5,
        (shape(halves, F32), shape(halves, BF16)),
        (vmem,) * 2,
        [pltpu.VMEM((2 * frag_dev,) + square, BF16), pltpu.VMEM((frag_dev + 1,) + square, F32)],
        work,
    )(ids, masked, mine, other, own_part, factors)

    slab = shape((1, pts_rows, block_cols), F32)
    own, pot, passed, *parts = call(
        sum_kernel,
        "own_sum",
        [vmem] * 5,
        (shape((frag_dev, share, nbasis), F32), slab, slab)
        + (shape((frag_dev, share, nbasis), BF16),) * (grid_size - 1),
        (vmem,) * (2 + grid_size),
    )(own_keep, turned(own_send, "sub", 1), before, near, far)
    parts = [turned(part, "grid", step) for step, part in enumerate(parts, 1)]
    passed = turned(passed, "frag", 1)

    scale = 8.0 / math.sqrt(frag_dev * teams * nbasis)
    return call(
        functools.partial(last_kernel, scale, slots),
        "last",
        [smem] + [vmem] * (4 + len(parts)),
        (shape((frag_dev, share, nbasis), BF16), shape((pts_rows, block_cols), F32)),
        (vmem,) * 2,
    )(ids, masked, own, pot, passed, *parts)


def solution(mesh):
    placed = (
        P(("groups", "frag"), None, None),
        P(),
        P(("groups", "frag", "grid", "sub"), None, None),
        P(("frag", "grid", "sub")),
        P(("frag", "grid", "sub")),
        P(("frag", "grid", "sub")),
        P(("groups", "frag"), None, None),
        P(("grid", "sub"), None),
    )
    return jax.shard_map(
        per_device,
        mesh=mesh,
        in_specs=placed,
        out_specs=(
            P(("groups", "frag"), ("grid", "sub"), None),
            P(("groups", "grid", "sub"), "frag"),
        ),
        check_vma=False,
    )
```

```python
import functools
import math

import jax
import jax.numpy as jnp
from jax import lax
from jax.experimental import pallas as pl
from jax.experimental.pallas import tpu as pltpu
from jax.sharding import PartitionSpec as P

VMEM_LIMIT = 24 * 1024 * 1024
EXTRA = 16
BF16, F32, I32 = jnp.bfloat16, jnp.float32, jnp.int32


def live_square(values, size):
    rows = lax.broadcasted_iota(I32, values.shape, 0)
    cols = lax.broadcasted_iota(I32, values.shape, 1)
    return jnp.where((rows < size) & (cols < size), values.astype(F32), 0.0).astype(BF16)


def charges(read, nbasis):
    tile = 128
    parts = []
    for at in range(0, nbasis, tile):
        block = read(at, at + tile).astype(F32)
        rows = lax.broadcasted_iota(I32, block.shape, 0)
        cols = lax.broadcasted_iota(I32, block.shape, 1)
        parts.append(jnp.sum(jnp.where(rows == cols, block, 0.0), axis=1, keepdims=True))
    return jnp.concatenate(parts, axis=0)


def charge_row(masked_ref, f):
    nbasis, tile = masked_ref.shape[1], 128
    parts = []
    for at in range(0, nbasis, tile):
        block = masked_ref[f, at : at + tile, at : at + tile].astype(F32)
        rows = lax.broadcasted_iota(I32, block.shape, 0)
        cols = lax.broadcasted_iota(I32, block.shape, 1)
        parts.append(jnp.sum(jnp.where(rows == cols, block, 0.0), axis=0, keepdims=True))
    return jnp.concatenate(parts, axis=1)


def at_rows(block, size):
    return pl.ds(pl.multiple_of(block * size, size), size)


def thirds(values):
    high = values.astype(BF16).astype(F32)
    middle = (values - high).astype(BF16).astype(F32)
    return [high, middle, values - high - middle]


def field(charge, place, point, row_x):
    src_x, src_y, src_z = place
    point_y, point_z = point
    in_plane = (point_y - src_y) ** 2 + (point_z - src_z) ** 2 + 1.0
    return [
        jnp.sum(charge * lax.rsqrt((x - src_x) ** 2 + in_plane), axis=0, keepdims=True) for x in row_x
    ]


def block_points(block, block_cols):
    col = block * block_cols + lax.broadcasted_iota(I32, (1, block_cols), 1)
    return 0.25 * (col // 64).astype(F32), 0.25 * (col % 64).astype(F32)


def row_places(pts_rows):
    member = lax.axis_index("grid") * lax.axis_size("sub") + lax.axis_index("sub")
    return [0.25 * (member * pts_rows + r).astype(F32) for r in range(pts_rows)]


def as_columns(rows):
    turned_rows = jnp.transpose(jnp.concatenate(rows + [jnp.zeros((8 - len(rows), rows[0].shape[1]), F32)]))
    return [turned_rows[:, d : d + 1] for d in range(len(rows))]


def place_rows(extra):
    return [sum(extra[3 * d + k : 3 * d + k + 1] for k in range(3)) for d in range(3)]


def by_core(total_ref, row, keep_ref, send_ref):
    me, rows = lax.axis_index("sub"), keep_ref.shape[-2]
    for f in range(keep_ref.shape[0]):
        keep_ref[f] = total_ref[f, pl.ds(row + pl.multiple_of(me * rows, rows), rows), :].astype(keep_ref.dtype)
        other = total_ref[f, pl.ds(row + pl.multiple_of((1 - me) * rows, rows), rows), :]
        send_ref[f, :rows] = other.astype(send_ref.dtype)


def pipelined(slots, first_dot, second_dot, add):
    held = None
    for slot in range(slots + 1):
        now = first_dot(slot).astype(BF16) if slot < slots else None
        if held is not None:
            add(slot - 1, second_dot(slot - 1, held))
        held = now


def dot(a, b):
    return jnp.dot(a, b, preferred_element_type=F32)


def dot_t(a, b):
    return lax.dot_general(a, b, (((1,), (1,)), ((), ())), preferred_element_type=F32)


def fetch(pairs, sems):
    copies = [pltpu.make_async_copy(source, target, sems.at[i]) for i, (source, target) in enumerate(pairs)]
    for copy in copies:
        copy.start()
    return copies


def head_kernel(density_hbm, coords_hbm, payload_ref, coords_ref, sems):
    half, nbasis = payload_ref.shape[0], payload_ref.shape[2]
    at = lax.axis_index("sub") * half
    copies = fetch(
        [(density_hbm.at[pl.ds(at, half)], payload_ref.at[:, pl.ds(0, nbasis)]), (coords_hbm, coords_ref)], sems
    )
    copies[1].wait()
    for f in range(half):
        rows = [part for d in range(3) for part in thirds(coords_ref[d, pl.ds(at + f, 1), :])]
        rows.append(jnp.zeros((EXTRA - len(rows), nbasis), F32))
        payload_ref[f, nbasis:, :] = jnp.concatenate(rows).astype(BF16)
    copies[0].wait()


def right_kernel(
    size_hbm, first_hbm, second_hbm, count_ref, density_hbm, coupling_hbm, coords_hbm, region_hbm,
    keep_ref, send_ref, own_ref, factor_ref, masked_ref, ids_ref, sizes_ref, here_ref, sources_ref, *rest,
):
    slab_refs, rest = rest[:4], rest[4:]
    size_ref, first_ref, second_ref, density_ref, coords_ref, region_ref, total_ref, sems = rest
    frag_dev, nbasis, slots = masked_ref.shape[0], masked_ref.shape[1], factor_ref.shape[0]
    copies = fetch(
        [
            (size_hbm, size_ref), (first_hbm, first_ref), (second_hbm, second_ref),
            (density_hbm, density_ref), (coords_hbm, coords_ref), (region_hbm, region_ref),
        ]
        + [(coupling_hbm.at[s], factor_ref.at[s]) for s in range(slots)],
        sems,
    )
    total_ref[...] = jnp.zeros_like(total_ref)
    for copy in copies[:6]:
        copy.wait()
    team = lax.axis_index("frag")
    base = team * frag_dev
    trash = 2 * frag_dev
    for s in range(slots):
        live = s < count_ref[0]
        first = jnp.clip(first_ref[s] - base, 0, frag_dev - 1)
        second = jnp.clip(second_ref[s] - base, 0, trash - 1)
        ids_ref[s] = first
        ids_ref[slots + s] = second
        ids_ref[2 * slots + s] = jnp.where(live, first, frag_dev)
        ids_ref[3 * slots + s] = jnp.where(live, second, trash)
    for f in range(2 * frag_dev):
        sizes_ref[f] = jnp.full((8, 128), size_ref[lax.rem(base + f, size_ref.shape[0])], I32)
    for f in range(frag_dev):
        masked_ref[f] = live_square(density_ref[f], size_ref[base + f])
    for copy in copies[6:]:
        copy.wait()

    for f in range(frag_dev):
        rows = [part for d in range(3) for part in thirds(coords_ref[d, f : f + 1, :])]
        rows.append(charge_row(masked_ref, f))
        rows.append(jnp.zeros((EXTRA - len(rows), nbasis), F32))
        sources_ref[f] = jnp.concatenate(rows).astype(BF16)

    pts_rows = region_ref.shape[0]
    each, block_cols = slab_refs[0].shape[0], slab_refs[0].shape[2]
    teams = len(slab_refs) * each
    sources = [
        (
            charges(lambda low, high, f=f: masked_ref[f, low:high, low:high], nbasis),
            as_columns([coords_ref[d, f : f + 1, :] for d in range(3)]),
        )
        for f in range(frag_dev)
    ]
    row_x = row_places(pts_rows)

    def one_block(step, slab_ref, at):
        block = lax.rem(team + step, teams)
        point = block_points(block, block_cols)
        region = region_ref[:, pl.ds(pl.multiple_of(block * block_cols, block_cols), block_cols)]
        fields = [field(charge, place, point, row_x) for charge, place in sources]
        for r in range(pts_rows):
            here = [jnp.where(region[r : r + 1] != base + f, fields[f][r], 0.0) for f in range(frag_dev)]
            slab_ref[at, r : r + 1, :] = sum(here)

    if each == 1:
        one_block(0, slab_refs[0], 0)
        one_block(2, slab_refs[2], 0)
    else:

        @pl.loop(0, each)
        def _(step):
            for k, slab_ref in enumerate(slab_refs):
                one_block(k * each + step, slab_ref, step)

    for k in (1, teams - 1):
        slab_refs[k // each][k % each] = jnp.zeros((pts_rows, block_cols), F32)
    here_ref[...] = region_ref[:, pl.ds(pl.multiple_of(team * block_cols, block_cols), block_cols)]

    def add(s, corr):
        target = ids_ref[3 * slots + s]
        total_ref[target] = total_ref[target] + corr

    pipelined(
        slots,
        lambda s: dot(factor_ref[s].T, masked_ref[ids_ref[s]]),
        lambda s, right: dot(right, factor_ref[s]),
        add,
    )
    own_ref[...] = total_ref[:frag_dev]
    by_core(total_ref.at[pl.ds(frag_dev, frag_dev)], 0, keep_ref, send_ref)
    send_ref[:, keep_ref.shape[1] :, :] = jnp.zeros((frag_dev, EXTRA, nbasis), BF16)


def left_kernel(
    ids_ref, sizes_ref, masked_ref, mine_ref, other_ref, own_ref, factor_ref, after_ref,
    keep_ref, send_ref,
    all_ref, total_ref,
):
    frag_dev, nbasis = masked_ref.shape[0], masked_ref.shape[1]
    slots, half = factor_ref.shape[0], mine_ref.shape[0]
    me = lax.axis_index("sub")
    for f in range(frag_dev):
        all_ref[f] = masked_ref[f]
    for f in range(half):
        at = frag_dev + me * half + f
        all_ref[at] = live_square(mine_ref[f, :nbasis], sizes_ref[at, 0:1, 0:1])
        at = frag_dev + (1 - me) * half + f
        all_ref[at] = live_square(other_ref[f, :nbasis], sizes_ref[at, 0:1, 0:1])
    total_ref[:frag_dev] = own_ref[...]
    total_ref[frag_dev] = jnp.zeros_like(total_ref[frag_dev])

    def add(s, corr):
        target = ids_ref[2 * slots + s]
        total_ref[target] = total_ref[target] + corr

    pipelined(
        slots,
        lambda s: dot(factor_ref[s], all_ref[ids_ref[slots + s]]),
        lambda s, left: dot_t(left, factor_ref[s]),
        add,
    )
    for g in range(keep_ref.shape[0]):
        by_core(total_ref, 2 * g * keep_ref.shape[2], keep_ref.at[g], send_ref.at[g])


def own_sum_kernel(keep_ref, recv_ref, own_ref, *part_refs):
    grid_size, frag_dev, share, nbasis = keep_ref.shape
    me = lax.axis_index("grid")
    own_ref[...] = keep_ref[me] + recv_ref[me].astype(F32)
    for step, part_ref in enumerate(part_refs, 1):
        at = lax.rem(me + step, grid_size)
        for f in range(frag_dev):
            part_ref[f * share : (f + 1) * share] = (keep_ref[at, f] + recv_ref[at, f].astype(F32)).astype(BF16)
        part_ref[frag_dev * share :] = jnp.zeros((EXTRA, nbasis), BF16)


def relay_kernel(here_ref, in_ref, out_ref):
    out_ref[...] = in_ref[...]


def next_kernel(keep_ref, recv_ref, sources_ref, *out_refs):
    out_refs, after_ref = out_refs[:-1], out_refs[-1]
    after_ref[...] = jnp.zeros_like(after_ref)
    rounds = len(out_refs)
    rows = out_refs[0].shape[1] - EXTRA
    for j, out_ref in enumerate(out_refs):
        at = at_rows(lax.rem(lax.axis_index("grid") + j, rounds), rows) if rounds > 1 else slice(0, rows)
        total = keep_ref[:, at, :].astype(F32) + recv_ref[:, at, :].astype(F32)
        out_ref[:, :rows, :] = total.astype(BF16)
        out_ref[:, rows:, :] = sources_ref[...]


def before_kernel(own_ref, far_ref, later_ref, *refs):
    in_refs, (keep_ref, send_ref, pot_ref) = refs[:-3], refs[-3:]
    me, rows = lax.axis_index("sub"), keep_ref.shape[1]
    keep_ref[...] = own_ref[...] + sum(r[:, at_rows(me, rows), :].astype(F32) for r in in_refs)
    send_ref[...] = sum(r[:, at_rows(1 - me, rows), :].astype(F32) for r in in_refs).astype(BF16)
    pot_ref[...] = far_ref[...] + later_ref[...]


def felt(sources, here_ref, out_ref):
    pts_rows, block_cols = here_ref.shape
    point, row_x = block_points(lax.axis_index("frag"), block_cols), row_places(pts_rows)
    totals = [jnp.zeros((1, block_cols), F32) for _ in range(pts_rows)]
    for fragment, charge, place in sources:
        fields = field(charge, place, point, row_x)
        for r in range(pts_rows):
            totals[r] = totals[r] + jnp.where(here_ref[r : r + 1, :] != fragment, fields[r], 0.0)
    for r in range(pts_rows):
        out_ref[0, r : r + 1, :] = totals[r]


def after_kernel(sizes_ref, mine_ref, other_ref, here_ref, out_ref):
    half, nbasis = mine_ref.shape[0], mine_ref.shape[2]
    me, team, teams = lax.axis_index("sub"), lax.axis_index("frag"), lax.axis_size("frag")
    column = lax.broadcasted_iota(I32, (nbasis, 1), 0)
    sources = []
    for ref, start in ((mine_ref, me * half), (other_ref, (1 - me) * half)):
        for f in range(half):
            charge = charges(lambda low, high, ref=ref, f=f: ref[f, low:high, low:high], nbasis)
            charge = jnp.where(column < sizes_ref[2 * half + start + f, 0:1, 0:1], charge, 0.0)
            place = as_columns(place_rows(ref[f, nbasis:, :].astype(F32)))
            sources.append((lax.rem(team + 1, teams) * 2 * half + start + f, charge, place))
    felt(sources, here_ref, out_ref)


def prior_kernel(here_ref, piece_ref, out_ref):
    frag_dev, team, teams = piece_ref.shape[0], lax.axis_index("frag"), lax.axis_size("frag")
    sources = []
    for f in range(frag_dev):
        extra = piece_ref[f, piece_ref.shape[1] - EXTRA :, :].astype(F32)
        *place, charge = as_columns(place_rows(extra) + [extra[9:10]])
        sources.append((lax.rem(team + teams - 1, teams) * frag_dev + f, charge, place))
    felt(sources, here_ref, out_ref)


def last_kernel(scale, slab_count, sizes_ref, masked_ref, own_ref, recv_ref, *rest):
    slab_refs, part_refs, (out_ref, potential_ref) = rest[:slab_count], rest[slab_count:-2], rest[-2:]
    frag_dev, share, nbasis = out_ref.shape
    member = lax.axis_index("grid") * lax.axis_size("sub") + lax.axis_index("sub")
    row_start = pl.multiple_of(member * share, share)
    rows = row_start + lax.broadcasted_iota(I32, (share, nbasis), 0)
    cols = lax.broadcasted_iota(I32, (share, nbasis), 1)
    for f in range(frag_dev):
        size = sizes_ref[f, 0:1, 0:1]
        correction = own_ref[f] + recv_ref[f].astype(F32)
        for part_ref in part_refs:
            correction = correction + part_ref[f * share : (f + 1) * share, :].astype(F32)
        correction = jnp.where((rows < size) & (cols < size), correction, 0.0)
        out_ref[f] = (masked_ref[f, pl.ds(row_start, share), :].astype(F32) + correction).astype(BF16)
    potential_ref[...] = sum(slab_ref[0] for slab_ref in slab_refs) * scale


def turned(value, axis, steps):
    count = lax.axis_size(axis)
    return lax.ppermute(value, axis, [(s, (s + steps) % count) for s in range(count)])


def in_hbm(value):
    return pltpu.with_memory_space_constraint(value, pltpu.HBM)


def shape(dims, dtype):
    return jax.ShapeDtypeStruct(dims, dtype)


def per_device(
    density, basis_size, coupling, pair_first, pair_second, dimer_count, source_coords, grid_region
):
    frag_dev, nbasis, _ = density.shape
    slots = coupling.shape[0]
    teams, grid_size, sub_size = (lax.axis_size(a) for a in ("frag", "grid", "sub"))
    assert sub_size == 2 and frag_dev == 2 and grid_size % sub_size == 0
    rounds = grid_size // sub_size
    assert teams >= 4 and teams & (teams - 1) == 0
    share = nbasis // (grid_size * sub_size)
    half = frag_dev // sub_size
    pts_rows, total_cols = grid_region.shape
    block_cols = total_cols // teams

    smem = pl.BlockSpec(memory_space=pltpu.SMEM)
    vmem = pl.BlockSpec(memory_space=pltpu.VMEM)
    hbm = pl.BlockSpec(memory_space=pltpu.HBM)
    square = (nbasis, nbasis)

    def call(kernel, name, ins, outs, out_specs, scratch=(), flops=0):
        return pl.pallas_call(
            kernel,
            out_shape=outs,
            in_specs=ins,
            out_specs=out_specs,
            scratch_shapes=scratch,
            compiler_params=pltpu.CompilerParams(vmem_limit_bytes=VMEM_LIMIT),
            cost_estimate=pl.CostEstimate(flops=flops, bytes_accessed=1 << 20, transcendentals=0),
            name=name,
        )

    work = 4 * slots * nbasis**3
    by_chip = (grid_size, frag_dev, share, nbasis)
    halves = shape((frag_dev, nbasis // sub_size, nbasis), BF16)
    sent_halves = shape((frag_dev, nbasis // sub_size + EXTRA, nbasis), BF16)
    places = in_hbm(jnp.transpose(source_coords, (1, 0, 2)))
    payload = call(
        head_kernel,
        "head",
        [hbm] * 2,
        shape((half, nbasis + EXTRA, nbasis), BF16),
        vmem,
        [pltpu.VMEM((3, frag_dev, nbasis), F32), pltpu.SemaphoreType.DMA((2,))],
    )(in_hbm(density), places)
    mine = turned(payload, "frag", -1)

    next_keep, next_send, own_part, factors, masked, ids, sizes, here, sources, *slabs = call(
        right_kernel,
        "right",
        [hbm] * 3 + [smem] + [hbm] * 4,
        (
            halves, sent_halves, shape((frag_dev,) + square, F32),
            shape((slots,) + square, BF16), shape((frag_dev,) + square, BF16),
            shape((4 * slots,), I32), shape((2 * frag_dev, 8, 128), I32), shape((pts_rows, block_cols), I32),
            shape((frag_dev, EXTRA, nbasis), BF16),
        ) + (shape((teams // 4, pts_rows, block_cols), F32),) * 4,
        (vmem,) * 5 + (smem,) + (vmem,) * 7,
        [
            pltpu.SMEM(basis_size.shape, I32), pltpu.SMEM((slots,), I32), pltpu.SMEM((slots,), I32),
            pltpu.VMEM(density.shape, BF16), pltpu.VMEM((3, frag_dev, nbasis), F32),
            pltpu.VMEM(grid_region.shape, I32), pltpu.VMEM((2 * frag_dev + 1,) + square, F32),
            pltpu.SemaphoreType.DMA((6 + slots,)),
        ],
        work,
    )(
        in_hbm(basis_size), in_hbm(pair_first), in_hbm(pair_second), dimer_count, in_hbm(density),
        in_hbm(coupling), places, in_hbm(grid_region),
    )

    if teams == 4:
        home, far = slabs[0], turned(slabs[2], "frag", 2)
    else:
        slabs = jnp.concatenate(slabs)
        while slabs.shape[0] > 1:
            rest = slabs.shape[0] // 2
            slabs = slabs[:rest] + turned(slabs[rest:], "frag", rest)
        home, far = slabs, jnp.zeros_like(slabs)

    *pieces, after = call(
        next_kernel,
        "next_sum",
        [vmem] * 3,
        [shape((frag_dev, nbasis // grid_size + EXTRA, nbasis), BF16)] * rounds + [shape((8, 128), F32)],
        (vmem,) * (rounds + 1),
    )(next_keep, turned(next_send, "sub", 1), sources)
    for j, value in enumerate(pieces):
        pairs = [
            (
                (t * grid_size + g) * sub_size + c,
                ((t + 1) % teams * grid_size + c * rounds + (g + j) % rounds) * sub_size + g // rounds,
            )
            for t in range(teams)
            for g in range(grid_size)
            for c in range(sub_size)
        ]
        pieces[j] = lax.ppermute(value, ("frag", "grid", "sub"), pairs)

    mine = call(relay_kernel, "relay", [vmem] * 2, shape(payload.shape, BF16), vmem)(here, mine)
    other = turned(mine, "sub", 1)
    own_keep, own_send = call(
        left_kernel,
        "left",
        [smem] + [vmem] * 7,
        (shape(by_chip, F32), shape(by_chip, BF16)),
        (vmem,) * 2,
        [pltpu.VMEM((2 * frag_dev,) + square, BF16), pltpu.VMEM((frag_dev + 1,) + square, F32)],
        work,
    )(ids, sizes, masked, mine, other, own_part, factors, after)
    mine_rows = (frag_dev, share, nbasis)
    own, *parts = call(
        own_sum_kernel,
        "own_sum",
        [vmem] * 2,
        [shape(mine_rows, F32)] + [shape((frag_dev * share + EXTRA, nbasis), BF16)] * (grid_size - 1),
        (vmem,) * grid_size,
    )(own_keep, turned(own_send, "sub", 1))
    parts = [turned(part, "grid", step) for step, part in enumerate(parts, 1)]

    slab = shape((1, pts_rows, block_cols), F32)
    later = call(after_kernel, "after", [vmem] * 4, slab, vmem)(sizes, mine, other, here)
    own, passed, far = call(
        before_kernel,
        "before",
        [vmem] * (3 + rounds),
        (shape(mine_rows, F32), shape(mine_rows, BF16), slab),
        (vmem,) * 3,
    )(own, far, later, *pieces)
    passed = turned(passed, "sub", 1)
    prior = call(prior_kernel, "prior", [vmem] * 2, slab, vmem)(here, pieces[0])

    scale = 8.0 / math.sqrt(frag_dev * teams * nbasis)
    return call(
        functools.partial(last_kernel, scale, 3),
        "last",
        [vmem] * (7 + len(parts)),
        (shape(mine_rows, BF16), shape((pts_rows, block_cols), F32)),
        (vmem,) * 2,
    )(sizes, masked, own, passed, home, far, prior, *parts)


def solution(mesh):
    placed = (
        P(("groups", "frag"), None, None),
        P(),
        P(("groups", "frag", "grid", "sub"), None, None),
        P(("frag", "grid", "sub")),
        P(("frag", "grid", "sub")),
        P(("frag", "grid", "sub")),
        P(("groups", "frag"), None, None),
        P(("grid", "sub"), None),
    )
    return jax.shard_map(
        per_device,
        mesh=mesh,
        in_specs=placed,
        out_specs=(
            P(("groups", "frag"), ("grid", "sub"), None),
            P(("groups", "grid", "sub"), "frag"),
        ),
        check_vma=False,
    )
```

```python
import functools
import math

import jax
import jax.numpy as jnp
from jax import lax
from jax.experimental import pallas as pl
from jax.experimental.pallas import tpu as pltpu
from jax.sharding import PartitionSpec as P

VMEM_LIMIT = 24 * 1024 * 1024
EXTRA = 16
BF16, F32, I32 = jnp.bfloat16, jnp.float32, jnp.int32


def live_square(values, size):
    rows = lax.broadcasted_iota(I32, values.shape, 0)
    cols = lax.broadcasted_iota(I32, values.shape, 1)
    return jnp.where((rows < size) & (cols < size), values.astype(F32), 0.0).astype(BF16)


def charge_row(read, nbasis):
    tile = 128
    parts = []
    for at in range(0, nbasis, tile):
        block = read(at, at + tile).astype(F32)
        rows = lax.broadcasted_iota(I32, block.shape, 0)
        cols = lax.broadcasted_iota(I32, block.shape, 1)
        parts.append(jnp.sum(jnp.where(rows == cols, block, 0.0), axis=0, keepdims=True))
    return jnp.concatenate(parts, axis=1)


def at_rows(block, size):
    return pl.ds(pl.multiple_of(block * size, size), size)


def thirds(values):
    high = values.astype(BF16).astype(F32)
    middle = (values - high).astype(BF16).astype(F32)
    return [high, middle, values - high - middle]


def field(charge, place, block, block_cols, row_x):
    src_x, src_y, src_z = place
    point_z = 0.25 * lax.broadcasted_iota(I32, (64, charge.shape[1]), 0).astype(F32)
    along_z = (point_z - src_z) ** 2 + 1.0
    parts = []
    for x in row_x:
        for step in range(block_cols // 64):
            point_y = 0.25 * (block * (block_cols // 64) + step).astype(F32)
            in_plane = (x - src_x) ** 2 + (point_y - src_y) ** 2
            value = charge * lax.rsqrt(along_z + in_plane)
            parts.append(sum(value[:, at : at + 128] for at in range(0, value.shape[1], 128)))
    return jnp.concatenate(parts)


def over_lanes(points, block_cols, pts_rows):
    rows = jnp.concatenate(points)
    ones = jnp.ones((16, 128), BF16)
    total = sum(dot_t(ones, part.astype(BF16)) for part in thirds(rows))
    size = pts_rows * block_cols
    return [
        [total[0:1, k * size + r * block_cols : k * size + (r + 1) * block_cols] for r in range(pts_rows)]
        for k in range(len(points))
    ]


def row_places(pts_rows):
    member = lax.axis_index("grid") * lax.axis_size("sub") + lax.axis_index("sub")
    return [0.25 * (member * pts_rows + r).astype(F32) for r in range(pts_rows)]


def place_rows(extra):
    return [sum(extra[3 * d + k : 3 * d + k + 1] for k in range(3)) for d in range(3)]


def by_core(total_ref, row, keep_ref, send_ref):
    me, rows = lax.axis_index("sub"), keep_ref.shape[-2]
    for f in range(keep_ref.shape[0]):
        keep_ref[f] = total_ref[f, pl.ds(row + pl.multiple_of(me * rows, rows), rows), :].astype(keep_ref.dtype)
        other = total_ref[f, pl.ds(row + pl.multiple_of((1 - me) * rows, rows), rows), :]
        send_ref[f, :rows] = other.astype(send_ref.dtype)


def pipelined(slots, first_dot, second_dot, add):
    held = None
    for slot in range(slots + 1):
        now = first_dot(slot).astype(BF16) if slot < slots else None
        if held is not None:
            add(slot - 1, second_dot(slot - 1, held))
        held = now


def dot(a, b):
    return jnp.dot(a, b, preferred_element_type=F32)


def dot_t(a, b):
    return lax.dot_general(a, b, (((1,), (1,)), ((), ())), preferred_element_type=F32)


def fetch(pairs, sems):
    copies = [pltpu.make_async_copy(source, target, sems.at[i]) for i, (source, target) in enumerate(pairs)]
    for copy in copies:
        copy.start()
    return copies


def head_kernel(density_hbm, coords_hbm, payload_ref, coords_ref, sems):
    half, nbasis = payload_ref.shape[0], payload_ref.shape[2]
    at = lax.axis_index("sub") * half
    copies = fetch(
        [(density_hbm.at[pl.ds(at, half)], payload_ref.at[:, pl.ds(0, nbasis)]), (coords_hbm, coords_ref)], sems
    )
    copies[1].wait()
    for f in range(half):
        rows = [part for d in range(3) for part in thirds(coords_ref[d, pl.ds(at + f, 1), :])]
        rows.append(jnp.zeros((EXTRA - len(rows), nbasis), F32))
        payload_ref[f, nbasis:, :] = jnp.concatenate(rows).astype(BF16)
    copies[0].wait()


def right_kernel(
    size_hbm, first_hbm, second_hbm, count_ref, density_hbm, coupling_hbm, coords_hbm, region_hbm,
    keep_ref, send_ref, own_ref, factor_ref, masked_ref, ids_ref, sizes_ref, here_ref, sources_ref, *rest,
):
    slab_refs, rest = rest[:4], rest[4:]
    size_ref, first_ref, second_ref, density_ref, coords_ref, region_ref, total_ref, sems = rest
    frag_dev, nbasis, slots = masked_ref.shape[0], masked_ref.shape[1], factor_ref.shape[0]
    copies = fetch(
        [
            (size_hbm, size_ref), (first_hbm, first_ref), (second_hbm, second_ref),
            (density_hbm, density_ref), (coords_hbm, coords_ref), (region_hbm, region_ref),
        ]
        + [(coupling_hbm.at[s], factor_ref.at[s]) for s in range(slots)],
        sems,
    )
    total_ref[...] = jnp.zeros_like(total_ref)
    for copy in copies[:6]:
        copy.wait()
    team = lax.axis_index("frag")
    base = team * frag_dev
    trash = 2 * frag_dev
    for s in range(slots):
        live = s < count_ref[0]
        first = jnp.clip(first_ref[s] - base, 0, frag_dev - 1)
        second = jnp.clip(second_ref[s] - base, 0, trash - 1)
        ids_ref[s] = first
        ids_ref[slots + s] = second
        ids_ref[2 * slots + s] = jnp.where(live, first, frag_dev)
        ids_ref[3 * slots + s] = jnp.where(live, second, trash)
    for f in range(2 * frag_dev):
        sizes_ref[f] = jnp.full((8, 128), size_ref[lax.rem(base + f, size_ref.shape[0])], I32)
    for f in range(frag_dev):
        masked_ref[f] = live_square(density_ref[f], size_ref[base + f])
    sources = [
        (
            charge_row(lambda low, high, f=f: masked_ref[f, low:high, low:high], nbasis),
            [coords_ref[d, f : f + 1, :] for d in range(3)],
        )
        for f in range(frag_dev)
    ]
    for f in range(frag_dev):
        rows = [part for d in range(3) for part in thirds(coords_ref[d, f : f + 1, :])]
        rows.append(sources[f][0])
        rows.append(jnp.zeros((EXTRA - len(rows), nbasis), F32))
        sources_ref[f] = jnp.concatenate(rows).astype(BF16)

    pts_rows = region_ref.shape[0]
    each, block_cols = slab_refs[0].shape[0], slab_refs[0].shape[2]
    teams = len(slab_refs) * each
    row_x = row_places(pts_rows)

    def one_block(step, slab_ref, at):
        block = lax.rem(team + step, teams)
        region = region_ref[:, pl.ds(pl.multiple_of(block * block_cols, block_cols), block_cols)]
        fields = [field(charge, place, block, block_cols, row_x) for charge, place in sources]
        fields = over_lanes(fields, block_cols, pts_rows)
        for r in range(pts_rows):
            here = [jnp.where(region[r : r + 1] != base + f, fields[f][r], 0.0) for f in range(frag_dev)]
            slab_ref[at, r : r + 1, :] = sum(here)

    if each == 1:
        one_block(0, slab_refs[0], 0)
        one_block(2, slab_refs[2], 0)
    else:

        @pl.loop(0, each)
        def _(step):
            for k, slab_ref in enumerate(slab_refs):
                one_block(k * each + step, slab_ref, step)

    for k in (1, teams - 1):
        slab_refs[k // each][k % each] = jnp.zeros((pts_rows, block_cols), F32)
    here_ref[...] = region_ref[:, pl.ds(pl.multiple_of(team * block_cols, block_cols), block_cols)]

    for copy in copies[6:]:
        copy.wait()

    def add(s, corr):
        target = ids_ref[3 * slots + s]
        total_ref[target] = total_ref[target] + corr

    pipelined(
        slots,
        lambda s: dot(factor_ref[s].T, masked_ref[ids_ref[s]]),
        lambda s, right: dot(right, factor_ref[s]),
        add,
    )
    own_ref[...] = total_ref[:frag_dev]
    by_core(total_ref.at[pl.ds(frag_dev, frag_dev)], 0, keep_ref, send_ref)
    send_ref[:, keep_ref.shape[1] :, :] = jnp.zeros((frag_dev, EXTRA, nbasis), BF16)


def left_kernel(
    ids_ref, sizes_ref, masked_ref, mine_ref, other_ref, own_ref, factor_ref, after_ref,
    keep_ref, *rest,
):
    send_refs, (all_ref, total_ref) = rest[:-2], rest[-2:]
    frag_dev, nbasis = masked_ref.shape[0], masked_ref.shape[1]
    slots, half = factor_ref.shape[0], mine_ref.shape[0]
    me = lax.axis_index("sub")
    for f in range(frag_dev):
        all_ref[f] = masked_ref[f]
    for f in range(half):
        at = frag_dev + me * half + f
        all_ref[at] = live_square(mine_ref[f, :nbasis], sizes_ref[at, 0:1, 0:1])
        at = frag_dev + (1 - me) * half + f
        all_ref[at] = live_square(other_ref[f, :nbasis], sizes_ref[at, 0:1, 0:1])
    total_ref[:frag_dev] = own_ref[...]
    total_ref[frag_dev] = jnp.zeros_like(total_ref[frag_dev])

    def add(s, corr):
        target = ids_ref[2 * slots + s]
        total_ref[target] = total_ref[target] + corr

    pipelined(
        slots,
        lambda s: dot(factor_ref[s], all_ref[ids_ref[slots + s]]),
        lambda s, left: dot_t(left, factor_ref[s]),
        add,
    )
    grid_size, _, share, _ = keep_ref.shape
    for g in range(grid_size):
        for f in range(frag_dev):
            chip = total_ref.at[f, 2 * g * share : 2 * (g + 1) * share]
            keep_ref[g, f] = chip[at_rows(me, share), :]
            send_refs[f][g] = chip[at_rows(1 - me, share), :].astype(BF16)


def own_sum_kernel(keep_ref, *rest):
    grid_size, frag_dev, share, nbasis = keep_ref.shape
    recv_refs, own_ref, part_refs = rest[:frag_dev], rest[frag_dev], rest[frag_dev + 1 :]
    me = lax.axis_index("grid")
    for f in range(frag_dev):
        own_ref[f] = keep_ref[me, f] + recv_refs[f][me].astype(F32)
        for step, part_ref in enumerate(part_refs, 1):
            at = lax.rem(me + step, grid_size)
            part_ref[f] = (keep_ref[at, f] + recv_refs[f][at].astype(F32)).astype(BF16)


def relay_kernel(here_ref, in_ref, out_ref):
    out_ref[...] = in_ref[...]


def next_kernel(keep_ref, recv_ref, sources_ref, *out_refs):
    out_refs, after_ref = out_refs[:-1], out_refs[-1]
    after_ref[...] = jnp.zeros_like(after_ref)
    rounds = len(out_refs)
    rows = out_refs[0].shape[1] - EXTRA
    for j, out_ref in enumerate(out_refs):
        at = at_rows(lax.rem(lax.axis_index("grid") + j, rounds), rows) if rounds > 1 else slice(0, rows)
        total = keep_ref[:, at, :].astype(F32) + recv_ref[:, at, :].astype(F32)
        out_ref[:, :rows, :] = total.astype(BF16)
        out_ref[:, rows:, :] = sources_ref[...]


def before_kernel(*refs):
    in_refs, (keep_ref, send_ref) = refs[:-2], refs[-2:]
    me, rows = lax.axis_index("sub"), keep_ref.shape[1]
    keep_ref[...] = sum(r[:, at_rows(me, rows), :].astype(F32) for r in in_refs)
    send_ref[...] = sum(r[:, at_rows(1 - me, rows), :].astype(F32) for r in in_refs).astype(BF16)


def middle_kernel(own_ref, home_ref, far_ref, later_ref, prior_ref, *rest):
    part_refs, (out_ref, pot_ref) = rest[:-2], rest[-2:]
    out_ref[...] = own_ref[...] + sum(part_ref[...].astype(F32) for part_ref in part_refs)
    pot_ref[...] = home_ref[...] + far_ref[...] + later_ref[...] + prior_ref[...]


def felt(sources, here_ref, out_ref):
    pts_rows, block_cols = here_ref.shape
    team, row_x = lax.axis_index("frag"), row_places(pts_rows)
    totals = [jnp.zeros((1, block_cols), F32) for _ in range(pts_rows)]
    fields = [field(charge, place, team, block_cols, row_x) for _, charge, place in sources]
    for (fragment, _, _), rows in zip(sources, over_lanes(fields, block_cols, pts_rows)):
        for r in range(pts_rows):
            totals[r] = totals[r] + jnp.where(here_ref[r : r + 1, :] != fragment, rows[r], 0.0)
    for r in range(pts_rows):
        out_ref[0, r : r + 1, :] = totals[r]


def after_kernel(sizes_ref, mine_ref, other_ref, here_ref, out_ref):
    half, nbasis = mine_ref.shape[0], mine_ref.shape[2]
    me, team, teams = lax.axis_index("sub"), lax.axis_index("frag"), lax.axis_size("frag")
    column = lax.broadcasted_iota(I32, (1, nbasis), 1)
    sources = []
    for ref, start in ((mine_ref, me * half), (other_ref, (1 - me) * half)):
        for f in range(half):
            charge = charge_row(lambda low, high, ref=ref, f=f: ref[f, low:high, low:high], nbasis)
            charge = jnp.where(column < sizes_ref[2 * half + start + f, 0:1, 0:1], charge, 0.0)
            place = place_rows(ref[f, nbasis:, :].astype(F32))
            sources.append((lax.rem(team + 1, teams) * 2 * half + start + f, charge, place))
    felt(sources, here_ref, out_ref)


def prior_kernel(here_ref, piece_ref, out_ref):
    frag_dev, team, teams = piece_ref.shape[0], lax.axis_index("frag"), lax.axis_size("frag")
    sources = []
    for f in range(frag_dev):
        extra = piece_ref[f, piece_ref.shape[1] - EXTRA :, :].astype(F32)
        sources.append((lax.rem(team + teams - 1, teams) * frag_dev + f, extra[9:10], place_rows(extra)))
    felt(sources, here_ref, out_ref)


def last_kernel(scale, sizes_ref, masked_ref, own_ref, before_ref, recv_ref, pot_ref, out_ref, potential_ref):
    frag_dev, share, nbasis = out_ref.shape
    member = lax.axis_index("grid") * lax.axis_size("sub") + lax.axis_index("sub")
    row_start = pl.multiple_of(member * share, share)
    rows = row_start + lax.broadcasted_iota(I32, (share, nbasis), 0)
    cols = lax.broadcasted_iota(I32, (share, nbasis), 1)
    for f in range(frag_dev):
        size = sizes_ref[f, 0:1, 0:1]
        correction = own_ref[f] + before_ref[f] + recv_ref[f].astype(F32)
        correction = jnp.where((rows < size) & (cols < size), correction, 0.0)
        out_ref[f] = (masked_ref[f, pl.ds(row_start, share), :].astype(F32) + correction).astype(BF16)
    potential_ref[...] = pot_ref[0] * scale


def turned(value, axis, steps):
    count = lax.axis_size(axis)
    return lax.ppermute(value, axis, [(s, (s + steps) % count) for s in range(count)])


def in_hbm(value):
    return pltpu.with_memory_space_constraint(value, pltpu.HBM)


def shape(dims, dtype):
    return jax.ShapeDtypeStruct(dims, dtype)


def per_device(
    density, basis_size, coupling, pair_first, pair_second, dimer_count, source_coords, grid_region
):
    frag_dev, nbasis, _ = density.shape
    slots = coupling.shape[0]
    teams, grid_size, sub_size = (lax.axis_size(a) for a in ("frag", "grid", "sub"))
    assert sub_size == 2 and frag_dev == 2 and grid_size % sub_size == 0
    rounds = grid_size // sub_size
    assert teams >= 4 and teams & (teams - 1) == 0
    share = nbasis // (grid_size * sub_size)
    half = frag_dev // sub_size
    pts_rows, total_cols = grid_region.shape
    block_cols = total_cols // teams

    smem = pl.BlockSpec(memory_space=pltpu.SMEM)
    vmem = pl.BlockSpec(memory_space=pltpu.VMEM)
    hbm = pl.BlockSpec(memory_space=pltpu.HBM)
    square = (nbasis, nbasis)

    def call(kernel, name, ins, outs, out_specs, scratch=(), flops=0):
        return pl.pallas_call(
            kernel,
            out_shape=outs,
            in_specs=ins,
            out_specs=out_specs,
            scratch_shapes=scratch,
            compiler_params=pltpu.CompilerParams(vmem_limit_bytes=VMEM_LIMIT),
            cost_estimate=pl.CostEstimate(flops=flops, bytes_accessed=1 << 20, transcendentals=0),
            name=name,
        )

    work = 4 * slots * nbasis**3
    by_chip = (grid_size, frag_dev, share, nbasis)
    halves = shape((frag_dev, nbasis // sub_size, nbasis), BF16)
    sent_halves = shape((frag_dev, nbasis // sub_size + EXTRA, nbasis), BF16)
    places = in_hbm(jnp.transpose(source_coords, (1, 0, 2)))
    payload = call(
        head_kernel,
        "head",
        [hbm] * 2,
        shape((half, nbasis + EXTRA, nbasis), BF16),
        vmem,
        [pltpu.VMEM((3, frag_dev, nbasis), F32), pltpu.SemaphoreType.DMA((2,))],
    )(in_hbm(density), places)
    mine = turned(payload, "frag", -1)

    next_keep, next_send, own_part, factors, masked, ids, sizes, here, sources, *slabs = call(
        right_kernel,
        "right",
        [hbm] * 3 + [smem] + [hbm] * 4,
        (
            halves, sent_halves, shape((frag_dev,) + square, F32),
            shape((slots,) + square, BF16), shape((frag_dev,) + square, BF16),
            shape((4 * slots,), I32), shape((2 * frag_dev, 8, 128), I32), shape((pts_rows, block_cols), I32),
            shape((frag_dev, EXTRA, nbasis), BF16),
        ) + (shape((teams // 4, pts_rows, block_cols), F32),) * 4,
        (vmem,) * 5 + (smem,) + (vmem,) * 7,
        [
            pltpu.SMEM(basis_size.shape, I32), pltpu.SMEM((slots,), I32), pltpu.SMEM((slots,), I32),
            pltpu.VMEM(density.shape, BF16), pltpu.VMEM((3, frag_dev, nbasis), F32),
            pltpu.VMEM(grid_region.shape, I32), pltpu.VMEM((2 * frag_dev + 1,) + square, F32),
            pltpu.SemaphoreType.DMA((6 + slots,)),
        ],
        work,
    )(
        in_hbm(basis_size), in_hbm(pair_first), in_hbm(pair_second), dimer_count, in_hbm(density),
        in_hbm(coupling), places, in_hbm(grid_region),
    )

    if teams == 4:
        home, far = slabs[0], turned(slabs[2], "frag", 2)
    else:
        slabs = jnp.concatenate(slabs)
        while slabs.shape[0] > 1:
            rest = slabs.shape[0] // 2
            slabs = slabs[:rest] + turned(slabs[rest:], "frag", rest)
        home, far = slabs, jnp.zeros_like(slabs)

    *pieces, after = call(
        next_kernel,
        "next_sum",
        [vmem] * 3,
        [shape((frag_dev, nbasis // grid_size + EXTRA, nbasis), BF16)] * rounds + [shape((8, 128), F32)],
        (vmem,) * (rounds + 1),
    )(next_keep, turned(next_send, "sub", 1), sources)
    for j, value in enumerate(pieces):
        pairs = []
        for t in range(teams):
            for g in range(grid_size):
                for c in range(sub_size):
                    to = (c * rounds + (g + j) % rounds, g // rounds) if t + 1 < teams else (g, c)
                    to = ((t + 1) % teams * grid_size + to[0]) * sub_size + to[1]
                    pairs.append(((t * grid_size + g) * sub_size + c, to))
        pieces[j] = lax.ppermute(value, ("frag", "grid", "sub"), pairs)

    mine = call(relay_kernel, "relay", [vmem] * 2, shape(payload.shape, BF16), vmem)(here, mine)
    other = turned(mine, "sub", 1)
    own_keep, *own_sends = call(
        left_kernel,
        "left",
        [smem] + [vmem] * 7,
        [shape(by_chip, F32)] + [shape((grid_size, share, nbasis), BF16)] * frag_dev,
        (vmem,) * (1 + frag_dev),
        [pltpu.VMEM((2 * frag_dev,) + square, BF16), pltpu.VMEM((frag_dev + 1,) + square, F32)],
        work,
    )(ids, sizes, masked, mine, other, own_part, factors, after)
    mine_rows = (frag_dev, share, nbasis)
    own, *parts = call(
        own_sum_kernel,
        "own_sum",
        [vmem] * (1 + frag_dev),
        [shape(mine_rows, F32)] + [shape(mine_rows, BF16)] * (grid_size - 1),
        (vmem,) * grid_size,
    )(own_keep, *[turned(value, "sub", 1) for value in own_sends])
    parts = [turned(part, "grid", step) for step, part in enumerate(parts, 1)]

    slab = shape((1, pts_rows, block_cols), F32)
    later = call(after_kernel, "after", [vmem] * 4, slab, vmem)(sizes, mine, other, here)
    before, passed = call(
        before_kernel,
        "before",
        [vmem] * rounds,
        (shape(mine_rows, F32), shape(mine_rows, BF16)),
        (vmem,) * 2,
    )(*pieces)
    passed = turned(passed, "sub", 1)
    prior = call(prior_kernel, "prior", [vmem] * 2, slab, vmem)(here, pieces[0])
    own, pot = call(
        middle_kernel,
        "middle",
        [vmem] * (5 + len(parts)),
        (shape(mine_rows, F32), slab),
        (vmem,) * 2,
        (),
        10**10,
    )(own, home, far, later, prior, *parts)

    scale = 8.0 / math.sqrt(frag_dev * teams * nbasis)
    return call(
        functools.partial(last_kernel, scale),
        "last",
        [vmem] * 6,
        (shape(mine_rows, BF16), shape((pts_rows, block_cols), F32)),
        (vmem,) * 2,
    )(sizes, masked, own, before, passed, pot)


def solution(mesh):
    placed = (
        P(("groups", "frag"), None, None),
        P(),
        P(("groups", "frag", "grid", "sub"), None, None),
        P(("frag", "grid", "sub")),
        P(("frag", "grid", "sub")),
        P(("frag", "grid", "sub")),
        P(("groups", "frag"), None, None),
        P(("grid", "sub"), None),
    )
    return jax.shard_map(
        per_device,
        mesh=mesh,
        in_specs=placed,
        out_specs=(
            P(("groups", "frag"), ("grid", "sub"), None),
            P(("groups", "grid", "sub"), "frag"),
        ),
        check_vma=False,
    )
```

```python
import functools
import math

import jax
import jax.numpy as jnp
from jax import lax
from jax.experimental import pallas as pl
from jax.experimental.pallas import tpu as pltpu
from jax.sharding import PartitionSpec as P

VMEM_LIMIT = 24 * 1024 * 1024
EXTRA = 16
BF16, F32, I32 = jnp.bfloat16, jnp.float32, jnp.int32


def live_square(values, size):
    rows = lax.broadcasted_iota(I32, values.shape, 0)
    cols = lax.broadcasted_iota(I32, values.shape, 1)
    return jnp.where((rows < size) & (cols < size), values.astype(F32), 0.0).astype(BF16)


def charge_row(read, nbasis):
    tile = 128
    parts = []
    for at in range(0, nbasis, tile):
        block = read(at, at + tile).astype(F32)
        rows = lax.broadcasted_iota(I32, block.shape, 0)
        cols = lax.broadcasted_iota(I32, block.shape, 1)
        parts.append(jnp.sum(jnp.where(rows == cols, block, 0.0), axis=0, keepdims=True))
    return jnp.concatenate(parts, axis=1)


def at_rows(block, size):
    return pl.ds(pl.multiple_of(block * size, size), size)


def thirds(values):
    high = values.astype(BF16).astype(F32)
    middle = (values - high).astype(BF16).astype(F32)
    return [high, middle, values - high - middle]


def field(charge, place, block, block_cols, row_x):
    src_x, src_y, src_z = place
    point_z = 0.25 * lax.broadcasted_iota(I32, (64, charge.shape[1]), 0).astype(F32)
    along_z = (point_z - src_z) ** 2 + 1.0
    parts = []
    for x in row_x:
        for step in range(block_cols // 64):
            point_y = 0.25 * (block * (block_cols // 64) + step).astype(F32)
            in_plane = (x - src_x) ** 2 + (point_y - src_y) ** 2
            value = charge * lax.rsqrt(along_z + in_plane)
            parts.append(sum(value[:, at : at + 128] for at in range(0, value.shape[1], 128)))
    return jnp.concatenate(parts)


def over_lanes(points, block_cols, pts_rows):
    rows = jnp.concatenate(points)
    ones = jnp.ones((16, 128), BF16)
    total = sum(dot_t(ones, part.astype(BF16)) for part in thirds(rows))
    size = pts_rows * block_cols
    return [
        [total[0:1, k * size + r * block_cols : k * size + (r + 1) * block_cols] for r in range(pts_rows)]
        for k in range(len(points))
    ]


def row_places(pts_rows):
    member = lax.axis_index("grid") * lax.axis_size("sub") + lax.axis_index("sub")
    return [0.25 * (member * pts_rows + r).astype(F32) for r in range(pts_rows)]


def place_rows(extra):
    return [sum(extra[3 * d + k : 3 * d + k + 1] for k in range(3)) for d in range(3)]


def by_core(total_ref, row, keep_ref, send_ref):
    me, rows = lax.axis_index("sub"), keep_ref.shape[-2]
    for f in range(keep_ref.shape[0]):
        keep_ref[f] = total_ref[f, pl.ds(row + pl.multiple_of(me * rows, rows), rows), :].astype(keep_ref.dtype)
        other = total_ref[f, pl.ds(row + pl.multiple_of((1 - me) * rows, rows), rows), :]
        send_ref[f, :rows] = other.astype(send_ref.dtype)


def pipelined(slots, first_dot, second_dot, add):
    held = None
    for slot in range(slots + 1):
        now = first_dot(slot).astype(BF16) if slot < slots else None
        if held is not None:
            add(slot - 1, second_dot(slot - 1, held))
        held = now


def dot(a, b):
    return jnp.dot(a, b, preferred_element_type=F32)


def dot_t(a, b):
    return lax.dot_general(a, b, (((1,), (1,)), ((), ())), preferred_element_type=F32)


def fetch(pairs, sems):
    copies = [pltpu.make_async_copy(source, target, sems.at[i]) for i, (source, target) in enumerate(pairs)]
    for copy in copies:
        copy.start()
    return copies


def head_kernel(density_hbm, coords_hbm, payload_ref, coords_ref, sems):
    half, nbasis = payload_ref.shape[0], payload_ref.shape[2]
    at = lax.axis_index("sub") * half
    copies = fetch(
        [(coords_hbm, coords_ref)]
        + [
            (density_hbm.at[pl.ds(at, half), pl.ds(low, 128)], payload_ref.at[:, pl.ds(low, 128)])
            for low in range(0, nbasis, 128)
        ],
        sems,
    )
    copies[0].wait()
    for f in range(half):
        rows = [part for d in range(3) for part in thirds(coords_ref[d, pl.ds(at + f, 1), :])]
        rows.append(jnp.zeros((EXTRA - len(rows), nbasis), F32))
        payload_ref[f, nbasis:, :] = jnp.concatenate(rows).astype(BF16)
    for copy in copies[1:]:
        copy.wait()


def right_kernel(
    size_hbm, first_hbm, second_hbm, count_ref, payload_ref, density_hbm, coupling_hbm, coords_hbm, region_hbm,
    keep_ref, send_ref, own_ref, factor_ref, masked_ref, slots_ref, sizes_ref, here_ref, sources_ref, *rest,
):
    slab_refs, rest = rest[:4], rest[4:]
    size_ref, first_ref, second_ref, ids_ref, density_ref, coords_ref, region_ref, total_ref, sems = rest
    frag_dev, nbasis, slots = masked_ref.shape[0], masked_ref.shape[1], factor_ref.shape[0]
    half = payload_ref.shape[0]
    mine, theirs = lax.axis_index("sub") * half, (1 - lax.axis_index("sub")) * half
    copies = fetch(
        [
            (size_hbm, size_ref), (first_hbm, first_ref), (second_hbm, second_ref),
            (density_hbm.at[pl.ds(theirs, half)], density_ref), (coords_hbm, coords_ref), (region_hbm, region_ref),
        ]
        + [(coupling_hbm.at[s], factor_ref.at[s]) for s in range(slots)],
        sems,
    )
    total_ref[...] = jnp.zeros_like(total_ref)
    for copy in copies[:6]:
        copy.wait()
    team = lax.axis_index("frag")
    base = team * frag_dev
    trash = 2 * frag_dev
    for s in range(slots):
        live = s < count_ref[0]
        first = jnp.clip(first_ref[s] - base, 0, frag_dev - 1)
        second = jnp.clip(second_ref[s] - base, 0, trash - 1)
        ids_ref[s] = first
        ids_ref[slots + s] = second
        ids_ref[2 * slots + s] = jnp.where(live, second, trash)
        ids_ref[3 * slots + s] = jnp.where(live, first, frag_dev)
    for f in range(2 * frag_dev):
        sizes_ref[f] = jnp.full((8, 128), size_ref[lax.rem(base + f, size_ref.shape[0])], I32)
    for f in range(half):
        masked_ref[mine + f] = live_square(payload_ref[f, :nbasis], size_ref[base + mine + f])
        masked_ref[theirs + f] = live_square(density_ref[f], size_ref[base + theirs + f])
    sources = [
        (
            charge_row(lambda low, high, f=f: masked_ref[f, low:high, low:high], nbasis),
            [coords_ref[d, f : f + 1, :] for d in range(3)],
        )
        for f in range(frag_dev)
    ]
    rows = []
    for charge, place in sources:
        rows += [part for values in place for part in thirds(values)[:2]] + [charge]
    rows.append(jnp.zeros((EXTRA - len(rows), nbasis), F32))
    sources_ref[...] = jnp.concatenate(rows).astype(BF16)

    pts_rows = region_ref.shape[0]
    each, block_cols = slab_refs[0].shape[0], slab_refs[0].shape[2]
    teams = len(slab_refs) * each
    row_x = row_places(pts_rows)

    def one_block(step, slab_ref, at):
        block = lax.rem(team + step, teams)
        region = region_ref[:, pl.ds(pl.multiple_of(block * block_cols, block_cols), block_cols)]
        fields = [field(charge, place, block, block_cols, row_x) for charge, place in sources]
        fields = over_lanes(fields, block_cols, pts_rows)
        for r in range(pts_rows):
            here = [jnp.where(region[r : r + 1] != base + f, fields[f][r], 0.0) for f in range(frag_dev)]
            slab_ref[at, r : r + 1, :] = sum(here)

    if each == 1:
        one_block(0, slab_refs[0], 0)
        one_block(2, slab_refs[2], 0)
    else:

        @pl.loop(0, each)
        def _(step):
            for k, slab_ref in enumerate(slab_refs):
                one_block(k * each + step, slab_ref, step)

    for k in (1, teams - 1):
        slab_refs[k // each][k % each] = jnp.zeros((pts_rows, block_cols), F32)
    here_ref[...] = region_ref[:, pl.ds(pl.multiple_of(team * block_cols, block_cols), block_cols)]

    for copy in copies[6:]:
        copy.wait()

    def add(s, corr):
        target = ids_ref[2 * slots + s]
        total_ref[target] = total_ref[target] + corr

    pipelined(
        slots,
        lambda s: dot(factor_ref[s].T, masked_ref[ids_ref[s]]),
        lambda s, right: dot(right, factor_ref[s]),
        add,
    )
    for s in range(slots):
        for k, row in ((1, s), (3, slots + s)):
            slots_ref[row : row + 1] = jnp.full((1, 128), ids_ref[k * slots + s], I32)
    own_ref[...] = total_ref[:frag_dev]
    by_core(total_ref.at[pl.ds(frag_dev, frag_dev)], 0, keep_ref, send_ref)
    send_ref[:, keep_ref.shape[1] :, :] = jnp.zeros((frag_dev, EXTRA, nbasis), BF16)


def left_kernel(
    slots_ref, sizes_ref, masked_ref, mine_ref, other_ref, own_ref, factor_ref, after_ref,
    keep_ref, *rest,
):
    send_refs, (ids_ref, all_ref, total_ref, sems) = rest[:-4], rest[-4:]
    copies = fetch([(slots_ref, ids_ref)], sems)
    frag_dev, nbasis = masked_ref.shape[0], masked_ref.shape[1]
    slots, half = factor_ref.shape[0], mine_ref.shape[0]
    me = lax.axis_index("sub")
    for f in range(frag_dev):
        all_ref[f] = masked_ref[f]
    for f in range(half):
        at = frag_dev + me * half + f
        all_ref[at] = live_square(mine_ref[f, :nbasis], sizes_ref[at, 0:1, 0:1])
        at = frag_dev + (1 - me) * half + f
        all_ref[at] = live_square(other_ref[f, :nbasis], sizes_ref[at, 0:1, 0:1])
    total_ref[:frag_dev] = own_ref[...]
    total_ref[frag_dev] = jnp.zeros_like(total_ref[frag_dev])
    copies[0].wait()

    def add(s, corr):
        target = ids_ref[slots + s, 0]
        total_ref[target] = total_ref[target] + corr

    pipelined(
        slots,
        lambda s: dot(factor_ref[s], all_ref[ids_ref[s, 0]]),
        lambda s, left: dot_t(left, factor_ref[s]),
        add,
    )
    grid_size, _, share, _ = keep_ref.shape
    for g in range(grid_size):
        for f in range(frag_dev):
            chip = total_ref.at[f, 2 * g * share : 2 * (g + 1) * share]
            keep_ref[g, f] = chip[at_rows(me, share), :]
            send_refs[f][g] = chip[at_rows(1 - me, share), :].astype(BF16)


def own_sum_kernel(keep_ref, *rest):
    grid_size, frag_dev, share, nbasis = keep_ref.shape
    recv_refs, own_ref, part_refs = rest[:frag_dev], rest[frag_dev], rest[frag_dev + 1 :]
    me = lax.axis_index("grid")
    for f in range(frag_dev):
        own_ref[f] = keep_ref[me, f] + recv_refs[f][me].astype(F32)
        for step, part_ref in enumerate(part_refs, 1):
            at = lax.rem(me + step, grid_size)
            part_ref[f] = (keep_ref[at, f] + recv_refs[f][at].astype(F32)).astype(BF16)


def relay_kernel(here_ref, in_ref, out_ref):
    out_ref[...] = in_ref[...]


def next_kernel(keep_ref, recv_ref, sources_ref, *out_refs):
    out_refs, after_ref = out_refs[:-1], out_refs[-1]
    after_ref[...] = jnp.zeros_like(after_ref)
    rounds, frag_dev = len(out_refs), keep_ref.shape[0]
    rows = keep_ref.shape[1] // rounds
    for j, out_ref in enumerate(out_refs):
        at = at_rows(lax.rem(lax.axis_index("grid") + j, rounds), rows) if rounds > 1 else slice(0, rows)
        for f in range(frag_dev):
            total = keep_ref[f, at, :].astype(F32) + recv_ref[f, at, :].astype(F32)
            out_ref[f * rows : (f + 1) * rows, :] = total.astype(BF16)
        out_ref[frag_dev * rows :, :] = sources_ref[...]


def before_kernel(*refs):
    in_refs, (keep_ref, send_ref) = refs[:-2], refs[-2:]
    me, (frag_dev, share, _) = lax.axis_index("sub"), keep_ref.shape
    for f in range(frag_dev):
        for at, ref in ((me, keep_ref), (1 - me, send_ref)):
            place = pl.ds(2 * f * share + pl.multiple_of(at * share, share), share)
            ref[f] = sum(in_ref[place, :].astype(F32) for in_ref in in_refs).astype(ref.dtype)


def middle_kernel(own_ref, home_ref, far_ref, around_ref, *rest):
    part_refs, (out_ref, pot_ref) = rest[:-2], rest[-2:]
    out_ref[...] = own_ref[...] + sum(part_ref[...].astype(F32) for part_ref in part_refs)
    pot_ref[...] = home_ref[...] + far_ref[...] + around_ref[...]


def around_kernel(frag_dev, sizes_ref, mine_ref, other_ref, here_ref, piece_ref, out_ref):
    half, nbasis = mine_ref.shape[0], mine_ref.shape[2]
    me, team, teams = lax.axis_index("sub"), lax.axis_index("frag"), lax.axis_size("frag")
    column = lax.broadcasted_iota(I32, (1, nbasis), 1)
    sources = []
    for ref, start in ((mine_ref, me * half), (other_ref, (1 - me) * half)):
        for f in range(half):
            charge = charge_row(lambda low, high, ref=ref, f=f: ref[f, low:high, low:high], nbasis)
            charge = jnp.where(column < sizes_ref[frag_dev + start + f, 0:1, 0:1], charge, 0.0)
            place = place_rows(ref[f, nbasis:, :].astype(F32))
            sources.append((lax.rem(team + 1, teams) * frag_dev + start + f, charge, place))
    extra = piece_ref[piece_ref.shape[0] - EXTRA :, :].astype(F32)
    for f in range(frag_dev):
        rows = [extra[7 * f + k : 7 * f + k + 1] for k in range(7)]
        place = [rows[2 * d] + rows[2 * d + 1] for d in range(3)]
        sources.append((lax.rem(team + teams - 1, teams) * frag_dev + f, rows[6], place))
    pts_rows, block_cols = here_ref.shape
    row_x = row_places(pts_rows)
    totals = [jnp.zeros((1, block_cols), F32) for _ in range(pts_rows)]
    fields = [field(charge, place, team, block_cols, row_x) for _, charge, place in sources]
    for (fragment, _, _), rows in zip(sources, over_lanes(fields, block_cols, pts_rows)):
        for r in range(pts_rows):
            totals[r] = totals[r] + jnp.where(here_ref[r : r + 1, :] != fragment, rows[r], 0.0)
    for r in range(pts_rows):
        out_ref[0, r : r + 1, :] = totals[r]


def last_kernel(scale, sizes_ref, masked_ref, own_ref, before_ref, recv_ref, pot_ref, out_ref, potential_ref):
    frag_dev, share, nbasis = out_ref.shape
    member = lax.axis_index("grid") * lax.axis_size("sub") + lax.axis_index("sub")
    row_start = pl.multiple_of(member * share, share)
    rows = row_start + lax.broadcasted_iota(I32, (share, nbasis), 0)
    cols = lax.broadcasted_iota(I32, (share, nbasis), 1)
    for f in range(frag_dev):
        size = sizes_ref[f, 0:1, 0:1]
        correction = own_ref[f] + before_ref[f] + recv_ref[f].astype(F32)
        correction = jnp.where((rows < size) & (cols < size), correction, 0.0)
        out_ref[f] = (masked_ref[f, pl.ds(row_start, share), :].astype(F32) + correction).astype(BF16)
    potential_ref[...] = pot_ref[0] * scale


def turned(value, axis, steps):
    count = lax.axis_size(axis)
    return lax.ppermute(value, axis, [(s, (s + steps) % count) for s in range(count)])


def in_hbm(value):
    return pltpu.with_memory_space_constraint(value, pltpu.HBM)


def shape(dims, dtype):
    return jax.ShapeDtypeStruct(dims, dtype)


def per_device(
    density, basis_size, coupling, pair_first, pair_second, dimer_count, source_coords, grid_region
):
    frag_dev, nbasis, _ = density.shape
    slots = coupling.shape[0]
    teams, grid_size, sub_size = (lax.axis_size(a) for a in ("frag", "grid", "sub"))
    assert sub_size == 2 and frag_dev == 2 and grid_size % sub_size == 0
    rounds = grid_size // sub_size
    assert teams >= 4 and teams & (teams - 1) == 0
    share = nbasis // (grid_size * sub_size)
    half = frag_dev // sub_size
    pts_rows, total_cols = grid_region.shape
    block_cols = total_cols // teams

    smem = pl.BlockSpec(memory_space=pltpu.SMEM)
    vmem = pl.BlockSpec(memory_space=pltpu.VMEM)
    hbm = pl.BlockSpec(memory_space=pltpu.HBM)
    square = (nbasis, nbasis)

    def call(kernel, name, ins, outs, out_specs, scratch=(), flops=0):
        return pl.pallas_call(
            kernel,
            out_shape=outs,
            in_specs=ins,
            out_specs=out_specs,
            scratch_shapes=scratch,
            compiler_params=pltpu.CompilerParams(vmem_limit_bytes=VMEM_LIMIT),
            cost_estimate=pl.CostEstimate(flops=flops, bytes_accessed=1 << 20, transcendentals=0),
            name=name,
        )

    work = 4 * slots * nbasis**3
    by_chip = (grid_size, frag_dev, share, nbasis)
    halves = shape((frag_dev, nbasis // sub_size, nbasis), BF16)
    sent_halves = shape((frag_dev, nbasis // sub_size + EXTRA, nbasis), BF16)
    places = in_hbm(jnp.transpose(source_coords, (1, 0, 2)))
    payload = call(
        head_kernel,
        "head",
        [hbm] * 2,
        shape((half, nbasis + EXTRA, nbasis), BF16),
        vmem,
        [pltpu.VMEM((3, frag_dev, nbasis), F32), pltpu.SemaphoreType.DMA((1 + nbasis // 128,))],
    )(in_hbm(density), places)
    mine = turned(payload, "frag", -1)

    next_keep, next_send, own_part, factors, masked, slot_ids, sizes, here, sources, *slabs = call(
        right_kernel,
        "right",
        [hbm] * 3 + [smem, vmem] + [hbm] * 4,
        (
            halves, sent_halves, shape((frag_dev,) + square, F32),
            shape((slots,) + square, BF16), shape((frag_dev,) + square, BF16),
            shape((2 * slots, 128), I32), shape((2 * frag_dev, 8, 128), I32), shape((pts_rows, block_cols), I32),
            shape((EXTRA, nbasis), BF16),
        ) + (shape((teams // 4, pts_rows, block_cols), F32),) * 4,
        (vmem,) * 13,
        [
            pltpu.SMEM(basis_size.shape, I32), pltpu.SMEM((slots,), I32), pltpu.SMEM((slots,), I32),
            pltpu.SMEM((4 * slots,), I32), pltpu.VMEM((half,) + square, BF16), pltpu.VMEM((3, frag_dev, nbasis), F32),
            pltpu.VMEM(grid_region.shape, I32), pltpu.VMEM((2 * frag_dev + 1,) + square, F32),
            pltpu.SemaphoreType.DMA((6 + slots,)),
        ],
        work,
    )(
        in_hbm(basis_size), in_hbm(pair_first), in_hbm(pair_second), dimer_count, payload, in_hbm(density),
        in_hbm(coupling), places, in_hbm(grid_region),
    )

    if teams == 4:
        home, far = slabs[0], turned(slabs[2], "frag", 2)
    else:
        slabs = jnp.concatenate(slabs)
        while slabs.shape[0] > 1:
            rest = slabs.shape[0] // 2
            slabs = slabs[:rest] + turned(slabs[rest:], "frag", rest)
        home, far = slabs, jnp.zeros_like(slabs)

    *pieces, after = call(
        next_kernel,
        "next_sum",
        [vmem] * 3,
        [shape((frag_dev * nbasis // grid_size + EXTRA, nbasis), BF16)] * rounds + [shape((8, 128), F32)],
        (vmem,) * (rounds + 1),
    )(next_keep, turned(next_send, "sub", 1), sources)
    for j, value in enumerate(pieces):
        pairs = []
        for t in range(teams):
            for g in range(grid_size):
                for c in range(sub_size):
                    to = (c * rounds + (g + j) % rounds, g // rounds) if t + 1 < teams else (g, c)
                    to = ((t + 1) % teams * grid_size + to[0]) * sub_size + to[1]
                    pairs.append(((t * grid_size + g) * sub_size + c, to))
        pieces[j] = lax.ppermute(value, ("frag", "grid", "sub"), pairs)

    mine = call(relay_kernel, "relay", [vmem] * 2, shape(payload.shape, BF16), vmem)(here, mine)
    other = turned(mine, "sub", 1)
    own_keep, *own_sends = call(
        left_kernel,
        "left",
        [vmem] * 8,
        [shape(by_chip, F32)] + [shape((grid_size, share, nbasis), BF16)] * frag_dev,
        (vmem,) * (1 + frag_dev),
        [
            pltpu.SMEM((2 * slots, 128), I32), pltpu.VMEM((2 * frag_dev,) + square, BF16),
            pltpu.VMEM((frag_dev + 1,) + square, F32), pltpu.SemaphoreType.DMA((1,)),
        ],
        work,
    )(slot_ids, sizes, masked, mine, other, own_part, factors, after)
    mine_rows = (frag_dev, share, nbasis)
    own, *parts = call(
        own_sum_kernel,
        "own_sum",
        [vmem] * (1 + frag_dev),
        [shape(mine_rows, F32)] + [shape(mine_rows, BF16)] * (grid_size - 1),
        (vmem,) * grid_size,
    )(own_keep, *[turned(value, "sub", 1) for value in own_sends])
    parts = [turned(part, "grid", step) for step, part in enumerate(parts, 1)]

    slab = shape((1, pts_rows, block_cols), F32)
    before, passed = call(
        before_kernel,
        "before",
        [vmem] * rounds,
        (shape(mine_rows, F32), shape(mine_rows, BF16)),
        (vmem,) * 2,
    )(*pieces)
    passed = turned(passed, "sub", 1)
    around = call(functools.partial(around_kernel, frag_dev), "around", [vmem] * 5, slab, vmem)(
        sizes, mine, other, here, pieces[0]
    )
    own, pot = call(
        middle_kernel,
        "middle",
        [vmem] * (4 + len(parts)),
        (shape(mine_rows, F32), slab),
        (vmem,) * 2,
        (),
        10**10,
    )(own, home, far, around, *parts)

    scale = 8.0 / math.sqrt(frag_dev * teams * nbasis)
    return call(
        functools.partial(last_kernel, scale),
        "last",
        [vmem] * 6,
        (shape(mine_rows, BF16), shape((pts_rows, block_cols), F32)),
        (vmem,) * 2,
    )(sizes, masked, own, before, passed, pot)


def solution(mesh):
    placed = (
        P(("groups", "frag"), None, None),
        P(),
        P(("groups", "frag", "grid", "sub"), None, None),
        P(("frag", "grid", "sub")),
        P(("frag", "grid", "sub")),
        P(("frag", "grid", "sub")),
        P(("groups", "frag"), None, None),
        P(("grid", "sub"), None),
    )
    return jax.shard_map(
        per_device,
        mesh=mesh,
        in_specs=placed,
        out_specs=(
            P(("groups", "frag"), ("grid", "sub"), None),
            P(("groups", "grid", "sub"), "frag"),
        ),
        check_vma=False,
    )
```

```python
import functools
import math

import jax
import jax.numpy as jnp
from jax import lax
from jax.experimental import pallas as pl
from jax.experimental.pallas import tpu as pltpu
from jax.sharding import PartitionSpec as P

VMEM_LIMIT = 24 * 1024 * 1024
EXTRA = 16
BF16, F32, I32 = jnp.bfloat16, jnp.float32, jnp.int32


def live_square(values, size):
    rows = lax.broadcasted_iota(I32, values.shape, 0)
    cols = lax.broadcasted_iota(I32, values.shape, 1)
    return jnp.where((rows < size) & (cols < size), values.astype(F32), 0.0).astype(BF16)


def charge_row(read, nbasis):
    tile = 128
    parts = []
    for at in range(0, nbasis, tile):
        block = read(at, at + tile).astype(F32)
        rows = lax.broadcasted_iota(I32, block.shape, 0)
        cols = lax.broadcasted_iota(I32, block.shape, 1)
        parts.append(jnp.sum(jnp.where(rows == cols, block, 0.0), axis=0, keepdims=True))
    return jnp.concatenate(parts, axis=1)


def at_rows(block, size):
    return pl.ds(pl.multiple_of(block * size, size), size)


def thirds(values):
    high = values.astype(BF16).astype(F32)
    middle = (values - high).astype(BF16).astype(F32)
    return [high, middle, values - high - middle]


def field(charge, place, block, block_cols, row_x):
    src_x, src_y, src_z = place
    point_z = 0.25 * lax.broadcasted_iota(I32, (64, charge.shape[1]), 0).astype(F32)
    along_z = (point_z - src_z) ** 2 + 1.0
    parts = []
    for x in row_x:
        for step in range(block_cols // 64):
            point_y = 0.25 * (block * (block_cols // 64) + step).astype(F32)
            in_plane = (x - src_x) ** 2 + (point_y - src_y) ** 2
            value = charge * lax.rsqrt(along_z + in_plane)
            parts.append(sum(value[:, at : at + 128] for at in range(0, value.shape[1], 128)))
    return jnp.concatenate(parts)


def over_lanes(points, block_cols, pts_rows):
    rows = jnp.concatenate(points)
    ones = jnp.ones((16, 128), BF16)
    total = sum(dot_t(ones, part.astype(BF16)) for part in thirds(rows))
    size = pts_rows * block_cols
    return [
        [total[0:1, k * size + r * block_cols : k * size + (r + 1) * block_cols] for r in range(pts_rows)]
        for k in range(len(points))
    ]


def row_places(pts_rows):
    member = lax.axis_index("grid") * lax.axis_size("sub") + lax.axis_index("sub")
    return [0.25 * (member * pts_rows + r).astype(F32) for r in range(pts_rows)]


def place_rows(extra):
    return [sum(extra[3 * d + k : 3 * d + k + 1] for k in range(3)) for d in range(3)]


def by_core(total_ref, row, keep_ref, send_ref):
    me, rows = lax.axis_index("sub"), keep_ref.shape[-2]
    for f in range(keep_ref.shape[0]):
        keep_ref[f] = total_ref[f, pl.ds(row + pl.multiple_of(me * rows, rows), rows), :].astype(keep_ref.dtype)
        other = total_ref[f, pl.ds(row + pl.multiple_of((1 - me) * rows, rows), rows), :]
        send_ref[f, :rows] = other.astype(send_ref.dtype)


def pipelined(slots, first_dot, second_dot, add):
    held = None
    for slot in range(slots + 1):
        now = first_dot(slot).astype(BF16) if slot < slots else None
        if held is not None:
            add(slot - 1, second_dot(slot - 1, held))
        held = now


def dot(a, b):
    return jnp.dot(a, b, preferred_element_type=F32)


def dot_t(a, b):
    return lax.dot_general(a, b, (((1,), (1,)), ((), ())), preferred_element_type=F32)


def fetch(pairs, sems):
    copies = [pltpu.make_async_copy(source, target, sems.at[i]) for i, (source, target) in enumerate(pairs)]
    for copy in copies:
        copy.start()
    return copies


def head_kernel(density_hbm, coords_hbm, payload_ref, coords_ref, sems):
    half, nbasis = payload_ref.shape[0], payload_ref.shape[2]
    at = lax.axis_index("sub") * half
    copies = fetch(
        [(coords_hbm, coords_ref)]
        + [
            (density_hbm.at[pl.ds(at, half), pl.ds(low, 128)], payload_ref.at[:, pl.ds(low, 128)])
            for low in range(0, nbasis, 128)
        ],
        sems,
    )
    copies[0].wait()
    for f in range(half):
        rows = [part for d in range(3) for part in thirds(coords_ref[d, pl.ds(at + f, 1), :])]
        rows.append(jnp.zeros((EXTRA - len(rows), nbasis), F32))
        payload_ref[f, nbasis:, :] = jnp.concatenate(rows).astype(BF16)
    for copy in copies[1:]:
        copy.wait()


def right_kernel(
    size_hbm, first_hbm, second_hbm, count_ref, payload_ref, density_hbm, coupling_hbm, coords_hbm, region_hbm,
    keep_ref, send_ref, own_ref, factor_ref, masked_ref, slots_ref, sizes_ref, here_ref, sources_ref, *rest,
):
    slab_refs, rest = rest[:4], rest[4:]
    size_ref, first_ref, second_ref, ids_ref, density_ref, coords_ref, region_ref, total_ref, sems = rest
    frag_dev, nbasis, slots = masked_ref.shape[0], masked_ref.shape[1], factor_ref.shape[0]
    half = payload_ref.shape[0]
    mine, theirs = lax.axis_index("sub") * half, (1 - lax.axis_index("sub")) * half
    copies = fetch(
        [
            (size_hbm, size_ref), (first_hbm, first_ref), (second_hbm, second_ref),
            (density_hbm.at[pl.ds(theirs, half)], density_ref), (coords_hbm, coords_ref), (region_hbm, region_ref),
        ]
        + [(coupling_hbm.at[s], factor_ref.at[s]) for s in range(slots)],
        sems,
    )
    total_ref[...] = jnp.zeros_like(total_ref)
    for copy in copies[:6]:
        copy.wait()
    team = lax.axis_index("frag")
    base = team * frag_dev
    trash = 2 * frag_dev
    for s in range(slots):
        live = s < count_ref[0]
        first = jnp.clip(first_ref[s] - base, 0, frag_dev - 1)
        second = jnp.clip(second_ref[s] - base, 0, trash - 1)
        ids_ref[s] = first
        ids_ref[slots + s] = second
        ids_ref[2 * slots + s] = jnp.where(live, second, trash)
        ids_ref[3 * slots + s] = jnp.where(live, first, frag_dev)
    for f in range(2 * frag_dev):
        sizes_ref[f] = jnp.full((8, 128), size_ref[lax.rem(base + f, size_ref.shape[0])], I32)
    for f in range(half):
        masked_ref[mine + f] = live_square(payload_ref[f, :nbasis], size_ref[base + mine + f])
        masked_ref[theirs + f] = live_square(density_ref[f], size_ref[base + theirs + f])
    sources = [
        (
            charge_row(lambda low, high, f=f: masked_ref[f, low:high, low:high], nbasis),
            [coords_ref[d, f : f + 1, :] for d in range(3)],
        )
        for f in range(frag_dev)
    ]
    rows = []
    for charge, place in sources:
        rows += [part for values in place for part in thirds(values)[:2]] + [charge]
    rows.append(jnp.zeros((EXTRA - len(rows), nbasis), F32))
    sources_ref[...] = jnp.concatenate(rows).astype(BF16)

    pts_rows = region_ref.shape[0]
    each, block_cols = slab_refs[0].shape[0], slab_refs[0].shape[2]
    teams = len(slab_refs) * each
    row_x = row_places(pts_rows)

    def one_block(step, slab_ref, at):
        block = lax.rem(team + step, teams)
        region = region_ref[:, pl.ds(pl.multiple_of(block * block_cols, block_cols), block_cols)]
        fields = [field(charge, place, block, block_cols, row_x) for charge, place in sources]
        fields = over_lanes(fields, block_cols, pts_rows)
        for r in range(pts_rows):
            here = [jnp.where(region[r : r + 1] != base + f, fields[f][r], 0.0) for f in range(frag_dev)]
            slab_ref[at, r : r + 1, :] = sum(here)

    if each == 1:
        one_block(2, slab_refs[2], 0)
    else:

        @pl.loop(0, each)
        def _(step):
            for k, slab_ref in enumerate(slab_refs):
                one_block(k * each + step, slab_ref, step)

    for k in (0, 1, teams - 1):
        slab_refs[k // each][k % each] = jnp.zeros((pts_rows, block_cols), F32)
    here_ref[...] = region_ref[:, pl.ds(pl.multiple_of(team * block_cols, block_cols), block_cols)]

    for copy in copies[6:]:
        copy.wait()

    def add(s, corr):
        target = ids_ref[2 * slots + s]
        total_ref[target] = total_ref[target] + corr

    pipelined(
        slots,
        lambda s: dot(factor_ref[s].T, masked_ref[ids_ref[s]]),
        lambda s, right: dot(right, factor_ref[s]),
        add,
    )
    for s in range(slots):
        for k, row in ((1, s), (3, slots + s)):
            slots_ref[row : row + 1] = jnp.full((1, 128), ids_ref[k * slots + s], I32)
    own_ref[...] = total_ref[:frag_dev]
    by_core(total_ref.at[pl.ds(frag_dev, frag_dev)], 0, keep_ref, send_ref)
    send_ref[:, keep_ref.shape[1] :, :] = jnp.zeros((frag_dev, EXTRA, nbasis), BF16)


def left_kernel(
    slots_ref, sizes_ref, masked_ref, mine_ref, other_ref, own_ref, factor_ref, after_ref,
    keep_ref, *rest,
):
    send_refs, (ids_ref, all_ref, total_ref, sems) = rest[:-4], rest[-4:]
    copies = fetch([(slots_ref, ids_ref)], sems)
    frag_dev, nbasis = masked_ref.shape[0], masked_ref.shape[1]
    slots, half = factor_ref.shape[0], mine_ref.shape[0]
    me = lax.axis_index("sub")
    for f in range(frag_dev):
        all_ref[f] = masked_ref[f]
    for f in range(half):
        at = frag_dev + me * half + f
        all_ref[at] = live_square(mine_ref[f, :nbasis], sizes_ref[at, 0:1, 0:1])
        at = frag_dev + (1 - me) * half + f
        all_ref[at] = live_square(other_ref[f, :nbasis], sizes_ref[at, 0:1, 0:1])
    total_ref[:frag_dev] = own_ref[...]
    total_ref[frag_dev] = jnp.zeros_like(total_ref[frag_dev])
    copies[0].wait()

    def add(s, corr):
        target = ids_ref[slots + s, 0]
        total_ref[target] = total_ref[target] + corr

    pipelined(
        slots,
        lambda s: dot(factor_ref[s], all_ref[ids_ref[s, 0]]),
        lambda s, left: dot_t(left, factor_ref[s]),
        add,
    )
    grid_size, _, share, _ = keep_ref.shape
    for step in range(grid_size):
        chip = lax.rem(lax.axis_index("grid") + step, grid_size)
        for f in range(frag_dev):
            keep_ref[step, f] = total_ref[f, at_rows(2 * chip + me, share), :]
            send_refs[step][f] = total_ref[f, at_rows(2 * chip + 1 - me, share), :].astype(BF16)


def away_sum_kernel(keep_ref, *refs):
    count = len(refs) // 2
    for step, (recv_ref, part_ref) in enumerate(zip(refs[:count], refs[count:]), 1):
        part_ref[...] = (keep_ref[step] + recv_ref[...].astype(F32)).astype(BF16)


def relay_kernel(here_ref, in_ref, out_ref):
    out_ref[...] = in_ref[...]


def next_kernel(keep_ref, recv_ref, sources_ref, *out_refs):
    out_refs, after_ref = out_refs[:-1], out_refs[-1]
    after_ref[...] = jnp.zeros_like(after_ref)
    rounds, frag_dev = len(out_refs), keep_ref.shape[0]
    rows = keep_ref.shape[1] // rounds
    for j, out_ref in enumerate(out_refs):
        at = at_rows(lax.rem(lax.axis_index("grid") + j, rounds), rows) if rounds > 1 else slice(0, rows)
        for f in range(frag_dev):
            total = keep_ref[f, at, :].astype(F32) + recv_ref[f, at, :].astype(F32)
            out_ref[f * rows : (f + 1) * rows, :] = total.astype(BF16)
        out_ref[frag_dev * rows :, :] = sources_ref[...]


def before_kernel(*refs):
    in_refs, (keep_ref, send_ref) = refs[:-2], refs[-2:]
    me, (frag_dev, share, _) = lax.axis_index("sub"), keep_ref.shape
    for f in range(frag_dev):
        for at, ref in ((me, keep_ref), (1 - me, send_ref)):
            place = pl.ds(2 * f * share + pl.multiple_of(at * share, share), share)
            ref[f] = sum(in_ref[place, :].astype(F32) for in_ref in in_refs).astype(ref.dtype)


def middle_kernel(keep_ref, home_ref, far_ref, around_ref, recv_ref, *rest):
    part_refs, (out_ref, pot_ref) = rest[:-2], rest[-2:]
    total = keep_ref[0] + recv_ref[...].astype(F32)
    out_ref[...] = total + sum(part_ref[...].astype(F32) for part_ref in part_refs)
    pot_ref[...] = home_ref[...] + far_ref[...] + around_ref[...]


def around_kernel(frag_dev, sizes_ref, mine_ref, other_ref, here_ref, sources_ref, piece_ref, out_ref):
    half, nbasis = mine_ref.shape[0], mine_ref.shape[2]
    me, team, teams = lax.axis_index("sub"), lax.axis_index("frag"), lax.axis_size("frag")
    column = lax.broadcasted_iota(I32, (1, nbasis), 1)
    sources = []
    for ref, start in ((mine_ref, me * half), (other_ref, (1 - me) * half)):
        for f in range(half):
            charge = charge_row(lambda low, high, ref=ref, f=f: ref[f, low:high, low:high], nbasis)
            charge = jnp.where(column < sizes_ref[frag_dev + start + f, 0:1, 0:1], charge, 0.0)
            place = place_rows(ref[f, nbasis:, :].astype(F32))
            sources.append((lax.rem(team + 1, teams) * frag_dev + start + f, charge, place))
    for whose, extra in ((team, sources_ref[...]), (team + teams - 1, piece_ref[piece_ref.shape[0] - EXTRA :, :])):
        for f in range(frag_dev):
            rows = [extra[7 * f + k : 7 * f + k + 1].astype(F32) for k in range(7)]
            place = [rows[2 * d] + rows[2 * d + 1] for d in range(3)]
            sources.append((lax.rem(whose, teams) * frag_dev + f, rows[6], place))
    pts_rows, block_cols = here_ref.shape
    row_x = row_places(pts_rows)
    totals = [jnp.zeros((1, block_cols), F32) for _ in range(pts_rows)]
    fields = [field(charge, place, team, block_cols, row_x) for _, charge, place in sources]
    for (fragment, _, _), rows in zip(sources, over_lanes(fields, block_cols, pts_rows)):
        for r in range(pts_rows):
            totals[r] = totals[r] + jnp.where(here_ref[r : r + 1, :] != fragment, rows[r], 0.0)
    for r in range(pts_rows):
        out_ref[0, r : r + 1, :] = totals[r]


def last_kernel(scale, sizes_ref, masked_ref, own_ref, before_ref, recv_ref, pot_ref, out_ref, potential_ref):
    frag_dev, share, nbasis = out_ref.shape
    member = lax.axis_index("grid") * lax.axis_size("sub") + lax.axis_index("sub")
    row_start = pl.multiple_of(member * share, share)
    rows = row_start + lax.broadcasted_iota(I32, (share, nbasis), 0)
    cols = lax.broadcasted_iota(I32, (share, nbasis), 1)
    for f in range(frag_dev):
        size = sizes_ref[f, 0:1, 0:1]
        correction = own_ref[f] + before_ref[f] + recv_ref[f].astype(F32)
        correction = jnp.where((rows < size) & (cols < size), correction, 0.0)
        out_ref[f] = (masked_ref[f, pl.ds(row_start, share), :].astype(F32) + correction).astype(BF16)
    potential_ref[...] = pot_ref[0] * scale


def turned(value, axis, steps):
    count = lax.axis_size(axis)
    return lax.ppermute(value, axis, [(s, (s + steps) % count) for s in range(count)])


def in_hbm(value):
    return pltpu.with_memory_space_constraint(value, pltpu.HBM)


def shape(dims, dtype):
    return jax.ShapeDtypeStruct(dims, dtype)


def per_device(
    density, basis_size, coupling, pair_first, pair_second, dimer_count, source_coords, grid_region
):
    frag_dev, nbasis, _ = density.shape
    slots = coupling.shape[0]
    teams, grid_size, sub_size = (lax.axis_size(a) for a in ("frag", "grid", "sub"))
    assert sub_size == 2 and frag_dev == 2 and grid_size % sub_size == 0
    rounds = grid_size // sub_size
    assert teams >= 4 and teams & (teams - 1) == 0
    share = nbasis // (grid_size * sub_size)
    half = frag_dev // sub_size
    pts_rows, total_cols = grid_region.shape
    block_cols = total_cols // teams

    smem = pl.BlockSpec(memory_space=pltpu.SMEM)
    vmem = pl.BlockSpec(memory_space=pltpu.VMEM)
    hbm = pl.BlockSpec(memory_space=pltpu.HBM)
    square = (nbasis, nbasis)

    def call(kernel, name, ins, outs, out_specs, scratch=(), flops=0):
        return pl.pallas_call(
            kernel,
            out_shape=outs,
            in_specs=ins,
            out_specs=out_specs,
            scratch_shapes=scratch,
            compiler_params=pltpu.CompilerParams(vmem_limit_bytes=VMEM_LIMIT),
            cost_estimate=pl.CostEstimate(flops=flops, bytes_accessed=1 << 20, transcendentals=0),
            name=name,
        )

    work = 4 * slots * nbasis**3
    by_chip = (grid_size, frag_dev, share, nbasis)
    halves = shape((frag_dev, nbasis // sub_size, nbasis), BF16)
    sent_halves = shape((frag_dev, nbasis // sub_size + EXTRA, nbasis), BF16)
    places = in_hbm(jnp.transpose(source_coords, (1, 0, 2)))
    payload = call(
        head_kernel,
        "head",
        [hbm] * 2,
        shape((half, nbasis + EXTRA, nbasis), BF16),
        vmem,
        [pltpu.VMEM((3, frag_dev, nbasis), F32), pltpu.SemaphoreType.DMA((1 + nbasis // 128,))],
    )(in_hbm(density), places)
    mine = turned(payload, "frag", -1)

    next_keep, next_send, own_part, factors, masked, slot_ids, sizes, here, sources, *slabs = call(
        right_kernel,
        "right",
        [hbm] * 3 + [smem, vmem] + [hbm] * 4,
        (
            halves, sent_halves, shape((frag_dev,) + square, F32),
            shape((slots,) + square, BF16), shape((frag_dev,) + square, BF16),
            shape((2 * slots, 128), I32), shape((2 * frag_dev, 8, 128), I32), shape((pts_rows, block_cols), I32),
            shape((EXTRA, nbasis), BF16),
        ) + (shape((teams // 4, pts_rows, block_cols), F32),) * 4,
        (vmem,) * 13,
        [
            pltpu.SMEM(basis_size.shape, I32), pltpu.SMEM((slots,), I32), pltpu.SMEM((slots,), I32),
            pltpu.SMEM((4 * slots,), I32), pltpu.VMEM((half,) + square, BF16), pltpu.VMEM((3, frag_dev, nbasis), F32),
            pltpu.VMEM(grid_region.shape, I32), pltpu.VMEM((2 * frag_dev + 1,) + square, F32),
            pltpu.SemaphoreType.DMA((6 + slots,)),
        ],
        work,
    )(
        in_hbm(basis_size), in_hbm(pair_first), in_hbm(pair_second), dimer_count, payload, in_hbm(density),
        in_hbm(coupling), places, in_hbm(grid_region),
    )

    if teams == 4:
        home, far = slabs[0], turned(slabs[2], "frag", 2)
    else:
        slabs = jnp.concatenate(slabs)
        while slabs.shape[0] > 1:
            rest = slabs.shape[0] // 2
            slabs = slabs[:rest] + turned(slabs[rest:], "frag", rest)
        home, far = slabs, jnp.zeros_like(slabs)

    *pieces, after = call(
        next_kernel,
        "next_sum",
        [vmem] * 3,
        [shape((frag_dev * nbasis // grid_size + EXTRA, nbasis), BF16)] * rounds + [shape((8, 128), F32)],
        (vmem,) * (rounds + 1),
    )(next_keep, turned(next_send, "sub", 1), sources)
    for j, value in enumerate(pieces):
        pairs = []
        for t in range(teams):
            for g in range(grid_size):
                for c in range(sub_size):
                    to = (c * rounds + (g + j) % rounds, g // rounds) if t + 1 < teams else (g, c)
                    to = ((t + 1) % teams * grid_size + to[0]) * sub_size + to[1]
                    pairs.append(((t * grid_size + g) * sub_size + c, to))
        pieces[j] = lax.ppermute(value, ("frag", "grid", "sub"), pairs)

    mine = call(relay_kernel, "relay", [vmem] * 2, shape(payload.shape, BF16), vmem)(here, mine)
    other = turned(mine, "sub", 1)
    own_keep, *own_sends = call(
        left_kernel,
        "left",
        [vmem] * 8,
        [shape(by_chip, F32)] + [shape((frag_dev, share, nbasis), BF16)] * grid_size,
        (vmem,) * (1 + grid_size),
        [
            pltpu.SMEM((2 * slots, 128), I32), pltpu.VMEM((2 * frag_dev,) + square, BF16),
            pltpu.VMEM((frag_dev + 1,) + square, F32), pltpu.SemaphoreType.DMA((1,)),
        ],
        work,
    )(slot_ids, sizes, masked, mine, other, own_part, factors, after)
    mine_rows = (frag_dev, share, nbasis)
    own_recv, *away_recvs = [turned(value, "sub", 1) for value in own_sends]
    parts = call(
        away_sum_kernel,
        "away_sum",
        [vmem] * grid_size,
        [shape(mine_rows, BF16)] * (grid_size - 1),
        (vmem,) * (grid_size - 1),
    )(own_keep, *away_recvs)
    parts = [turned(part, "grid", step) for step, part in enumerate(parts, 1)]

    slab = shape((1, pts_rows, block_cols), F32)
    before, passed = call(
        before_kernel,
        "before",
        [vmem] * rounds,
        (shape(mine_rows, F32), shape(mine_rows, BF16)),
        (vmem,) * 2,
    )(*pieces)
    passed = turned(passed, "sub", 1)
    around = call(functools.partial(around_kernel, frag_dev), "around", [vmem] * 6, slab, vmem)(
        sizes, mine, other, here, sources, pieces[0]
    )
    own, pot = call(
        middle_kernel,
        "middle",
        [vmem] * (5 + len(parts)),
        (shape(mine_rows, F32), slab),
        (vmem,) * 2,
        (),
        10**10,
    )(own_keep, home, far, around, own_recv, *parts)

    scale = 8.0 / math.sqrt(frag_dev * teams * nbasis)
    return call(
        functools.partial(last_kernel, scale),
        "last",
        [vmem] * 6,
        (shape(mine_rows, BF16), shape((pts_rows, block_cols), F32)),
        (vmem,) * 2,
    )(sizes, masked, own, before, passed, pot)


def solution(mesh):
    placed = (
        P(("groups", "frag"), None, None),
        P(),
        P(("groups", "frag", "grid", "sub"), None, None),
        P(("frag", "grid", "sub")),
        P(("frag", "grid", "sub")),
        P(("frag", "grid", "sub")),
        P(("groups", "frag"), None, None),
        P(("grid", "sub"), None),
    )
    return jax.shard_map(
        per_device,
        mesh=mesh,
        in_specs=placed,
        out_specs=(
            P(("groups", "frag"), ("grid", "sub"), None),
            P(("groups", "grid", "sub"), "frag"),
        ),
        check_vma=False,
    )
```

```python
import functools
import math

import jax
import jax.numpy as jnp
from jax import lax
from jax.experimental import pallas as pl
from jax.experimental.pallas import tpu as pltpu
from jax.sharding import PartitionSpec as P

VMEM_LIMIT = 24 * 1024 * 1024
EXTRA = 16
BF16, F32, I32 = jnp.bfloat16, jnp.float32, jnp.int32


def live_square(values, size):
    rows = lax.broadcasted_iota(I32, values.shape, 0)
    cols = lax.broadcasted_iota(I32, values.shape, 1)
    return jnp.where((rows < size) & (cols < size), values.astype(F32), 0.0).astype(BF16)


def charge_row(read, nbasis):
    tile = 128
    parts = []
    for at in range(0, nbasis, tile):
        block = read(at, at + tile).astype(F32)
        rows = lax.broadcasted_iota(I32, block.shape, 0)
        cols = lax.broadcasted_iota(I32, block.shape, 1)
        parts.append(jnp.sum(jnp.where(rows == cols, block, 0.0), axis=0, keepdims=True))
    return jnp.concatenate(parts, axis=1)


def at_rows(block, size):
    return pl.ds(pl.multiple_of(block * size, size), size)


def thirds(values):
    high = values.astype(BF16).astype(F32)
    middle = (values - high).astype(BF16).astype(F32)
    return [high, middle, values - high - middle]


def field(charge, place, block, block_cols, row_x):
    src_x, src_y, src_z = place
    point_z = 0.25 * lax.broadcasted_iota(I32, (64, charge.shape[1]), 0).astype(F32)
    along_z = (point_z - src_z) ** 2 + 1.0
    parts = []
    for x in row_x:
        for step in range(block_cols // 64):
            point_y = 0.25 * (block * (block_cols // 64) + step).astype(F32)
            in_plane = (x - src_x) ** 2 + (point_y - src_y) ** 2
            value = charge * lax.rsqrt(along_z + in_plane)
            parts.append(sum(value[:, at : at + 128] for at in range(0, value.shape[1], 128)))
    return jnp.concatenate(parts)


def over_lanes(points, block_cols, pts_rows):
    rows = jnp.concatenate(points)
    ones = jnp.ones((16, 128), BF16)
    total = sum(dot_t(ones, part.astype(BF16)) for part in thirds(rows))
    size = pts_rows * block_cols
    return [
        [total[0:1, k * size + r * block_cols : k * size + (r + 1) * block_cols] for r in range(pts_rows)]
        for k in range(len(points))
    ]


def row_places(pts_rows):
    member = lax.axis_index("grid") * lax.axis_size("sub") + lax.axis_index("sub")
    return [0.25 * (member * pts_rows + r).astype(F32) for r in range(pts_rows)]


def place_rows(extra):
    return [sum(extra[3 * d + k : 3 * d + k + 1] for k in range(3)) for d in range(3)]


def by_core(total_ref, row, keep_ref, send_ref):
    me, rows = lax.axis_index("sub"), keep_ref.shape[-2]
    for f in range(keep_ref.shape[0]):
        keep_ref[f] = total_ref[f, pl.ds(row + pl.multiple_of(me * rows, rows), rows), :].astype(keep_ref.dtype)
        other = total_ref[f, pl.ds(row + pl.multiple_of((1 - me) * rows, rows), rows), :]
        send_ref[f, :rows] = other.astype(send_ref.dtype)


def pipelined(slots, first_dot, second_dot, add):
    held = None
    for slot in range(slots + 1):
        now = first_dot(slot).astype(BF16) if slot < slots else None
        if held is not None:
            add(slot - 1, second_dot(slot - 1, held))
        held = now


def dot(a, b):
    return jnp.dot(a, b, preferred_element_type=F32)


def dot_t(a, b):
    return lax.dot_general(a, b, (((1,), (1,)), ((), ())), preferred_element_type=F32)


def fetch(pairs, sems):
    copies = [pltpu.make_async_copy(source, target, sems.at[i]) for i, (source, target) in enumerate(pairs)]
    for copy in copies:
        copy.start()
    return copies


def head_kernel(density_hbm, coords_hbm, payload_ref, coords_ref, sems):
    half, nbasis = payload_ref.shape[0], payload_ref.shape[2]
    at = lax.axis_index("sub") * half
    copies = fetch(
        [(coords_hbm, coords_ref)]
        + [
            (density_hbm.at[pl.ds(at, half), pl.ds(low, 128)], payload_ref.at[:, pl.ds(low, 128)])
            for low in range(0, nbasis, 128)
        ],
        sems,
    )
    copies[0].wait()
    for f in range(half):
        rows = [part for d in range(3) for part in thirds(coords_ref[d, pl.ds(at + f, 1), :])]
        rows.append(jnp.zeros((EXTRA - len(rows), nbasis), F32))
        payload_ref[f, nbasis:, :] = jnp.concatenate(rows).astype(BF16)
    for copy in copies[1:]:
        copy.wait()


def right_kernel(
    size_hbm, first_hbm, second_hbm, count_ref, payload_ref, density_hbm, coupling_hbm, coords_hbm, region_hbm,
    keep_ref, send_ref, own_ref, factor_ref, masked_ref, slots_ref, sizes_ref, here_ref, sources_ref, *rest,
):
    slab_refs, rest = rest[:4], rest[4:]
    size_ref, first_ref, second_ref, ids_ref, density_ref, coords_ref, region_ref, total_ref, sems = rest
    frag_dev, nbasis, slots = masked_ref.shape[0], masked_ref.shape[1], factor_ref.shape[0]
    half = payload_ref.shape[0]
    mine, theirs = lax.axis_index("sub") * half, (1 - lax.axis_index("sub")) * half
    copies = fetch(
        [
            (size_hbm, size_ref), (first_hbm, first_ref), (second_hbm, second_ref),
            (density_hbm.at[pl.ds(theirs, half)], density_ref), (coords_hbm, coords_ref), (region_hbm, region_ref),
        ]
        + [(coupling_hbm.at[s], factor_ref.at[s]) for s in range(slots)],
        sems,
    )
    total_ref[...] = jnp.zeros_like(total_ref)
    for copy in copies[:6]:
        copy.wait()
    team = lax.axis_index("frag")
    base = team * frag_dev
    trash = 2 * frag_dev
    for s in range(slots):
        live = s < count_ref[0]
        first = jnp.clip(first_ref[s] - base, 0, frag_dev - 1)
        second = jnp.clip(second_ref[s] - base, 0, trash - 1)
        ids_ref[s] = first
        ids_ref[slots + s] = second
        ids_ref[2 * slots + s] = jnp.where(live, second, trash)
        ids_ref[3 * slots + s] = jnp.where(live, first, frag_dev)
    for f in range(2 * frag_dev):
        sizes_ref[f] = jnp.full((8, 128), size_ref[lax.rem(base + f, size_ref.shape[0])], I32)
    for f in range(half):
        masked_ref[mine + f] = live_square(payload_ref[f, :nbasis], size_ref[base + mine + f])
        masked_ref[theirs + f] = live_square(density_ref[f], size_ref[base + theirs + f])
    sources = [
        (
            charge_row(lambda low, high, f=f: masked_ref[f, low:high, low:high], nbasis),
            [coords_ref[d, f : f + 1, :] for d in range(3)],
        )
        for f in range(frag_dev)
    ]
    rows = []
    for charge, place in sources:
        rows += [part for values in place for part in thirds(values)[:2]] + [charge]
    rows.append(jnp.zeros((EXTRA - len(rows), nbasis), F32))
    sources_ref[...] = jnp.concatenate(rows).astype(BF16)

    pts_rows = region_ref.shape[0]
    each, block_cols = slab_refs[0].shape[0], slab_refs[0].shape[2]
    teams = len(slab_refs) * each
    row_x = row_places(pts_rows)

    def one_block(step, slab_ref, at):
        block = lax.rem(team + step, teams)
        region = region_ref[:, pl.ds(pl.multiple_of(block * block_cols, block_cols), block_cols)]
        fields = [field(charge, place, block, block_cols, row_x) for charge, place in sources]
        fields = over_lanes(fields, block_cols, pts_rows)
        for r in range(pts_rows):
            here = [jnp.where(region[r : r + 1] != base + f, fields[f][r], 0.0) for f in range(frag_dev)]
            slab_ref[at, r : r + 1, :] = sum(here)

    if each == 1:
        one_block(2, slab_refs[2], 0)
    else:

        @pl.loop(0, each)
        def _(step):
            for k, slab_ref in enumerate(slab_refs):
                one_block(k * each + step, slab_ref, step)

    for k in (0, 1, teams - 1):
        slab_refs[k // each][k % each] = jnp.zeros((pts_rows, block_cols), F32)
    here_ref[...] = region_ref[:, pl.ds(pl.multiple_of(team * block_cols, block_cols), block_cols)]

    for copy in copies[6:]:
        copy.wait()

    def add(s, corr):
        target = ids_ref[2 * slots + s]
        total_ref[target] = total_ref[target] + corr

    pipelined(
        slots,
        lambda s: dot(factor_ref[s].T, masked_ref[ids_ref[s]]),
        lambda s, right: dot(right, factor_ref[s]),
        add,
    )
    for s in range(slots):
        for k, row in ((1, s), (3, slots + s)):
            slots_ref[row : row + 1] = jnp.full((1, 128), ids_ref[k * slots + s], I32)
    own_ref[...] = total_ref[:frag_dev]
    by_core(total_ref.at[pl.ds(frag_dev, frag_dev)], 0, keep_ref, send_ref)
    send_ref[:, keep_ref.shape[1] :, :] = jnp.zeros((frag_dev, EXTRA, nbasis), BF16)


def left_kernel(
    slots_ref, sizes_ref, masked_ref, mine_ref, other_ref, own_ref, factor_ref, after_ref,
    keep_ref, *rest,
):
    send_refs, (ids_ref, all_ref, total_ref, sems) = rest[:-4], rest[-4:]
    copies = fetch([(slots_ref, ids_ref)], sems)
    frag_dev, nbasis = masked_ref.shape[0], masked_ref.shape[1]
    slots, half = factor_ref.shape[0], mine_ref.shape[0]
    me = lax.axis_index("sub")
    for f in range(frag_dev):
        all_ref[f] = masked_ref[f]
    for f in range(half):
        at = frag_dev + me * half + f
        all_ref[at] = live_square(mine_ref[f, :nbasis], sizes_ref[at, 0:1, 0:1])
        at = frag_dev + (1 - me) * half + f
        all_ref[at] = live_square(other_ref[f, :nbasis], sizes_ref[at, 0:1, 0:1])
    copies[0].wait()
    total_ref[:frag_dev] = own_ref[...]
    total_ref[frag_dev] = jnp.zeros_like(total_ref[frag_dev])

    def add(s, corr):
        target = ids_ref[slots + s, 0]
        total_ref[target] = total_ref[target] + corr

    pipelined(
        slots,
        lambda s: dot(factor_ref[s], all_ref[ids_ref[s, 0]]),
        lambda s, left: dot_t(left, factor_ref[s]),
        add,
    )
    grid_size, _, share, _ = keep_ref.shape
    for step in range(grid_size):
        chip = lax.rem(lax.axis_index("grid") + step, grid_size)
        for f in range(frag_dev):
            keep_ref[step, f] = total_ref[f, at_rows(2 * chip + me, share), :]
            send_refs[step][f] = total_ref[f, at_rows(2 * chip + 1 - me, share), :].astype(BF16)


def away_sum_kernel(keep_ref, *refs):
    count = len(refs) // 2
    for step, (recv_ref, part_ref) in enumerate(zip(refs[:count], refs[count:]), 1):
        part_ref[...] = (keep_ref[step] + recv_ref[...].astype(F32)).astype(BF16)


def relay_kernel(here_ref, in_ref, out_ref):
    out_ref[...] = in_ref[...]


def next_kernel(keep_ref, recv_ref, sources_ref, *out_refs):
    out_refs, after_ref = out_refs[:-1], out_refs[-1]
    after_ref[...] = jnp.zeros_like(after_ref)
    rounds, frag_dev = len(out_refs), keep_ref.shape[0]
    rows = keep_ref.shape[1] // rounds
    for j, out_ref in enumerate(out_refs):
        at = at_rows(lax.rem(lax.axis_index("grid") + j, rounds), rows) if rounds > 1 else slice(0, rows)
        for f in range(frag_dev):
            total = keep_ref[f, at, :].astype(F32) + recv_ref[f, at, :].astype(F32)
            out_ref[f * rows : (f + 1) * rows, :] = total.astype(BF16)
        out_ref[frag_dev * rows :, :] = sources_ref[...]


def before_kernel(*refs):
    in_refs, (keep_ref, send_ref) = refs[:-2], refs[-2:]
    me, (frag_dev, share, _) = lax.axis_index("sub"), keep_ref.shape
    for f in range(frag_dev):
        for at, ref in ((me, keep_ref), (1 - me, send_ref)):
            place = pl.ds(2 * f * share + pl.multiple_of(at * share, share), share)
            ref[f] = sum(in_ref[place, :].astype(F32) for in_ref in in_refs).astype(ref.dtype)


def middle_kernel(keep_ref, home_ref, far_ref, around_ref, *rest):
    part_refs, (out_ref, pot_ref) = rest[:-2], rest[-2:]
    out_ref[...] = keep_ref[0] + sum(part_ref[...].astype(F32) for part_ref in part_refs)
    pot_ref[...] = home_ref[...] + far_ref[...] + around_ref[...]


def around_kernel(frag_dev, sizes_ref, mine_ref, other_ref, here_ref, sources_ref, piece_ref, out_ref):
    half, nbasis = mine_ref.shape[0], mine_ref.shape[2]
    me, team, teams = lax.axis_index("sub"), lax.axis_index("frag"), lax.axis_size("frag")
    column = lax.broadcasted_iota(I32, (1, nbasis), 1)
    sources = []
    for ref, start in ((mine_ref, me * half), (other_ref, (1 - me) * half)):
        for f in range(half):
            charge = charge_row(lambda low, high, ref=ref, f=f: ref[f, low:high, low:high], nbasis)
            charge = jnp.where(column < sizes_ref[frag_dev + start + f, 0:1, 0:1], charge, 0.0)
            place = place_rows(ref[f, nbasis:, :].astype(F32))
            sources.append((lax.rem(team + 1, teams) * frag_dev + start + f, charge, place))
    for whose, extra in ((team, sources_ref[...]), (team + teams - 1, piece_ref[piece_ref.shape[0] - EXTRA :, :])):
        for f in range(frag_dev):
            rows = [extra[7 * f + k : 7 * f + k + 1].astype(F32) for k in range(7)]
            place = [rows[2 * d] + rows[2 * d + 1] for d in range(3)]
            sources.append((lax.rem(whose, teams) * frag_dev + f, rows[6], place))
    pts_rows, block_cols = here_ref.shape
    row_x = row_places(pts_rows)
    totals = [jnp.zeros((1, block_cols), F32) for _ in range(pts_rows)]
    fields = [field(charge, place, team, block_cols, row_x) for _, charge, place in sources]
    for (fragment, _, _), rows in zip(sources, over_lanes(fields, block_cols, pts_rows)):
        for r in range(pts_rows):
            totals[r] = totals[r] + jnp.where(here_ref[r : r + 1, :] != fragment, rows[r], 0.0)
    for r in range(pts_rows):
        out_ref[0, r : r + 1, :] = totals[r]


def last_kernel(
    scale, sizes_ref, masked_ref, own_ref, too_ref, before_ref, recv_ref, pot_ref, out_ref, potential_ref
):
    frag_dev, share, nbasis = out_ref.shape
    member = lax.axis_index("grid") * lax.axis_size("sub") + lax.axis_index("sub")
    row_start = pl.multiple_of(member * share, share)
    rows = row_start + lax.broadcasted_iota(I32, (share, nbasis), 0)
    cols = lax.broadcasted_iota(I32, (share, nbasis), 1)
    for f in range(frag_dev):
        size = sizes_ref[f, 0:1, 0:1]
        correction = own_ref[f] + before_ref[f] + (recv_ref[f].astype(F32) + too_ref[f].astype(F32))
        correction = jnp.where((rows < size) & (cols < size), correction, 0.0)
        out_ref[f] = (masked_ref[f, pl.ds(row_start, share), :].astype(F32) + correction).astype(BF16)
    potential_ref[...] = pot_ref[0] * scale


def turned(value, axis, steps):
    count = lax.axis_size(axis)
    return lax.ppermute(value, axis, [(s, (s + steps) % count) for s in range(count)])


def in_hbm(value):
    return pltpu.with_memory_space_constraint(value, pltpu.HBM)


def shape(dims, dtype):
    return jax.ShapeDtypeStruct(dims, dtype)


def per_device(
    density, basis_size, coupling, pair_first, pair_second, dimer_count, source_coords, grid_region
):
    frag_dev, nbasis, _ = density.shape
    slots = coupling.shape[0]
    teams, grid_size, sub_size = (lax.axis_size(a) for a in ("frag", "grid", "sub"))
    assert sub_size == 2 and frag_dev == 2 and grid_size % sub_size == 0
    rounds = grid_size // sub_size
    assert teams >= 4 and teams & (teams - 1) == 0
    share = nbasis // (grid_size * sub_size)
    half = frag_dev // sub_size
    pts_rows, total_cols = grid_region.shape
    block_cols = total_cols // teams

    smem = pl.BlockSpec(memory_space=pltpu.SMEM)
    vmem = pl.BlockSpec(memory_space=pltpu.VMEM)
    hbm = pl.BlockSpec(memory_space=pltpu.HBM)
    square = (nbasis, nbasis)

    def call(kernel, name, ins, outs, out_specs, scratch=(), flops=0):
        return pl.pallas_call(
            kernel,
            out_shape=outs,
            in_specs=ins,
            out_specs=out_specs,
            scratch_shapes=scratch,
            compiler_params=pltpu.CompilerParams(vmem_limit_bytes=VMEM_LIMIT),
            cost_estimate=pl.CostEstimate(flops=flops, bytes_accessed=1 << 20, transcendentals=0),
            name=name,
        )

    work = 4 * slots * nbasis**3
    by_chip = (grid_size, frag_dev, share, nbasis)
    halves = shape((frag_dev, nbasis // sub_size, nbasis), BF16)
    sent_halves = shape((frag_dev, nbasis // sub_size + EXTRA, nbasis), BF16)
    places = in_hbm(jnp.transpose(source_coords, (1, 0, 2)))
    payload = call(
        head_kernel,
        "head",
        [hbm] * 2,
        shape((half, nbasis + EXTRA, nbasis), BF16),
        vmem,
        [pltpu.VMEM((3, frag_dev, nbasis), F32), pltpu.SemaphoreType.DMA((1 + nbasis // 128,))],
    )(in_hbm(density), places)
    mine = turned(payload, "frag", -1)

    next_keep, next_send, own_part, factors, masked, slot_ids, sizes, here, sources, *slabs = call(
        right_kernel,
        "right",
        [hbm] * 3 + [smem, vmem] + [hbm] * 4,
        (
            halves, sent_halves, shape((frag_dev,) + square, F32),
            shape((slots,) + square, BF16), shape((frag_dev,) + square, BF16),
            shape((2 * slots, 128), I32), shape((2 * frag_dev, 8, 128), I32), shape((pts_rows, block_cols), I32),
            shape((EXTRA, nbasis), BF16),
        ) + (shape((teams // 4, pts_rows, block_cols), F32),) * 4,
        (vmem,) * 13,
        [
            pltpu.SMEM(basis_size.shape, I32), pltpu.SMEM((slots,), I32), pltpu.SMEM((slots,), I32),
            pltpu.SMEM((4 * slots,), I32), pltpu.VMEM((half,) + square, BF16), pltpu.VMEM((3, frag_dev, nbasis), F32),
            pltpu.VMEM(grid_region.shape, I32), pltpu.VMEM((2 * frag_dev + 1,) + square, F32),
            pltpu.SemaphoreType.DMA((6 + slots,)),
        ],
        work,
    )(
        in_hbm(basis_size), in_hbm(pair_first), in_hbm(pair_second), dimer_count, payload, in_hbm(density),
        in_hbm(coupling), places, in_hbm(grid_region),
    )

    if teams == 4:
        home, far = slabs[0], turned(slabs[2], "frag", 2)
    else:
        slabs = jnp.concatenate(slabs)
        while slabs.shape[0] > 1:
            rest = slabs.shape[0] // 2
            slabs = slabs[:rest] + turned(slabs[rest:], "frag", rest)
        home, far = slabs, jnp.zeros_like(slabs)

    *pieces, after = call(
        next_kernel,
        "next_sum",
        [vmem] * 3,
        [shape((frag_dev * nbasis // grid_size + EXTRA, nbasis), BF16)] * rounds + [shape((8, 128), F32)],
        (vmem,) * (rounds + 1),
    )(next_keep, turned(next_send, "sub", 1), sources)
    for j, value in enumerate(pieces):
        pairs = []
        for t in range(teams):
            for g in range(grid_size):
                for c in range(sub_size):
                    to = (c * rounds + (g + j) % rounds, g // rounds) if t + 1 < teams else (g, c)
                    to = ((t + 1) % teams * grid_size + to[0]) * sub_size + to[1]
                    pairs.append(((t * grid_size + g) * sub_size + c, to))
        pieces[j] = lax.ppermute(value, ("frag", "grid", "sub"), pairs)

    mine = call(relay_kernel, "relay", [vmem] * 2, shape(payload.shape, BF16), vmem)(here, mine)
    other = turned(mine, "sub", 1)
    own_keep, *own_sends = call(
        left_kernel,
        "left",
        [vmem] * 8,
        [shape(by_chip, F32)] + [shape((frag_dev, share, nbasis), BF16)] * grid_size,
        (vmem,) * (1 + grid_size),
        [
            pltpu.SMEM((2 * slots, 128), I32), pltpu.VMEM((2 * frag_dev,) + square, BF16),
            pltpu.VMEM((frag_dev + 1,) + square, F32), pltpu.SemaphoreType.DMA((1,)),
        ],
        work,
    )(slot_ids, sizes, masked, mine, other, own_part, factors, after)
    mine_rows = (frag_dev, share, nbasis)
    own_recv, *away_recvs = [turned(value, "sub", 1) for value in own_sends]
    parts = call(
        away_sum_kernel,
        "away_sum",
        [vmem] * grid_size,
        [shape(mine_rows, BF16)] * (grid_size - 1),
        (vmem,) * (grid_size - 1),
    )(own_keep, *away_recvs)
    parts = [turned(part, "grid", step) for step, part in enumerate(parts, 1)]

    slab = shape((1, pts_rows, block_cols), F32)
    before, passed = call(
        before_kernel,
        "before",
        [vmem] * rounds,
        (shape(mine_rows, F32), shape(mine_rows, BF16)),
        (vmem,) * 2,
    )(*pieces)
    passed = turned(passed, "sub", 1)
    around = call(functools.partial(around_kernel, frag_dev), "around", [vmem] * 6, slab, vmem)(
        sizes, mine, other, here, sources, pieces[0]
    )
    own, pot = call(
        middle_kernel,
        "middle",
        [vmem] * (4 + len(parts)),
        (shape(mine_rows, F32), slab),
        (vmem,) * 2,
        (),
        10**10,
    )(own_keep, home, far, around, *parts)

    scale = 8.0 / math.sqrt(frag_dev * teams * nbasis)
    return call(
        functools.partial(last_kernel, scale),
        "last",
        [vmem] * 7,
        (shape(mine_rows, BF16), shape((pts_rows, block_cols), F32)),
        (vmem,) * 2,
    )(sizes, masked, own, own_recv, before, passed, pot)


def solution(mesh):
    placed = (
        P(("groups", "frag"), None, None),
        P(),
        P(("groups", "frag", "grid", "sub"), None, None),
        P(("frag", "grid", "sub")),
        P(("frag", "grid", "sub")),
        P(("frag", "grid", "sub")),
        P(("groups", "frag"), None, None),
        P(("grid", "sub"), None),
    )
    return jax.shard_map(
        per_device,
        mesh=mesh,
        in_specs=placed,
        out_specs=(
            P(("groups", "frag"), ("grid", "sub"), None),
            P(("groups", "grid", "sub"), "frag"),
        ),
        check_vma=False,
    )
```

```python
import functools
import math

import jax
import jax.numpy as jnp
from jax import lax
from jax.experimental import pallas as pl
from jax.experimental.pallas import tpu as pltpu
from jax.sharding import PartitionSpec as P

VMEM_LIMIT = 24 * 1024 * 1024
EXTRA = 16
BF16, F32, I32 = jnp.bfloat16, jnp.float32, jnp.int32


def live_square(values, size):
    rows = lax.broadcasted_iota(I32, values.shape, 0)
    cols = lax.broadcasted_iota(I32, values.shape, 1)
    return jnp.where((rows < size) & (cols < size), values.astype(F32), 0.0).astype(BF16)


def charge_row(read, nbasis):
    tile = 128
    parts = []
    for at in range(0, nbasis, tile):
        block = read(at, at + tile).astype(F32)
        rows = lax.broadcasted_iota(I32, block.shape, 0)
        cols = lax.broadcasted_iota(I32, block.shape, 1)
        parts.append(jnp.sum(jnp.where(rows == cols, block, 0.0), axis=0, keepdims=True))
    return jnp.concatenate(parts, axis=1)


def at_rows(block, size):
    return pl.ds(pl.multiple_of(block * size, size), size)


def thirds(values):
    high = values.astype(BF16).astype(F32)
    middle = (values - high).astype(BF16).astype(F32)
    return [high, middle, values - high - middle]


def field(charge, place, block, block_cols, row_x):
    src_x, src_y, src_z = place
    point_z = 0.25 * lax.broadcasted_iota(I32, (64, charge.shape[1]), 0).astype(F32)
    along_z = (point_z - src_z) ** 2 + 1.0
    parts = []
    for x in row_x:
        for step in range(block_cols // 64):
            point_y = 0.25 * (block * (block_cols // 64) + step).astype(F32)
            in_plane = (x - src_x) ** 2 + (point_y - src_y) ** 2
            value = charge * lax.rsqrt(along_z + in_plane)
            parts.append(sum(value[:, at : at + 128] for at in range(0, value.shape[1], 128)))
    return jnp.concatenate(parts)


def over_lanes(points, block_cols, pts_rows):
    rows = jnp.concatenate(points)
    ones = jnp.ones((16, 128), BF16)
    total = sum(dot_t(ones, part.astype(BF16)) for part in thirds(rows)[:2])
    size = pts_rows * block_cols
    return [
        [total[0:1, k * size + r * block_cols : k * size + (r + 1) * block_cols] for r in range(pts_rows)]
        for k in range(len(points))
    ]


def row_places(pts_rows):
    member = lax.axis_index("grid") * lax.axis_size("sub") + lax.axis_index("sub")
    return [0.25 * (member * pts_rows + r).astype(F32) for r in range(pts_rows)]


def place_rows(extra):
    return [sum(extra[3 * d + k : 3 * d + k + 1] for k in range(3)) for d in range(3)]


def by_core(total_ref, row, keep_ref, send_ref):
    me, rows = lax.axis_index("sub"), keep_ref.shape[-2]
    for f in range(keep_ref.shape[0]):
        keep_ref[f] = total_ref[f, pl.ds(row + pl.multiple_of(me * rows, rows), rows), :].astype(keep_ref.dtype)
        other = total_ref[f, pl.ds(row + pl.multiple_of((1 - me) * rows, rows), rows), :]
        send_ref[f, :rows] = other.astype(send_ref.dtype)


def pipelined(slots, first_dot, second_dot, add):
    held = None
    for slot in range(slots + 1):
        now = first_dot(slot).astype(BF16) if slot < slots else None
        if held is not None:
            add(slot - 1, second_dot(slot - 1, held))
        held = now


def dot(a, b):
    return jnp.dot(a, b, preferred_element_type=F32)


def dot_t(a, b):
    return lax.dot_general(a, b, (((1,), (1,)), ((), ())), preferred_element_type=F32)


def fetch(pairs, sems):
    copies = [pltpu.make_async_copy(source, target, sems.at[i]) for i, (source, target) in enumerate(pairs)]
    for copy in copies:
        copy.start()
    return copies


def head_kernel(density_hbm, coords_hbm, payload_ref, coords_ref, sems):
    half, nbasis = payload_ref.shape[0], payload_ref.shape[2]
    at = lax.axis_index("sub") * half
    copies = fetch(
        [(coords_hbm, coords_ref)]
        + [
            (density_hbm.at[pl.ds(at, half), pl.ds(low, 128)], payload_ref.at[:, pl.ds(low, 128)])
            for low in range(0, nbasis, 128)
        ],
        sems,
    )
    copies[0].wait()
    for f in range(half):
        rows = [part for d in range(3) for part in thirds(coords_ref[d, pl.ds(at + f, 1), :])]
        rows.append(jnp.zeros((EXTRA - len(rows), nbasis), F32))
        payload_ref[f, nbasis:, :] = jnp.concatenate(rows).astype(BF16)
    for copy in copies[1:]:
        copy.wait()


def right_kernel(
    size_hbm, first_hbm, second_hbm, count_ref, payload_ref, density_hbm, coupling_hbm, coords_hbm, region_hbm,
    keep_ref, send_ref, own_ref, factor_ref, masked_ref, slots_ref, sizes_ref, here_ref, sources_ref, *rest,
):
    slab_refs, rest = rest[:4], rest[4:]
    size_ref, first_ref, second_ref, ids_ref, density_ref, coords_ref, region_ref, total_ref, sems = rest
    frag_dev, nbasis, slots = masked_ref.shape[0], masked_ref.shape[1], factor_ref.shape[0]
    half = payload_ref.shape[0]
    mine, theirs = lax.axis_index("sub") * half, (1 - lax.axis_index("sub")) * half
    copies = fetch(
        [
            (size_hbm, size_ref), (first_hbm, first_ref), (second_hbm, second_ref),
            (density_hbm.at[pl.ds(theirs, half)], density_ref), (coords_hbm, coords_ref), (region_hbm, region_ref),
        ]
        + [(coupling_hbm.at[s], factor_ref.at[s]) for s in range(slots)],
        sems,
    )
    total_ref[...] = jnp.zeros_like(total_ref)
    for copy in copies[:6]:
        copy.wait()
    team = lax.axis_index("frag")
    base = team * frag_dev
    trash = 2 * frag_dev
    for s in range(slots):
        live = s < count_ref[0]
        first = jnp.clip(first_ref[s] - base, 0, frag_dev - 1)
        second = jnp.clip(second_ref[s] - base, 0, trash - 1)
        ids_ref[s] = first
        ids_ref[slots + s] = second
        ids_ref[2 * slots + s] = jnp.where(live, second, trash)
        ids_ref[3 * slots + s] = jnp.where(live, first, frag_dev)
    for f in range(2 * frag_dev):
        sizes_ref[f] = jnp.full((8, 128), size_ref[lax.rem(base + f, size_ref.shape[0])], I32)
    for f in range(half):
        masked_ref[mine + f] = live_square(payload_ref[f, :nbasis], size_ref[base + mine + f])
        masked_ref[theirs + f] = live_square(density_ref[f], size_ref[base + theirs + f])
    sources = [
        (
            charge_row(lambda low, high, f=f: masked_ref[f, low:high, low:high], nbasis),
            [coords_ref[d, f : f + 1, :] for d in range(3)],
        )
        for f in range(frag_dev)
    ]
    rows = []
    for charge, place in sources:
        rows += [part for values in place for part in thirds(values)[:2]] + [charge]
    rows.append(jnp.zeros((EXTRA - len(rows), nbasis), F32))
    sources_ref[...] = jnp.concatenate(rows).astype(BF16)

    pts_rows = region_ref.shape[0]
    each, block_cols = slab_refs[0].shape[0], slab_refs[0].shape[2]
    teams = len(slab_refs) * each
    row_x = row_places(pts_rows)

    def one_block(step, slab_ref, at):
        block = lax.rem(team + step, teams)
        region = region_ref[:, pl.ds(pl.multiple_of(block * block_cols, block_cols), block_cols)]
        fields = [field(charge, place, block, block_cols, row_x) for charge, place in sources]
        fields = over_lanes(fields, block_cols, pts_rows)
        for r in range(pts_rows):
            here = [jnp.where(region[r : r + 1] != base + f, fields[f][r], 0.0) for f in range(frag_dev)]
            slab_ref[at, r : r + 1, :] = sum(here)

    if each == 1:
        one_block(2, slab_refs[2], 0)
    else:

        @pl.loop(0, each)
        def _(step):
            for k, slab_ref in enumerate(slab_refs):
                one_block(k * each + step, slab_ref, step)

    for k in (0, 1, teams - 1):
        slab_refs[k // each][k % each] = jnp.zeros((pts_rows, block_cols), F32)
    here_ref[...] = region_ref[:, pl.ds(pl.multiple_of(team * block_cols, block_cols), block_cols)]

    for copy in copies[6:]:
        copy.wait()

    def add(s, corr):
        target = ids_ref[2 * slots + s]
        total_ref[target] = total_ref[target] + corr

    pipelined(
        slots,
        lambda s: dot(factor_ref[s].T, masked_ref[ids_ref[s]]),
        lambda s, right: dot(right, factor_ref[s]),
        add,
    )
    for s in range(slots):
        for k, row in ((1, s), (3, slots + s)):
            slots_ref[row : row + 1] = jnp.full((1, 128), ids_ref[k * slots + s], I32)
    own_ref[...] = total_ref[:frag_dev]
    by_core(total_ref.at[pl.ds(frag_dev, frag_dev)], 0, keep_ref, send_ref)
    send_ref[:, keep_ref.shape[1] :, :] = jnp.zeros((frag_dev, EXTRA, nbasis), BF16)


def left_kernel(
    slots_ref, sizes_ref, masked_ref, mine_ref, other_ref, own_ref, factor_ref, after_ref,
    keep_ref, *rest,
):
    send_refs, (ids_ref, all_ref, total_ref, sems) = rest[:-4], rest[-4:]
    copies = fetch([(slots_ref, ids_ref)], sems)
    frag_dev, nbasis = masked_ref.shape[0], masked_ref.shape[1]
    slots, half = factor_ref.shape[0], mine_ref.shape[0]
    me = lax.axis_index("sub")
    for f in range(frag_dev):
        all_ref[f] = masked_ref[f]
    for f in range(half):
        at = frag_dev + me * half + f
        all_ref[at] = live_square(mine_ref[f, :nbasis], sizes_ref[at, 0:1, 0:1])
        at = frag_dev + (1 - me) * half + f
        all_ref[at] = live_square(other_ref[f, :nbasis], sizes_ref[at, 0:1, 0:1])
    copies[0].wait()
    total_ref[:frag_dev] = own_ref[...]
    total_ref[frag_dev] = jnp.zeros_like(total_ref[frag_dev])

    def add(s, corr):
        target = ids_ref[slots + s, 0]
        total_ref[target] = total_ref[target] + corr

    pipelined(
        slots,
        lambda s: dot(factor_ref[s], all_ref[ids_ref[s, 0]]),
        lambda s, left: dot_t(left, factor_ref[s]),
        add,
    )
    grid_size, _, share, _ = keep_ref.shape
    for step in range(grid_size):
        chip = lax.rem(lax.axis_index("grid") + step, grid_size)
        for f in range(frag_dev):
            keep_ref[step, f] = total_ref[f, at_rows(2 * chip + me, share), :]
            send_refs[step][f] = total_ref[f, at_rows(2 * chip + 1 - me, share), :].astype(BF16)


def away_sum_kernel(keep_ref, *refs):
    count = len(refs) // 2
    for step, (recv_ref, part_ref) in enumerate(zip(refs[:count], refs[count:]), 1):
        part_ref[...] = (keep_ref[step] + recv_ref[...].astype(F32)).astype(BF16)


def relay_kernel(here_ref, in_ref, out_ref):
    out_ref[...] = in_ref[...]


def next_kernel(keep_ref, recv_ref, sources_ref, *out_refs):
    out_refs, after_ref = out_refs[:-1], out_refs[-1]
    after_ref[...] = jnp.zeros_like(after_ref)
    rounds, frag_dev = len(out_refs), keep_ref.shape[0]
    rows = keep_ref.shape[1] // rounds
    for j, out_ref in enumerate(out_refs):
        at = at_rows(lax.rem(lax.axis_index("grid") + j, rounds), rows) if rounds > 1 else slice(0, rows)
        for f in range(frag_dev):
            total = keep_ref[f, at, :].astype(F32) + recv_ref[f, at, :].astype(F32)
            out_ref[f * rows : (f + 1) * rows, :] = total.astype(BF16)
        out_ref[frag_dev * rows :, :] = sources_ref[...]


def before_kernel(*refs):
    in_refs, (keep_ref, send_ref) = refs[:-2], refs[-2:]
    me, (frag_dev, share, _) = lax.axis_index("sub"), keep_ref.shape
    for f in range(frag_dev):
        for at, ref in ((me, keep_ref), (1 - me, send_ref)):
            place = pl.ds(2 * f * share + pl.multiple_of(at * share, share), share)
            ref[f] = sum(in_ref[place, :].astype(F32) for in_ref in in_refs).astype(ref.dtype)


def middle_kernel(keep_ref, home_ref, far_ref, around_ref, *rest):
    part_refs, (out_ref, pot_ref) = rest[:-2], rest[-2:]
    out_ref[...] = keep_ref[0] + sum(part_ref[...].astype(F32) for part_ref in part_refs)
    pot_ref[...] = home_ref[...] + far_ref[...] + around_ref[...]


def around_kernel(frag_dev, sizes_ref, mine_ref, other_ref, here_ref, sources_ref, piece_ref, out_ref):
    half, nbasis = mine_ref.shape[0], mine_ref.shape[2]
    me, team, teams = lax.axis_index("sub"), lax.axis_index("frag"), lax.axis_size("frag")
    column = lax.broadcasted_iota(I32, (1, nbasis), 1)
    sources = []
    for ref, start in ((mine_ref, me * half), (other_ref, (1 - me) * half)):
        for f in range(half):
            charge = charge_row(lambda low, high, ref=ref, f=f: ref[f, low:high, low:high], nbasis)
            charge = jnp.where(column < sizes_ref[frag_dev + start + f, 0:1, 0:1], charge, 0.0)
            place = place_rows(ref[f, nbasis:, :].astype(F32))
            sources.append((lax.rem(team + 1, teams) * frag_dev + start + f, charge, place))
    for whose, extra in ((team, sources_ref[...]), (team + teams - 1, piece_ref[piece_ref.shape[0] - EXTRA :, :])):
        for f in range(frag_dev):
            rows = [extra[7 * f + k : 7 * f + k + 1].astype(F32) for k in range(7)]
            place = [rows[2 * d] + rows[2 * d + 1] for d in range(3)]
            sources.append((lax.rem(whose, teams) * frag_dev + f, rows[6], place))
    pts_rows, block_cols = here_ref.shape
    row_x = row_places(pts_rows)
    totals = [jnp.zeros((1, block_cols), F32) for _ in range(pts_rows)]
    fields = [field(charge, place, team, block_cols, row_x) for _, charge, place in sources]
    for (fragment, _, _), rows in zip(sources, over_lanes(fields, block_cols, pts_rows)):
        for r in range(pts_rows):
            totals[r] = totals[r] + jnp.where(here_ref[r : r + 1, :] != fragment, rows[r], 0.0)
    for r in range(pts_rows):
        out_ref[0, r : r + 1, :] = totals[r]


def last_kernel(
    scale, sizes_ref, masked_ref, own_ref, too_ref, before_ref, recv_ref, pot_ref, out_ref, potential_ref
):
    frag_dev, share, nbasis = out_ref.shape
    member = lax.axis_index("grid") * lax.axis_size("sub") + lax.axis_index("sub")
    row_start = pl.multiple_of(member * share, share)
    rows = row_start + lax.broadcasted_iota(I32, (share, nbasis), 0)
    cols = lax.broadcasted_iota(I32, (share, nbasis), 1)
    for f in range(frag_dev):
        size = sizes_ref[f, 0:1, 0:1]
        correction = own_ref[f] + before_ref[f] + (recv_ref[f].astype(F32) + too_ref[f].astype(F32))
        correction = jnp.where((rows < size) & (cols < size), correction, 0.0)
        out_ref[f] = (masked_ref[f, pl.ds(row_start, share), :].astype(F32) + correction).astype(BF16)
    potential_ref[...] = pot_ref[0] * scale


def turned(value, axis, steps):
    count = lax.axis_size(axis)
    return lax.ppermute(value, axis, [(s, (s + steps) % count) for s in range(count)])


def in_hbm(value):
    return pltpu.with_memory_space_constraint(value, pltpu.HBM)


def shape(dims, dtype):
    return jax.ShapeDtypeStruct(dims, dtype)


def per_device(
    density, basis_size, coupling, pair_first, pair_second, dimer_count, source_coords, grid_region
):
    frag_dev, nbasis, _ = density.shape
    slots = coupling.shape[0]
    teams, grid_size, sub_size = (lax.axis_size(a) for a in ("frag", "grid", "sub"))
    assert sub_size == 2 and frag_dev == 2 and grid_size % sub_size == 0
    rounds = grid_size // sub_size
    assert teams >= 4 and teams & (teams - 1) == 0
    share = nbasis // (grid_size * sub_size)
    half = frag_dev // sub_size
    pts_rows, total_cols = grid_region.shape
    block_cols = total_cols // teams

    smem = pl.BlockSpec(memory_space=pltpu.SMEM)
    vmem = pl.BlockSpec(memory_space=pltpu.VMEM)
    hbm = pl.BlockSpec(memory_space=pltpu.HBM)
    square = (nbasis, nbasis)

    def call(kernel, name, ins, outs, out_specs, scratch=(), flops=0):
        return pl.pallas_call(
            kernel,
            out_shape=outs,
            in_specs=ins,
            out_specs=out_specs,
            scratch_shapes=scratch,
            compiler_params=pltpu.CompilerParams(vmem_limit_bytes=VMEM_LIMIT),
            cost_estimate=pl.CostEstimate(flops=flops, bytes_accessed=1 << 20, transcendentals=0),
            name=name,
        )

    work = 4 * slots * nbasis**3
    by_chip = (grid_size, frag_dev, share, nbasis)
    halves = shape((frag_dev, nbasis // sub_size, nbasis), BF16)
    sent_halves = shape((frag_dev, nbasis // sub_size + EXTRA, nbasis), BF16)
    places = in_hbm(jnp.transpose(source_coords, (1, 0, 2)))
    payload = call(
        head_kernel,
        "head",
        [hbm] * 2,
        shape((half, nbasis + EXTRA, nbasis), BF16),
        vmem,
        [pltpu.VMEM((3, frag_dev, nbasis), F32), pltpu.SemaphoreType.DMA((1 + nbasis // 128,))],
    )(in_hbm(density), places)
    mine = turned(payload, "frag", -1)

    next_keep, next_send, own_part, factors, masked, slot_ids, sizes, here, sources, *slabs = call(
        right_kernel,
        "right",
        [hbm] * 3 + [smem, vmem] + [hbm] * 4,
        (
            halves, sent_halves, shape((frag_dev,) + square, F32),
            shape((slots,) + square, BF16), shape((frag_dev,) + square, BF16),
            shape((2 * slots, 128), I32), shape((2 * frag_dev, 8, 128), I32), shape((pts_rows, block_cols), I32),
            shape((EXTRA, nbasis), BF16),
        ) + (shape((teams // 4, pts_rows, block_cols), F32),) * 4,
        (vmem,) * 13,
        [
            pltpu.SMEM(basis_size.shape, I32), pltpu.SMEM((slots,), I32), pltpu.SMEM((slots,), I32),
            pltpu.SMEM((4 * slots,), I32), pltpu.VMEM((half,) + square, BF16), pltpu.VMEM((3, frag_dev, nbasis), F32),
            pltpu.VMEM(grid_region.shape, I32), pltpu.VMEM((2 * frag_dev + 1,) + square, F32),
            pltpu.SemaphoreType.DMA((6 + slots,)),
        ],
        work,
    )(
        in_hbm(basis_size), in_hbm(pair_first), in_hbm(pair_second), dimer_count, payload, in_hbm(density),
        in_hbm(coupling), places, in_hbm(grid_region),
    )

    if teams == 4:
        home, far = slabs[0], turned(slabs[2], "frag", 2)
    else:
        slabs = jnp.concatenate(slabs)
        while slabs.shape[0] > 1:
            rest = slabs.shape[0] // 2
            slabs = slabs[:rest] + turned(slabs[rest:], "frag", rest)
        home, far = slabs, jnp.zeros_like(slabs)

    *pieces, after = call(
        next_kernel,
        "next_sum",
        [vmem] * 3,
        [shape((frag_dev * nbasis // grid_size + EXTRA, nbasis), BF16)] * rounds + [shape((8, 128), F32)],
        (vmem,) * (rounds + 1),
    )(next_keep, turned(next_send, "sub", 1), sources)
    for j, value in enumerate(pieces):
        pairs = []
        for t in range(teams):
            for g in range(grid_size):
                for c in range(sub_size):
                    to = (c * rounds + (g + j) % rounds, g // rounds) if t + 1 < teams else (g, c)
                    to = ((t + 1) % teams * grid_size + to[0]) * sub_size + to[1]
                    pairs.append(((t * grid_size + g) * sub_size + c, to))
        pieces[j] = lax.ppermute(value, ("frag", "grid", "sub"), pairs)

    mine = call(relay_kernel, "relay", [vmem] * 2, shape(payload.shape, BF16), vmem)(here, mine)
    other = turned(mine, "sub", 1)
    own_keep, *own_sends = call(
        left_kernel,
        "left",
        [vmem] * 8,
        [shape(by_chip, F32)] + [shape((frag_dev, share, nbasis), BF16)] * grid_size,
        (vmem,) * (1 + grid_size),
        [
            pltpu.SMEM((2 * slots, 128), I32), pltpu.VMEM((2 * frag_dev,) + square, BF16),
            pltpu.VMEM((frag_dev + 1,) + square, F32), pltpu.SemaphoreType.DMA((1,)),
        ],
        work,
    )(slot_ids, sizes, masked, mine, other, own_part, factors, after)
    mine_rows = (frag_dev, share, nbasis)
    own_recv, *away_recvs = [turned(value, "sub", 1) for value in own_sends]
    parts = call(
        away_sum_kernel,
        "away_sum",
        [vmem] * grid_size,
        [shape(mine_rows, BF16)] * (grid_size - 1),
        (vmem,) * (grid_size - 1),
    )(own_keep, *away_recvs)
    parts = [turned(part, "grid", step) for step, part in enumerate(parts, 1)]

    slab = shape((1, pts_rows, block_cols), F32)
    before, passed = call(
        before_kernel,
        "before",
        [vmem] * rounds,
        (shape(mine_rows, F32), shape(mine_rows, BF16)),
        (vmem,) * 2,
    )(*pieces)
    passed = turned(passed, "sub", 1)
    around = call(functools.partial(around_kernel, frag_dev), "around", [vmem] * 6, slab, vmem)(
        sizes, mine, other, here, sources, pieces[0]
    )
    own, pot = call(
        middle_kernel,
        "middle",
        [vmem] * (4 + len(parts)),
        (shape(mine_rows, F32), slab),
        (vmem,) * 2,
        (),
        10**10,
    )(own_keep, home, far, around, *parts)

    scale = 8.0 / math.sqrt(frag_dev * teams * nbasis)
    return call(
        functools.partial(last_kernel, scale),
        "last",
        [vmem] * 7,
        (shape(mine_rows, BF16), shape((pts_rows, block_cols), F32)),
        (vmem,) * 2,
    )(sizes, masked, own, own_recv, before, passed, pot)


def solution(mesh):
    placed = (
        P(("groups", "frag"), None, None),
        P(),
        P(("groups", "frag", "grid", "sub"), None, None),
        P(("frag", "grid", "sub")),
        P(("frag", "grid", "sub")),
        P(("frag", "grid", "sub")),
        P(("groups", "frag"), None, None),
        P(("grid", "sub"), None),
    )
    return jax.shard_map(
        per_device,
        mesh=mesh,
        in_specs=placed,
        out_specs=(
            P(("groups", "frag"), ("grid", "sub"), None),
            P(("groups", "grid", "sub"), "frag"),
        ),
        check_vma=False,
    )
```

```python
import functools
import math

import jax
import jax.numpy as jnp
from jax import lax
from jax.experimental import pallas as pl
from jax.experimental.pallas import tpu as pltpu
from jax.sharding import PartitionSpec as P

VMEM_LIMIT = 24 * 1024 * 1024
EXTRA = 16
BF16, F32, I32 = jnp.bfloat16, jnp.float32, jnp.int32


def live_square(values, size):
    rows = lax.broadcasted_iota(I32, values.shape, 0)
    cols = lax.broadcasted_iota(I32, values.shape, 1)
    return jnp.where((rows < size) & (cols < size), values.astype(F32), 0.0).astype(BF16)


def charge_row(read, nbasis):
    tile = 128
    parts = []
    for at in range(0, nbasis, tile):
        block = read(at, at + tile).astype(F32)
        rows = lax.broadcasted_iota(I32, block.shape, 0)
        cols = lax.broadcasted_iota(I32, block.shape, 1)
        parts.append(jnp.sum(jnp.where(rows == cols, block, 0.0), axis=0, keepdims=True))
    return jnp.concatenate(parts, axis=1)


def at_rows(block, size):
    return pl.ds(pl.multiple_of(block * size, size), size)


def thirds(values):
    high = values.astype(BF16).astype(F32)
    middle = (values - high).astype(BF16).astype(F32)
    return [high, middle, values - high - middle]


def field(charge, place, block, block_cols, row_x):
    src_x, src_y, src_z = place
    point_z = 0.25 * lax.broadcasted_iota(I32, (64, charge.shape[1]), 0).astype(F32)
    along_z = (point_z - src_z) ** 2 + 1.0
    parts = []
    for x in row_x:
        for step in range(block_cols // 64):
            point_y = 0.25 * (block * (block_cols // 64) + step).astype(F32)
            in_plane = (x - src_x) ** 2 + (point_y - src_y) ** 2
            value = charge * lax.rsqrt(along_z + in_plane)
            parts.append(sum(value[:, at : at + 128] for at in range(0, value.shape[1], 128)))
    return jnp.concatenate(parts)


def over_lanes(points, block_cols, pts_rows):
    rows = jnp.concatenate(points)
    ones = jnp.ones((16, 128), BF16)
    total = sum(dot_t(ones, part.astype(BF16)) for part in thirds(rows))
    size = pts_rows * block_cols
    return [
        [total[0:1, k * size + r * block_cols : k * size + (r + 1) * block_cols] for r in range(pts_rows)]
        for k in range(len(points))
    ]


def row_places(pts_rows):
    member = lax.axis_index("grid") * lax.axis_size("sub") + lax.axis_index("sub")
    return [0.25 * (member * pts_rows + r).astype(F32) for r in range(pts_rows)]


def place_rows(extra):
    return [sum(extra[3 * d + k : 3 * d + k + 1] for k in range(3)) for d in range(3)]


def by_core(total_ref, row, keep_ref, send_ref):
    me, rows = lax.axis_index("sub"), keep_ref.shape[-2]
    for f in range(keep_ref.shape[0]):
        keep_ref[f] = total_ref[f, pl.ds(row + pl.multiple_of(me * rows, rows), rows), :].astype(keep_ref.dtype)
        other = total_ref[f, pl.ds(row + pl.multiple_of((1 - me) * rows, rows), rows), :]
        send_ref[f, :rows] = other.astype(send_ref.dtype)


def pipelined(slots, first_dot, second_dot, add):
    held = None
    for slot in range(slots + 1):
        now = first_dot(slot).astype(BF16) if slot < slots else None
        if held is not None:
            add(slot - 1, second_dot(slot - 1, held))
        held = now


def dot(a, b):
    return jnp.dot(a, b, preferred_element_type=F32)


def dot_t(a, b):
    return lax.dot_general(a, b, (((1,), (1,)), ((), ())), preferred_element_type=F32)


def fetch(pairs, sems):
    copies = [pltpu.make_async_copy(source, target, sems.at[i]) for i, (source, target) in enumerate(pairs)]
    for copy in copies:
        copy.start()
    return copies


def head_kernel(density_hbm, coords_hbm, payload_ref, coords_ref, sems):
    half, nbasis = payload_ref.shape[0], payload_ref.shape[2]
    at = lax.axis_index("sub") * half
    copies = fetch(
        [(coords_hbm, coords_ref)]
        + [
            (density_hbm.at[pl.ds(at, half), pl.ds(low, 128)], payload_ref.at[:, pl.ds(low, 128)])
            for low in range(0, nbasis, 128)
        ],
        sems,
    )
    copies[0].wait()
    for f in range(half):
        rows = [part for d in range(3) for part in thirds(coords_ref[d, pl.ds(at + f, 1), :])]
        rows.append(jnp.zeros((EXTRA - len(rows), nbasis), F32))
        payload_ref[f, nbasis:, :] = jnp.concatenate(rows).astype(BF16)
    for copy in copies[1:]:
        copy.wait()


def right_kernel(
    size_hbm, first_hbm, second_hbm, count_ref, payload_ref, density_hbm, coupling_hbm, coords_hbm, region_hbm,
    keep_ref, send_ref, own_ref, factor_ref, masked_ref, slots_ref, sizes_ref, here_ref, sources_ref, *rest,
):
    slab_refs, rest = rest[:4], rest[4:]
    size_ref, first_ref, second_ref, ids_ref, density_ref, coords_ref, region_ref, total_ref, sems = rest
    frag_dev, nbasis, slots = masked_ref.shape[0], masked_ref.shape[1], factor_ref.shape[0]
    half = payload_ref.shape[0]
    mine, theirs = lax.axis_index("sub") * half, (1 - lax.axis_index("sub")) * half
    copies = fetch(
        [
            (size_hbm, size_ref), (first_hbm, first_ref), (second_hbm, second_ref),
            (density_hbm.at[pl.ds(theirs, half)], density_ref), (coords_hbm, coords_ref), (region_hbm, region_ref),
        ]
        + [(coupling_hbm.at[s], factor_ref.at[s]) for s in range(slots)],
        sems,
    )
    total_ref[...] = jnp.zeros_like(total_ref)
    for copy in copies[:6]:
        copy.wait()
    team = lax.axis_index("frag")
    base = team * frag_dev
    trash = 2 * frag_dev
    for s in range(slots):
        live = s < count_ref[0]
        first = jnp.clip(first_ref[s] - base, 0, frag_dev - 1)
        second = jnp.clip(second_ref[s] - base, 0, trash - 1)
        ids_ref[s] = first
        ids_ref[slots + s] = second
        ids_ref[2 * slots + s] = jnp.where(live, second, trash)
        ids_ref[3 * slots + s] = jnp.where(live, first, frag_dev)
    for f in range(2 * frag_dev):
        sizes_ref[f] = jnp.full((8, 128), size_ref[lax.rem(base + f, size_ref.shape[0])], I32)
    for f in range(half):
        masked_ref[mine + f] = live_square(payload_ref[f, :nbasis], size_ref[base + mine + f])
        masked_ref[theirs + f] = live_square(density_ref[f], size_ref[base + theirs + f])
    sources = [
        (
            charge_row(lambda low, high, f=f: masked_ref[f, low:high, low:high], nbasis),
            [coords_ref[d, f : f + 1, :] for d in range(3)],
        )
        for f in range(frag_dev)
    ]
    rows = []
    for charge, place in sources:
        rows += [part for values in place for part in thirds(values)[:2]] + [charge]
    rows.append(jnp.zeros((EXTRA - len(rows), nbasis), F32))
    sources_ref[...] = jnp.concatenate(rows).astype(BF16)

    pts_rows = region_ref.shape[0]
    each, block_cols = slab_refs[0].shape[0], slab_refs[0].shape[2]
    teams = len(slab_refs) * each
    row_x = row_places(pts_rows)

    def one_block(step, slab_ref, at):
        block = lax.rem(team + step, teams)
        region = region_ref[:, pl.ds(pl.multiple_of(block * block_cols, block_cols), block_cols)]
        fields = [field(charge, place, block, block_cols, row_x) for charge, place in sources]
        fields = over_lanes(fields, block_cols, pts_rows)
        for r in range(pts_rows):
            here = [jnp.where(region[r : r + 1] != base + f, fields[f][r], 0.0) for f in range(frag_dev)]
            slab_ref[at, r : r + 1, :] = sum(here)

    if each == 1:
        one_block(2, slab_refs[2], 0)
    else:

        @pl.loop(0, each)
        def _(step):
            for k, slab_ref in enumerate(slab_refs):
                one_block(k * each + step, slab_ref, step)

    for k in (0, 1, teams - 1):
        slab_refs[k // each][k % each] = jnp.zeros((pts_rows, block_cols), F32)
    here_ref[...] = region_ref[:, pl.ds(pl.multiple_of(team * block_cols, block_cols), block_cols)]

    for copy in copies[6:]:
        copy.wait()

    def add(s, corr):
        target = ids_ref[2 * slots + s]
        total_ref[target] = total_ref[target] + corr

    pipelined(
        slots,
        lambda s: dot(factor_ref[s].T, masked_ref[ids_ref[s]]),
        lambda s, right: dot(right, factor_ref[s]),
        add,
    )
    for s in range(slots):
        for k, row in ((1, s), (3, slots + s)):
            slots_ref[row : row + 1] = jnp.full((1, 128), ids_ref[k * slots + s], I32)
    own_ref[...] = total_ref[:frag_dev]
    by_core(total_ref.at[pl.ds(frag_dev, frag_dev)], 0, keep_ref, send_ref)
    send_ref[:, keep_ref.shape[1] :, :] = jnp.zeros((frag_dev, EXTRA, nbasis), BF16)


def left_kernel(
    slots_ref, sizes_ref, masked_ref, mine_ref, other_ref, own_ref, factor_ref, after_ref,
    keep_ref, *rest,
):
    send_refs, (ids_ref, all_ref, total_ref, sems) = rest[:-4], rest[-4:]
    copies = fetch([(slots_ref, ids_ref)], sems)
    frag_dev, nbasis = masked_ref.shape[0], masked_ref.shape[1]
    slots, half = factor_ref.shape[0], mine_ref.shape[0]
    me = lax.axis_index("sub")
    for f in range(frag_dev):
        all_ref[f] = masked_ref[f]
    for f in range(half):
        at = frag_dev + me * half + f
        all_ref[at] = live_square(mine_ref[f, :nbasis], sizes_ref[at, 0:1, 0:1])
        at = frag_dev + (1 - me) * half + f
        all_ref[at] = live_square(other_ref[f, :nbasis], sizes_ref[at, 0:1, 0:1])
    copies[0].wait()
    total_ref[:frag_dev] = own_ref[...]
    total_ref[frag_dev] = jnp.zeros_like(total_ref[frag_dev])

    def add(s, corr):
        target = ids_ref[slots + s, 0]
        total_ref[target] = total_ref[target] + corr

    pipelined(
        slots,
        lambda s: dot(factor_ref[s], all_ref[ids_ref[s, 0]]),
        lambda s, left: dot_t(left, factor_ref[s]),
        add,
    )
    grid_size, _, share, _ = keep_ref.shape
    for step in range(grid_size):
        chip = lax.rem(lax.axis_index("grid") + step, grid_size)
        for f in range(frag_dev):
            keep_ref[step, f] = total_ref[f, at_rows(2 * chip + me, share), :]
            send_refs[step][f] = total_ref[f, at_rows(2 * chip + 1 - me, share), :].astype(BF16)


def away_sum_kernel(keep_ref, *refs):
    count = len(refs) // 2
    for step, (recv_ref, part_ref) in enumerate(zip(refs[:count], refs[count:]), 1):
        part_ref[...] = (keep_ref[step] + recv_ref[...].astype(F32)).astype(BF16)


def relay_kernel(here_ref, in_ref, out_ref):
    out_ref[...] = in_ref[...]


def next_kernel(keep_ref, recv_ref, sources_ref, *out_refs):
    out_refs, after_ref = out_refs[:-1], out_refs[-1]
    after_ref[...] = jnp.zeros_like(after_ref)
    rounds, frag_dev = len(out_refs), keep_ref.shape[0]
    rows = keep_ref.shape[1] // rounds
    for j, out_ref in enumerate(out_refs):
        at = at_rows(lax.rem(lax.axis_index("grid") + j, rounds), rows) if rounds > 1 else slice(0, rows)
        for f in range(frag_dev):
            total = keep_ref[f, at, :].astype(F32) + recv_ref[f, at, :].astype(F32)
            out_ref[f * rows : (f + 1) * rows, :] = total.astype(BF16)
        out_ref[frag_dev * rows :, :] = sources_ref[...]


def before_kernel(*refs):
    in_refs, (keep_ref, send_ref) = refs[:-2], refs[-2:]
    me, (frag_dev, share, _) = lax.axis_index("sub"), keep_ref.shape
    for f in range(frag_dev):
        for at, ref in ((me, keep_ref), (1 - me, send_ref)):
            place = pl.ds(2 * f * share + pl.multiple_of(at * share, share), share)
            ref[f] = sum(in_ref[place, :].astype(F32) for in_ref in in_refs).astype(ref.dtype)


def middle_kernel(keep_ref, home_ref, far_ref, around_ref, *rest):
    part_refs, (out_ref, pot_ref) = rest[:-2], rest[-2:]
    out_ref[...] = keep_ref[0] + sum(part_ref[...].astype(F32) for part_ref in part_refs)
    pot_ref[...] = home_ref[...] + far_ref[...] + around_ref[...]


def around_kernel(frag_dev, sizes_ref, mine_ref, other_ref, here_ref, sources_ref, piece_ref, out_ref):
    half, nbasis = mine_ref.shape[0], mine_ref.shape[2]
    me, team, teams = lax.axis_index("sub"), lax.axis_index("frag"), lax.axis_size("frag")
    column = lax.broadcasted_iota(I32, (1, nbasis), 1)
    sources = []
    for ref, start in ((mine_ref, me * half), (other_ref, (1 - me) * half)):
        for f in range(half):
            charge = charge_row(lambda low, high, ref=ref, f=f: ref[f, low:high, low:high], nbasis)
            charge = jnp.where(column < sizes_ref[frag_dev + start + f, 0:1, 0:1], charge, 0.0)
            place = place_rows(ref[f, nbasis:, :].astype(F32))
            sources.append((lax.rem(team + 1, teams) * frag_dev + start + f, charge, place))
    for whose, extra in ((team, sources_ref[...]), (team + teams - 1, piece_ref[piece_ref.shape[0] - EXTRA :, :])):
        for f in range(frag_dev):
            rows = [extra[7 * f + k : 7 * f + k + 1].astype(F32) for k in range(7)]
            place = [rows[2 * d] + rows[2 * d + 1] for d in range(3)]
            sources.append((lax.rem(whose, teams) * frag_dev + f, rows[6], place))
    pts_rows, block_cols = here_ref.shape
    row_x = row_places(pts_rows)
    totals = [jnp.zeros((1, block_cols), F32) for _ in range(pts_rows)]
    fields = [field(charge, place, team, block_cols, row_x) for _, charge, place in sources]
    for (fragment, _, _), rows in zip(sources, over_lanes(fields, block_cols, pts_rows)):
        for r in range(pts_rows):
            totals[r] = totals[r] + jnp.where(here_ref[r : r + 1, :] != fragment, rows[r], 0.0)
    for r in range(pts_rows):
        out_ref[0, r : r + 1, :] = totals[r]


def last_kernel(
    scale, sizes_ref, masked_ref, own_ref, too_ref, before_ref, recv_ref, pot_ref, out_hbm, potential_hbm,
    out_ref, potential_ref, sems,
):
    frag_dev, share, nbasis = out_ref.shape
    member = lax.axis_index("grid") * lax.axis_size("sub") + lax.axis_index("sub")
    row_start = pl.multiple_of(member * share, share)
    rows = row_start + lax.broadcasted_iota(I32, (share, nbasis), 0)
    cols = lax.broadcasted_iota(I32, (share, nbasis), 1)
    potential_ref[...] = pot_ref[0] * scale
    copies = fetch([(potential_ref, potential_hbm)], sems)
    for f in range(frag_dev):
        size = sizes_ref[f, 0:1, 0:1]
        correction = own_ref[f] + before_ref[f] + (recv_ref[f].astype(F32) + too_ref[f].astype(F32))
        correction = jnp.where((rows < size) & (cols < size), correction, 0.0)
        out_ref[f] = (masked_ref[f, pl.ds(row_start, share), :].astype(F32) + correction).astype(BF16)
        copy = pltpu.make_async_copy(out_ref.at[f], out_hbm.at[f], sems.at[1 + f])
        copy.start()
        copies.append(copy)
    for copy in copies:
        copy.wait()


def turned(value, axis, steps):
    count = lax.axis_size(axis)
    return lax.ppermute(value, axis, [(s, (s + steps) % count) for s in range(count)])


def in_hbm(value):
    return pltpu.with_memory_space_constraint(value, pltpu.HBM)


def shape(dims, dtype):
    return jax.ShapeDtypeStruct(dims, dtype)


def per_device(
    density, basis_size, coupling, pair_first, pair_second, dimer_count, source_coords, grid_region
):
    frag_dev, nbasis, _ = density.shape
    slots = coupling.shape[0]
    teams, grid_size, sub_size = (lax.axis_size(a) for a in ("frag", "grid", "sub"))
    assert sub_size == 2 and frag_dev == 2 and grid_size % sub_size == 0
    rounds = grid_size // sub_size
    assert teams >= 4 and teams & (teams - 1) == 0
    share = nbasis // (grid_size * sub_size)
    half = frag_dev // sub_size
    pts_rows, total_cols = grid_region.shape
    block_cols = total_cols // teams

    smem = pl.BlockSpec(memory_space=pltpu.SMEM)
    vmem = pl.BlockSpec(memory_space=pltpu.VMEM)
    hbm = pl.BlockSpec(memory_space=pltpu.HBM)
    square = (nbasis, nbasis)

    def call(kernel, name, ins, outs, out_specs, scratch=(), flops=0):
        return pl.pallas_call(
            kernel,
            out_shape=outs,
            in_specs=ins,
            out_specs=out_specs,
            scratch_shapes=scratch,
            compiler_params=pltpu.CompilerParams(vmem_limit_bytes=VMEM_LIMIT),
            cost_estimate=pl.CostEstimate(flops=flops, bytes_accessed=1 << 20, transcendentals=0),
            name=name,
        )

    work = 4 * slots * nbasis**3
    by_chip = (grid_size, frag_dev, share, nbasis)
    halves = shape((frag_dev, nbasis // sub_size, nbasis), BF16)
    sent_halves = shape((frag_dev, nbasis // sub_size + EXTRA, nbasis), BF16)
    places = in_hbm(jnp.transpose(source_coords, (1, 0, 2)))
    payload = call(
        head_kernel,
        "head",
        [hbm] * 2,
        shape((half, nbasis + EXTRA, nbasis), BF16),
        vmem,
        [pltpu.VMEM((3, frag_dev, nbasis), F32), pltpu.SemaphoreType.DMA((1 + nbasis // 128,))],
    )(in_hbm(density), places)
    mine = turned(payload, "frag", -1)

    next_keep, next_send, own_part, factors, masked, slot_ids, sizes, here, sources, *slabs = call(
        right_kernel,
        "right",
        [hbm] * 3 + [smem, vmem] + [hbm] * 4,
        (
            halves, sent_halves, shape((frag_dev,) + square, F32),
            shape((slots,) + square, BF16), shape((frag_dev,) + square, BF16),
            shape((2 * slots, 128), I32), shape((2 * frag_dev, 8, 128), I32), shape((pts_rows, block_cols), I32),
            shape((EXTRA, nbasis), BF16),
        ) + (shape((teams // 4, pts_rows, block_cols), F32),) * 4,
        (vmem,) * 13,
        [
            pltpu.SMEM(basis_size.shape, I32), pltpu.SMEM((slots,), I32), pltpu.SMEM((slots,), I32),
            pltpu.SMEM((4 * slots,), I32), pltpu.VMEM((half,) + square, BF16), pltpu.VMEM((3, frag_dev, nbasis), F32),
            pltpu.VMEM(grid_region.shape, I32), pltpu.VMEM((2 * frag_dev + 1,) + square, F32),
            pltpu.SemaphoreType.DMA((6 + slots,)),
        ],
        work,
    )(
        in_hbm(basis_size), in_hbm(pair_first), in_hbm(pair_second), dimer_count, payload, in_hbm(density),
        in_hbm(coupling), places, in_hbm(grid_region),
    )

    if teams == 4:
        home, far = slabs[0], turned(slabs[2], "frag", 2)
    else:
        slabs = jnp.concatenate(slabs)
        while slabs.shape[0] > 1:
            rest = slabs.shape[0] // 2
            slabs = slabs[:rest] + turned(slabs[rest:], "frag", rest)
        home, far = slabs, jnp.zeros_like(slabs)

    *pieces, after = call(
        next_kernel,
        "next_sum",
        [vmem] * 3,
        [shape((frag_dev * nbasis // grid_size + EXTRA, nbasis), BF16)] * rounds + [shape((8, 128), F32)],
        (vmem,) * (rounds + 1),
    )(next_keep, turned(next_send, "sub", 1), sources)
    for j, value in enumerate(pieces):
        pairs = []
        for t in range(teams):
            for g in range(grid_size):
                for c in range(sub_size):
                    to = (c * rounds + (g + j) % rounds, g // rounds) if t + 1 < teams else (g, c)
                    to = ((t + 1) % teams * grid_size + to[0]) * sub_size + to[1]
                    pairs.append(((t * grid_size + g) * sub_size + c, to))
        pieces[j] = lax.ppermute(value, ("frag", "grid", "sub"), pairs)

    mine = call(relay_kernel, "relay", [vmem] * 2, shape(payload.shape, BF16), vmem)(here, mine)
    other = turned(mine, "sub", 1)
    own_keep, *own_sends = call(
        left_kernel,
        "left",
        [vmem] * 8,
        [shape(by_chip, F32)] + [shape((frag_dev, share, nbasis), BF16)] * grid_size,
        (vmem,) * (1 + grid_size),
        [
            pltpu.SMEM((2 * slots, 128), I32), pltpu.VMEM((2 * frag_dev,) + square, BF16),
            pltpu.VMEM((frag_dev + 1,) + square, F32), pltpu.SemaphoreType.DMA((1,)),
        ],
        work,
    )(slot_ids, sizes, masked, mine, other, own_part, factors, after)
    mine_rows = (frag_dev, share, nbasis)
    own_recv, *away_recvs = [turned(value, "sub", 1) for value in own_sends]
    parts = call(
        away_sum_kernel,
        "away_sum",
        [vmem] * grid_size,
        [shape(mine_rows, BF16)] * (grid_size - 1),
        (vmem,) * (grid_size - 1),
    )(own_keep, *away_recvs)
    parts = [turned(part, "grid", step) for step, part in enumerate(parts, 1)]

    slab = shape((1, pts_rows, block_cols), F32)
    before, passed = call(
        before_kernel,
        "before",
        [vmem] * rounds,
        (shape(mine_rows, F32), shape(mine_rows, BF16)),
        (vmem,) * 2,
    )(*pieces)
    passed = turned(passed, "sub", 1)
    around = call(functools.partial(around_kernel, frag_dev), "around", [vmem] * 6, slab, vmem)(
        sizes, mine, other, here, sources, pieces[0]
    )
    own, pot = call(
        middle_kernel,
        "middle",
        [vmem] * (4 + len(parts)),
        (shape(mine_rows, F32), slab),
        (vmem,) * 2,
        (),
        10**10,
    )(own_keep, home, far, around, *parts)

    scale = 8.0 / math.sqrt(frag_dev * teams * nbasis)
    return call(
        functools.partial(last_kernel, scale),
        "last",
        [vmem] * 7,
        (shape(mine_rows, BF16), shape((pts_rows, block_cols), F32)),
        (hbm,) * 2,
        [
            pltpu.VMEM(mine_rows, BF16), pltpu.VMEM((pts_rows, block_cols), F32),
            pltpu.SemaphoreType.DMA((1 + frag_dev,)),
        ],
    )(sizes, masked, own, own_recv, before, passed, pot)


def solution(mesh):
    placed = (
        P(("groups", "frag"), None, None),
        P(),
        P(("groups", "frag", "grid", "sub"), None, None),
        P(("frag", "grid", "sub")),
        P(("frag", "grid", "sub")),
        P(("frag", "grid", "sub")),
        P(("groups", "frag"), None, None),
        P(("grid", "sub"), None),
    )
    return jax.shard_map(
        per_device,
        mesh=mesh,
        in_specs=placed,
        out_specs=(
            P(("groups", "frag"), ("grid", "sub"), None),
            P(("groups", "grid", "sub"), "frag"),
        ),
        check_vma=False,
    )
```
